32 devices in a mesh: corr: 4 (over y, x), tile: 8 (over z, core).
Axes of the slice: x: 2, y: 2, z: 4, core: 2. Of those that a mesh axis runs over, the one named last changes fastest.
Arguments:
- visibilities: bfloat16 [2048, 8, 256], P(('corr', 'tile')), may hold values from -6 to 6
- coords: float32 [2048, 3, 256], P(('corr', 'tile')), may hold values from -12 to 12
- stations: int32 [2048, 2], P(('corr', 'tile')), may hold values from 0 to 511
- tile_ids: int32 [2048, 1], P(('corr', 'tile')), may hold values from 0 to 63; in each aligned block of 64 rows (0 to 63, 64 to 127, ...) at most 2 rows name the same one
- offsets: int32 [2048, 2], P(('corr', 'tile')), may hold values from 0 to 96
- screens: bfloat16 [512, 8, 1024], P('tile'), may hold values from -4 to 4
Outputs:
- grid_tiles: float32 [4, 64, 2, 128, 128], P('corr', 'tile')
The draws below stay inside these ranges and needn't reach their ends.
Inputs may be any that keep to these rules, and one draw needn't show every extreme that they name: `tile_ids`: within the rows of one device (aligned blocks of 64 rows) no uv-tile is named more than 2 times, and some uv-tile exactly 2 times.
All inputs are finite; a program needn't handle non-finite values.
Results may differ from the reference program's by a relative error of at most 0.0061.
Values may be sent and summed in bfloat16 or wider, within the bound.
No kernel may reach another device: no remote copies, remote signals or barrier semaphores. Data moves between devices by JAX's collectives and lax.ppermute only.
A program may use at most 64 MiB of HBM per device.

```python
import math
import jax
import jax.numpy as jnp
import numpy as np
from jax import lax

NCORR = 4
SUB = 32
STATIONS = 512
NT = 64
TILE_SIDE = 128
SG_DEV = 64
NVIS = 256
PIX = 1024
SUBGRIDS = 2048
CAP = 2


def plant(result, stream_key, low, top_value):
    longest = result.shape.index(max(result.shape))
    spots = []
    for shift in (0, 1):
        where = [jax.random.randint(jax.random.fold_in(stream_key, axis), (), 0, length) for axis, length in enumerate(result.shape)]
        where[longest] = (where[longest] + shift) % result.shape[longest]
        spots.append(tuple(where))
    return result.at[spots[0]].set(low).at[spots[1]].set(top_value)


def level_of(rng, shape, cuts, smallest, top_value):
    factor_of = 1.0
    for axis_at, blocks in cuts:
        heights = jax.random.uniform(jax.random.fold_in(jax.random.fold_in(rng, 6), axis_at), (blocks,), jnp.float32, smallest / len(cuts), top_value / len(cuts))
        factor_of = factor_of * jnp.repeat(jnp.exp(heights), shape[axis_at] // blocks).reshape((-1,) + (1,) * (len(shape) - 1 - axis_at))
    return factor_of


def routed_block(stream_key, own, number, rows, amount, top, reach, slope):
    sequence = jax.random.permutation(stream_key, amount)
    crowded, common = load_shares(amount, rows * top, reach, slope, True), load_shares(amount, rows * top, reach, slope, False)
    places = jnp.arange(amount)

    def named(tallies, turn):
        used = int((tallies > 0).sum())
        fixed = max(1, used // 4)
        passed = fixed + (places - fixed + turn * (used - fixed)) % max(1, amount - fixed)
        return jnp.zeros((amount,), jnp.int32).at[sequence[jnp.where(places < fixed, places, passed)]].set(jnp.asarray(tallies, jnp.int32))

    tallies = jnp.where(number % 4 == 0, named(crowded, number // 4), named(common, number - number // 4 - 1))
    mixed = jax.random.permutation(jax.random.fold_in(own, 3), amount)
    source_of, taker = mixed[0:amount // 2 * 2:2], mixed[1:amount // 2 * 2:2]
    margin = jnp.minimum(tallies[source_of] - 1, reach - tallies[taker]) // 2
    margin = jnp.where((source_of == sequence[0]) | (taker == sequence[0]) | (tallies[taker] == 0), 0, jnp.maximum(margin, 0))
    passed = jax.random.randint(jax.random.fold_in(own, 4), (amount // 2,), 0, 1 << 20) % (margin + 1)
    tallies = tallies.at[source_of].add(-passed).at[taker].add(passed)
    labels = jnp.searchsorted(jnp.cumsum(tallies), jnp.arange(rows * top), side="right").astype(jnp.int32)
    table = labels.reshape(top, rows).T
    table = table[jax.random.permutation(jax.random.fold_in(own, 1), rows)]
    turn = jax.random.randint(jax.random.fold_in(own, 2), (rows, 1), 0, top)
    return jnp.take_along_axis(table, (jnp.arange(top)[None, :] + turn) % top, axis=1)


def load_shares(amount, total, most, lean, full):
    weights = [(1 << 20) // math.isqrt(rank ** lean) + 1 for rank in range(1, amount + 1)]
    largest = most if full else min(most, max(-(-total // amount), total * weights[0] // sum(weights)))
    least = 1 if total - largest >= amount - 1 else 0
    given, surplus = [largest] + [least] * (amount - 1), total - largest - least * (amount - 1)
    while surplus > 0:
        candidates = [i for i in range(1, amount) if given[i] < largest] or [i for i in range(1, amount) if given[i] < most]
        mass, budget = sum([weights[i] for i in candidates]), surplus
        for i in candidates:
            more = min(most - given[i], max(1, budget * weights[i] // mass), surplus)
            given[i] = given[i] + more
            surplus = surplus - more
    return np.array(given)


def centred(stream_key, dims, deviation, bound, shards=(), kind=jnp.bfloat16):
    level = level_of(stream_key, dims, shards, -0.22, 0.18) if shards else 1.0
    drawn = jax.random.normal(stream_key, dims, jnp.float32) * deviation * level
    return jnp.minimum(jnp.maximum(drawn, -bound), bound).astype(kind)


def setup_inputs(seed: int = 0) -> dict:
    arg_keys = jax.random.split(jax.random.key(seed), 7)
    visibilities = centred(arg_keys[0], (SUBGRIDS, 2 * NCORR, NVIS), 1.0, 6.0, ((0, 32),))
    coords = jnp.clip(jax.random.uniform(arg_keys[1], (SUBGRIDS, 3, NVIS), jnp.float32, -12.0, 12.0) * level_of(arg_keys[1], (SUBGRIDS, 3, NVIS), ((0, 32),), -0.4, 0.0), -12.0, 12.0)
    stations = plant(jax.random.randint(arg_keys[2], (SUBGRIDS, 2), 0, STATIONS), jax.random.fold_in(arg_keys[2], 1), 0, STATIONS - 1).astype(jnp.int32)
    tile_ids_keys = jax.random.split(jax.random.fold_in(arg_keys[3], 1), SUBGRIDS // SG_DEV)
    tile_ids_turns = jax.random.permutation(jax.random.fold_in(arg_keys[3], 3), SUBGRIDS // SG_DEV)
    tile_ids = jax.vmap(lambda own, number: routed_block(jax.random.fold_in(arg_keys[3], 2), own, number, SG_DEV, NT, 1, CAP, 2))(tile_ids_keys, tile_ids_turns).reshape((SUBGRIDS, 1))
    offsets = plant(jax.random.randint(arg_keys[4], (SUBGRIDS, 2), 0, TILE_SIDE - SUB + 1), jax.random.fold_in(arg_keys[4], 1), 0, TILE_SIDE - SUB).astype(jnp.int32)
    screens = centred(arg_keys[5], (STATIONS, 2 * NCORR, PIX), 0.7, 4.0, ((0, 8),))
    return dict(visibilities=visibilities, coords=coords, stations=stations, tile_ids=tile_ids, offsets=offsets, screens=screens)


def dft_table(scale):
    index = jnp.arange(SUB, dtype=jnp.int32) - SUB // 2
    product = (index[:, None] * index[None, :]) % SUB
    angle = (-2.0 * math.pi / SUB) * product.astype(jnp.float32)
    part_re = (jnp.cos(angle) * scale).astype(jnp.bfloat16)
    part_im = (jnp.sin(angle) * scale).astype(jnp.bfloat16)
    upper = jnp.stack([part_re, part_im], axis=1)
    lower = jnp.stack([-part_im, part_re], axis=1)
    return jnp.stack([upper, lower], axis=0)


def tables():
    pixel = jnp.arange(PIX, dtype=jnp.int32)
    row_index = pixel // SUB
    col_index = pixel % SUB
    centred_row = row_index - SUB // 2
    centred_col = col_index - SUB // 2
    coord_l = centred_row.astype(jnp.float32) / SUB
    coord_m = centred_col.astype(jnp.float32) / SUB
    coord_n = -0.5 * (coord_l * coord_l + coord_m * coord_m)
    half = SUB / 2.0
    row_pos = (row_index.astype(jnp.float32) - half + 0.5) / half
    col_pos = (col_index.astype(jnp.float32) - half + 0.5) / half
    taper = (1.0 - 0.8 * row_pos * row_pos) * (1.0 - 0.8 * col_pos * col_pos)
    return coord_l, coord_m, coord_n, taper, dft_table(1.0 / SUB), dft_table(1.0)


def sandwich(image_re, image_im, near, far):
    result_re = []
    result_im = []
    for row_out in range(2):
        for col_out in range(2):
            total_re = 0.0
            total_im = 0.0
            for inner in range(2):
                mid_re = 0.0
                mid_im = 0.0
                for first in range(2):
                    near_re = near[:, 2 * first + row_out]
                    near_im = near[:, 4 + 2 * first + row_out]
                    vis_re = image_re[:, 2 * first + inner]
                    vis_im = image_im[:, 2 * first + inner]
                    mid_re = mid_re + near_re * vis_re + near_im * vis_im
                    mid_im = mid_im + near_re * vis_im - near_im * vis_re
                far_re = far[:, 2 * inner + col_out]
                far_im = far[:, 4 + 2 * inner + col_out]
                total_re = total_re + mid_re * far_re - mid_im * far_im
                total_im = total_im + mid_re * far_im + mid_im * far_re
            result_re.append(total_re)
            result_im.append(total_im)
    return jnp.stack(result_re, axis=1), jnp.stack(result_im, axis=1)


def image_blocks(visibilities, coords, near, far, tabs):
    coord_l, coord_m, coord_n, taper, col_table, row_table = tabs
    phase = (2.0 * math.pi) * (coords[:, 0, :, None] * coord_l[None, None, :] + coords[:, 1, :, None] * coord_m[None, None, :] + coords[:, 2, :, None] * coord_n[None, None, :])
    cosines = jnp.cos(phase).astype(jnp.bfloat16)
    sines = jnp.sin(phase).astype(jnp.bfloat16)
    vis_wide = visibilities.astype(jnp.float32)
    with_cos = jnp.einsum("bfv,bvp->bfp", vis_wide, cosines.astype(jnp.float32), precision=lax.Precision.HIGHEST)
    with_sin = jnp.einsum("bfv,bvp->bfp", vis_wide, sines.astype(jnp.float32), precision=lax.Precision.HIGHEST)
    image_re = (with_cos[:, :4] - with_sin[:, 4:]) * (1.0 / NVIS)
    image_im = (with_cos[:, 4:] + with_sin[:, :4]) * (1.0 / NVIS)
    out_re, out_im = sandwich(image_re, image_im, near, far)
    stacked = jnp.stack([out_re, out_im], axis=2) * taper[None, None, None, :]
    return stacked.astype(jnp.bfloat16)


def reference(visibilities, coords, stations, tile_ids, offsets, screens):
    tabs = tables()
    col_table = tabs[4].astype(jnp.float32)
    row_table = tabs[5].astype(jnp.float32)
    count = visibilities.shape[0]
    block = 16

    def one_block(item):
        vis_part, coord_part, station_part = item
        near = jnp.take(screens, station_part[:, 0], axis=0).astype(jnp.float32)
        far = jnp.take(screens, station_part[:, 1], axis=0).astype(jnp.float32)
        images = image_blocks(vis_part, coord_part, near, far, tabs)
        square = images.astype(jnp.float32).reshape(block * NCORR, 2, SUB, SUB)
        half_block = jnp.einsum("nirc,icod->nord", square, col_table, precision=lax.Precision.HIGHEST).astype(jnp.bfloat16)
        uv_square = jnp.einsum("nord,orpe->npde", half_block.astype(jnp.float32), row_table, precision=lax.Precision.HIGHEST)
        return uv_square.astype(jnp.bfloat16).reshape(block, NCORR, 2, PIX)

    blocks = lax.map(one_block, (visibilities.reshape(count // block, block, 2 * NCORR, NVIS), coords.reshape(count // block, block, 3, NVIS), stations.reshape(count // block, block, 2)))
    blocks = blocks.reshape(count, NCORR, 2, SUB, SUB)

    def place(grid, item):
        uv_block, tile_one, offset_one = item
        start = (jnp.int32(0), tile_one.astype(jnp.int32), jnp.int32(0), offset_one[0].astype(jnp.int32), offset_one[1].astype(jnp.int32))
        current = lax.dynamic_slice(grid, start, (NCORR, 1, 2, SUB, SUB))
        grid = lax.dynamic_update_slice(grid, current + uv_block.astype(jnp.float32)[:, None], start)
        return grid, None

    grid = jnp.zeros((NCORR, NT, 2, TILE_SIDE, TILE_SIDE), jnp.float32)
    grid, _ = lax.scan(place, grid, (blocks, tile_ids[:, 0], offsets))
    return grid
```

```python
import functools
import math

import jax
import jax.numpy as jnp
import numpy as np
from jax import lax
from jax.experimental import pallas as pl
from jax.experimental.pallas import tpu as pltpu
from jax.sharding import PartitionSpec as P

SUB = 32
NT = 64
TILE_SIDE = 128
PIX = SUB * SUB
LANES = 128
VMEM_LIMIT = 48 * 1024 * 1024

ROOT2 = math.sqrt(2.0)


def half_turn_series():
    grid = np.cos(np.pi * (np.arange(400) + 0.5) / 800.0) * 0.5
    z = grid * grid
    sine = np.polynomial.polynomial.Polynomial.fit(z, np.sin(np.pi * grid) / grid, 4, domain=[0, 0.25], window=[0, 0.25]).coef
    cosine = np.polynomial.polynomial.Polynomial.fit(z, np.cos(np.pi * grid), 4, domain=[0, 0.25], window=[0, 0.25]).coef
    return [float(x) * ROOT2 for x in sine], [float(x) * ROOT2 for x in cosine]


SINE, COSINE = half_turn_series()


def horner(coefficients, z):
    total = coefficients[-1]
    for value in coefficients[-2::-1]:
        total = total * z + value
    return total


def cis_turns(turns):
    t = turns - jnp.round(turns)
    z = t * t
    s = t * horner(SINE, z)
    c = horner(COSINE, z)
    return 1.0 - s * s, s * c


def image_kernel(ncorr, groups, vis_ref, coord_ref, out_ref, square):
    step = vis_ref.shape[0]
    nvis = vis_ref.shape[2]
    centred = (lax.broadcasted_iota(jnp.int32, (SUB, nvis), 0) - SUB // 2).astype(jnp.float32) * (1.0 / SUB)
    bend = 0.5 * centred * centred
    rows = ncorr * SUB

    def one(s):
        u = coord_ref[s, 0:1, :]
        v = coord_ref[s, 1:2, :]
        w = coord_ref[s, 2:3, :]
        sag = w * bend
        e_re, e_im = cis_turns(u * centred - sag)
        f_re, f_im = cis_turns(v * centred - sag)
        vis = vis_ref[s].astype(jnp.float32)
        g_re = []
        g_im = []
        for e in range(ncorr):
            vr = vis[e : e + 1]
            vi = vis[ncorr + e : ncorr + e + 1]
            g_re.append((vr * e_re - vi * e_im).astype(jnp.bfloat16))
            g_im.append((vr * e_im + vi * e_re).astype(jnp.bfloat16))
        left = jnp.concatenate([jnp.concatenate(g_re, axis=0), jnp.concatenate(g_im, axis=0)], axis=1)
        f_re = f_re.astype(jnp.bfloat16)
        f_im = f_im.astype(jnp.bfloat16)
        right = jnp.concatenate(
            [jnp.concatenate([f_re, f_im], axis=0), jnp.concatenate([-f_im, f_re], axis=0)], axis=1
        )
        image = lax.dot_general(left, right, (((1,), (1,)), ((), ())), preferred_element_type=jnp.float32)
        square[pl.ds(pl.multiple_of(s * rows, rows), rows), 0 : 2 * SUB] = image

    def several(i, carry):
        for j in range(4):
            one(i * 4 + j)
        return carry

    lax.fori_loop(0, step // 4, several, 0)

    lane = lax.broadcasted_iota(jnp.int32, (step, LANES), 1)
    per_tile = LANES // SUB
    halves = SUB // groups // per_tile
    for g in range(groups):
        for h in range(halves):
            for e in range(ncorr):
                real = None
                imag = None
                for j in range(per_tile):
                    r = (g * halves + h) * per_tile + j
                    piece = square[pl.ds(e * SUB + r, step, stride=rows), :]
                    a = piece if j == 0 else pltpu.roll(piece, SUB * j, 1)
                    b = piece if j == 1 else pltpu.roll(piece, (SUB * (j - 1)) % LANES, 1)
                    keep = lane < SUB * (j + 1)
                    real = a if real is None else jnp.where(lane < SUB * j, real, a)
                    imag = b if imag is None else jnp.where(lane < SUB * j, imag, b)
                base = h * 2 * ncorr * LANES
                out_ref[g, :, base + e * LANES : base + (e + 1) * LANES] = real.astype(jnp.bfloat16)
                out_ref[g, :, base + (ncorr + e) * LANES : base + (ncorr + e + 1) * LANES] = imag.astype(jnp.bfloat16)


def make_images(visibilities, coords, groups):
    count, fields, nvis = visibilities.shape
    ncorr = fields // 2
    step = 16
    width = fields * PIX // groups
    return pl.pallas_call(
        functools.partial(image_kernel, ncorr, groups),
        grid=(count // step,),
        in_specs=[
            pl.BlockSpec((step, fields, nvis), lambda i: (i, 0, 0)),
            pl.BlockSpec((step, 3, nvis), lambda i: (i, 0, 0)),
        ],
        out_specs=pl.BlockSpec((groups, step, width), lambda i: (0, i, 0)),
        out_shape=jax.ShapeDtypeStruct((groups, count, width), jnp.bfloat16),
        scratch_shapes=[pltpu.VMEM((step * ncorr * SUB, LANES), jnp.float32)],
        compiler_params=pltpu.CompilerParams(vmem_limit_bytes=VMEM_LIMIT),
        cost_estimate=pl.CostEstimate(flops=count * 2 * 128 * 512 * 256, bytes_accessed=2 << 20, transcendentals=0),
        name="images",
    )(visibilities, coords)


def owner_targets(tiles, owners, per_owner, capacity):
    n = tiles.shape[1]
    mine = lax.broadcasted_iota(jnp.int32, (owners, n), 0) == tiles // per_owner
    hot = mine.astype(jnp.float32).astype(jnp.bfloat16)
    before = lax.broadcasted_iota(jnp.int32, (n, n), 0) < lax.broadcasted_iota(jnp.int32, (n, n), 1)
    before = before.astype(jnp.float32).astype(jnp.bfloat16)
    ahead = jnp.dot(hot, before, preferred_element_type=jnp.float32)
    first = (lax.broadcasted_iota(jnp.int32, (owners, n), 0) * capacity).astype(jnp.float32)
    return jnp.sum(jnp.where(mine, ahead + first, 0.0), axis=0, keepdims=True)


def aterm_kernel(ncorr, owners, per_owner, capacity, stations_ref, tiles_ref, taper_ref, image_ref, screen_ref, out_ref, near_ref, far_ref, block_ref):
    n = image_ref.shape[0]
    nst = screen_ref.shape[0]
    number = lax.broadcasted_iota(jnp.int32, (n, nst), 1)
    for column, ref in ((0, near_ref), (1, far_ref)):
        pick = (number == stations_ref[:, column : column + 1]).astype(jnp.float32).astype(jnp.bfloat16)
        ref[...] = jnp.dot(pick, screen_ref[...], preferred_element_type=jnp.float32)
    taper = taper_ref[0]
    chunk = 16

    def part(ref, rows, field):
        return ref[rows, field * LANES : (field + 1) * LANES].astype(jnp.float32)

    def body(i, carry):
        rows = pl.ds(pl.multiple_of(i * chunk, chunk), chunk)
        image_re = [part(image_ref, rows, e) for e in range(ncorr)]
        image_im = [part(image_ref, rows, ncorr + e) for e in range(ncorr)]
        for row_out in range(2):
            mid_re = []
            mid_im = []
            for inner in range(2):
                m_re = 0.0
                m_im = 0.0
                for first in range(2):
                    near_re = part(near_ref, rows, 2 * first + row_out)
                    near_im = part(near_ref, rows, ncorr + 2 * first + row_out)
                    vis_re = image_re[2 * first + inner]
                    vis_im = image_im[2 * first + inner]
                    m_re = m_re + near_re * vis_re + near_im * vis_im
                    m_im = m_im + near_re * vis_im - near_im * vis_re
                mid_re.append(m_re)
                mid_im.append(m_im)
            for col_out in range(2):
                t_re = 0.0
                t_im = 0.0
                for inner in range(2):
                    far_re = part(far_ref, rows, 2 * inner + col_out)
                    far_im = part(far_ref, rows, ncorr + 2 * inner + col_out)
                    t_re = t_re + mid_re[inner] * far_re - mid_im[inner] * far_im
                    t_im = t_im + mid_re[inner] * far_im + mid_im[inner] * far_re
                place = 2 * (2 * row_out + col_out) * LANES
                block_ref[rows, place : place + LANES] = (t_re * taper).astype(jnp.bfloat16)
                block_ref[rows, place + LANES : place + 2 * LANES] = (t_im * taper).astype(jnp.bfloat16)
        return carry

    lax.fori_loop(0, n // chunk, body, 0)
    target = owner_targets(tiles_ref[...], owners, per_owner, capacity)
    slots = lax.broadcasted_iota(jnp.int32, (owners * capacity, n), 0).astype(jnp.float32)
    move = (slots == target).astype(jnp.float32).astype(jnp.bfloat16)
    for e in range(ncorr):
        moved = jnp.dot(move, block_ref[:, 2 * e * LANES : 2 * (e + 1) * LANES], preferred_element_type=jnp.float32)
        out_ref[e] = moved.astype(jnp.bfloat16)


def apply_aterms(images, screens, stations, tiles, taper, ncorr, owners, per_owner, capacity):
    n = images.shape[0]
    nst = screens.shape[0]
    fields = 2 * ncorr
    halves = images.shape[1] // (fields * LANES)
    half = fields * LANES
    return pl.pallas_call(
        functools.partial(aterm_kernel, ncorr, owners, per_owner, capacity),
        grid=(halves,),
        in_specs=[
            pl.BlockSpec((n, 2), lambda h: (0, 0)),
            pl.BlockSpec((1, n), lambda h: (0, 0)),
            pl.BlockSpec((1, 1, LANES), lambda h: (h, 0, 0)),
            pl.BlockSpec((n, half), lambda h: (0, h)),
            pl.BlockSpec((nst, half), lambda h: (0, h)),
        ],
        out_specs=pl.BlockSpec((ncorr, owners * capacity, 2 * LANES), lambda h: (0, 0, h)),
        out_shape=jax.ShapeDtypeStruct((ncorr, owners * capacity, halves * 2 * LANES), jnp.bfloat16),
        scratch_shapes=[
            pltpu.VMEM((n, half), jnp.float32),
            pltpu.VMEM((n, half), jnp.float32),
            pltpu.VMEM((n, half), jnp.bfloat16),
        ],
        compiler_params=pltpu.CompilerParams(vmem_limit_bytes=VMEM_LIMIT),
        name="aterms",
    )(stations, tiles, taper, images, screens)


def places_kernel(owners, per_owner, capacity, tiles_ref, offset_ref, out_ref):
    me = lax.axis_index("tile")
    sources = tiles_ref.shape[0]
    n = tiles_ref.shape[2]
    for t in range(sources):
        tiles = tiles_ref[t]
        target = owner_targets(tiles, owners, per_owner, capacity)
        slots = lax.broadcasted_iota(jnp.int32, (capacity, n), 0) + me * capacity
        hit = (slots.astype(jnp.float32) == target).astype(jnp.float32).astype(jnp.bfloat16)
        local = jnp.where(tiles // per_owner == me, tiles - me * per_owner, 0).astype(jnp.float32)
        used = jnp.where(tiles // per_owner == me, 1.0, 0.0)
        total = jnp.broadcast_to(jnp.sum(used, axis=1, keepdims=True), (1, n))
        offsets = offset_ref[t].astype(jnp.float32)
        values = jnp.concatenate([offsets, local, used, jnp.zeros((4, n), jnp.float32)], axis=0).astype(jnp.bfloat16)
        found = lax.dot_general(values, hit, (((1,), (1,)), ((), ())), preferred_element_type=jnp.float32)
        row = lax.broadcasted_iota(jnp.int32, found.shape, 0)
        out_ref[t] = jnp.where(row == 4, total[:, :capacity], found).astype(jnp.int32)


def find_places(tiles, offsets, owners, per_owner, capacity):
    sources = tiles.shape[0]
    return pl.pallas_call(
        functools.partial(places_kernel, owners, per_owner, capacity),
        out_shape=jax.ShapeDtypeStruct((sources, 8, capacity), jnp.int32),
        compiler_params=pltpu.CompilerParams(vmem_limit_bytes=VMEM_LIMIT),
        name="places",
    )(tiles, offsets)


def grid_kernel(sources, capacity, place_ref, block_ref, factor_ref, out_ref, uv_ref):
    step = pl.program_id(0)
    groups = block_ref.shape[0]
    depth = block_ref.shape[2]
    rows = block_ref.shape[1]
    width = factor_ref.shape[1]
    per_slot = 2 * PIX // LANES
    total = None
    for g in range(groups):
        part = jnp.dot(
            block_ref[g], factor_ref[g * depth : (g + 1) * depth, :], preferred_element_type=jnp.float32
        )
        total = part if total is None else total + part
    for j in range(width // LANES):
        uv_ref[pl.ds(step * (width // LANES) + j, rows, stride=per_slot), :] = total[:, j * LANES : (j + 1) * LANES]

    @pl.when(step == pl.num_programs(0) - 1)
    def _():
        out_ref[...] = jnp.zeros_like(out_ref)
        lane = lax.broadcasted_iota(jnp.int32, (8, LANES), 1)
        pieces = LANES // SUB

        for t in range(sources):

            def add(j, carry):
                x = place_ref[t, 0, j]
                y = place_ref[t, 1, j]
                k = place_ref[t, 2, j]
                inside = (lane >= y) & (lane < y + SUB)
                base = pl.multiple_of((t * capacity + j) * per_slot, per_slot)
                new = []
                for part in range(2):
                    block = uv_ref[pl.ds(base + part * 8, 8), :]
                    for g in range(pieces):
                        turned = pltpu.roll(block, lax.rem(y + (LANES - g * SUB), LANES), 1)
                        old = out_ref[k, part, pl.ds(x + 8 * g, 8), :]
                        new.append(old + jnp.where(inside, turned, 0.0))
                for part in range(2):
                    for g in range(pieces):
                        out_ref[k, part, pl.ds(x + 8 * g, 8), :] = new[part * pieces + g]
                return carry

            lax.fori_loop(0, place_ref[t, 4, 0], add, 0)


def place_on_grid(places, blocks, factors, per_owner, capacity):
    groups, rows, depth = blocks.shape
    sources = rows // capacity
    width = 2 * LANES
    return pl.pallas_call(
        functools.partial(grid_kernel, sources, capacity),
        grid=(factors.shape[1] // width,),
        in_specs=[
            pl.BlockSpec(memory_space=pltpu.SMEM),
            pl.BlockSpec((groups, rows, depth), lambda i: (0, 0, 0)),
            pl.BlockSpec((factors.shape[0], width), lambda i: (0, i)),
        ],
        out_specs=pl.BlockSpec((per_owner, 2, TILE_SIDE, TILE_SIDE), lambda i: (0, 0, 0, 0)),
        out_shape=jax.ShapeDtypeStruct((per_owner, 2, TILE_SIDE, TILE_SIDE), jnp.float32),
        scratch_shapes=[pltpu.VMEM((rows * 2 * PIX // LANES, LANES), jnp.float32)],
        compiler_params=pltpu.CompilerParams(vmem_limit_bytes=VMEM_LIMIT),
        name="grid",
    )(places, blocks, factors)


def uv_factors():
    per_tile = LANES // SUB
    index = np.arange(SUB) - SUB // 2
    angle = -2.0 * np.pi / SUB * ((index[:, None] * index[None, :]) % SUB)
    factor = np.exp(1j * angle)
    both = (factor / SUB)[None, :, :, None] * factor[:, None, None, :]
    both = both.reshape(SUB // per_tile, per_tile, SUB, SUB // 8, 8, SUB).transpose(0, 1, 2, 4, 3, 5)
    table = np.empty((SUB // per_tile, 2, per_tile, SUB, 2, 8, SUB // 8, SUB))
    table[:, 0, :, :, 0] = both.real
    table[:, 0, :, :, 1] = both.imag
    table[:, 1, :, :, 0] = -both.imag
    table[:, 1, :, :, 1] = both.real
    return table.reshape(2 * PIX, 2 * PIX).astype(jnp.bfloat16)


def taper_table(scale):
    pos = (np.arange(SUB) - SUB / 2 + 0.5) / (SUB / 2)
    one = 1.0 - 0.8 * pos * pos
    return (one[:, None] * one[None, :] * scale).astype(np.float32)


def per_device(visibilities, coords, stations, tile_ids, offsets, screens):
    count, fields, nvis = visibilities.shape
    ncorr = fields // 2
    groups = lax.axis_size("corr")
    owners = lax.axis_size("tile")
    corr = lax.axis_index("corr")
    tile = lax.axis_index("tile")
    per_owner = NT // owners
    capacity = per_owner * groups * (2 * count // NT)
    local = PIX // groups
    halves = local // LANES

    meta = jnp.concatenate([tile_ids, offsets, stations], axis=1)
    every = lax.all_gather(meta, ("corr", "tile"), axis=0, tiled=True).reshape(groups, owners, count, 5)
    station_list = lax.dynamic_index_in_dim(every, tile, axis=1, keepdims=False)[..., 3:].reshape(groups * count, 2)
    by_row = jnp.transpose(every[..., :3], (3, 1, 0, 2)).reshape(3, owners, groups * count)
    all_tiles = by_row[0][:, None, :]
    all_offsets = jnp.transpose(by_row[1:], (1, 0, 2))
    my_tiles = lax.dynamic_index_in_dim(all_tiles, tile, axis=0, keepdims=False)

    part = lax.dynamic_slice_in_dim(screens, corr * local, local, axis=2)
    part = part.reshape(-1, fields, halves, LANES).transpose(0, 2, 1, 3).reshape(-1, fields * local)
    all_screens = lax.all_gather(part, "tile", axis=0, tiled=True)

    images = make_images(visibilities, coords, groups)
    images = lax.all_to_all(images, "corr", split_axis=0, concat_axis=0, tiled=True)
    images = images.reshape(groups * count, fields * local)

    taper = jnp.asarray(taper_table(1.0 / nvis)).reshape(groups, halves, 1, LANES)
    taper = lax.dynamic_index_in_dim(taper, corr, axis=0, keepdims=False)
    sending = apply_aterms(images, all_screens, station_list, my_tiles, taper, ncorr, owners, per_owner, capacity)
    received = lax.all_to_all(
        sending.reshape(groups * owners, capacity, 2 * local), ("corr", "tile"), split_axis=0, concat_axis=0, tiled=True
    )
    places = find_places(all_tiles, all_offsets, owners, per_owner, capacity)
    factors = jnp.asarray(uv_factors())
    grid = place_on_grid(places, received.reshape(groups, owners * capacity, 2 * local), factors, per_owner, capacity)
    return grid[None]


def solution(mesh):
    return jax.shard_map(
        per_device,
        mesh=mesh,
        in_specs=(
            P(("corr", "tile"), None, None),
            P(("corr", "tile"), None, None),
            P(("corr", "tile"), None),
            P(("corr", "tile"), None),
            P(("corr", "tile"), None),
            P("tile", None, None),
        ),
        out_specs=P("corr", "tile", None, None, None),
        check_vma=False,
    )
```

```python
import functools
import math

import jax
import jax.numpy as jnp
import numpy as np
from jax import lax
from jax.experimental import pallas as pl
from jax.experimental.pallas import tpu as pltpu
from jax.sharding import PartitionSpec as P

SUB = 32
NT = 64
TILE_SIDE = 128
PIX = SUB * SUB
LANES = 128
VMEM_LIMIT = 48 * 1024 * 1024

ROOT2 = math.sqrt(2.0)


def half_turn_series():
    grid = np.cos(np.pi * (np.arange(400) + 0.5) / 800.0) * 0.5
    z = grid * grid
    sine = np.polynomial.polynomial.Polynomial.fit(z, np.sin(np.pi * grid) / grid, 4, domain=[0, 0.25], window=[0, 0.25]).coef
    cosine = np.polynomial.polynomial.Polynomial.fit(z, np.cos(np.pi * grid), 4, domain=[0, 0.25], window=[0, 0.25]).coef
    return [float(x) * ROOT2 for x in sine], [float(x) * ROOT2 for x in cosine]


SINE, COSINE = half_turn_series()


def horner(coefficients, z):
    total = coefficients[-1]
    for value in coefficients[-2::-1]:
        total = total * z + value
    return total


def cis_turns(turns):
    t = turns - jnp.round(turns)
    z = t * t
    s = t * horner(SINE, z)
    c = horner(COSINE, z)
    return 1.0 - s * s, s * c


def image_kernel(ncorr, groups, vis_ref, coord_ref, station_ref, tile_ref, offset_ref, out_ref, square):
    step = vis_ref.shape[0]
    nvis = vis_ref.shape[2]
    centred = (lax.broadcasted_iota(jnp.int32, (SUB, nvis), 0) - SUB // 2).astype(jnp.float32) * (1.0 / SUB)
    bend = 0.5 * centred * centred
    rows = ncorr * SUB

    def one(s):
        u = coord_ref[s, 0:1, :]
        v = coord_ref[s, 1:2, :]
        w = coord_ref[s, 2:3, :]
        sag = w * bend
        e_re, e_im = cis_turns(u * centred - sag)
        f_re, f_im = cis_turns(v * centred - sag)
        vis = vis_ref[s].astype(jnp.float32)
        g_re = []
        g_im = []
        for e in range(ncorr):
            vr = vis[e : e + 1]
            vi = vis[ncorr + e : ncorr + e + 1]
            g_re.append((vr * e_re - vi * e_im).astype(jnp.bfloat16))
            g_im.append((vr * e_im + vi * e_re).astype(jnp.bfloat16))
        left = jnp.concatenate([jnp.concatenate(g_re, axis=0), jnp.concatenate(g_im, axis=0)], axis=1)
        f_re = f_re.astype(jnp.bfloat16)
        f_im = f_im.astype(jnp.bfloat16)
        right = jnp.concatenate(
            [jnp.concatenate([f_re, f_im], axis=0), jnp.concatenate([-f_im, f_re], axis=0)], axis=1
        )
        image = lax.dot_general(left, right, (((1,), (1,)), ((), ())), preferred_element_type=jnp.float32)
        square[pl.ds(pl.multiple_of(s * rows, rows), rows), 0 : 2 * SUB] = image

    def several(i, carry):
        for j in range(4):
            one(i * 4 + j)
        return carry

    lax.fori_loop(0, step // 4, several, 0)

    lane = lax.broadcasted_iota(jnp.int32, (step, LANES), 1)
    per_tile = LANES // SUB
    halves = SUB // groups // per_tile
    for g in range(groups):
        for h in range(halves):
            for e in range(ncorr):
                real = None
                imag = None
                for j in range(per_tile):
                    r = (g * halves + h) * per_tile + j
                    piece = square[pl.ds(e * SUB + r, step, stride=rows), :]
                    a = piece if j == 0 else pltpu.roll(piece, SUB * j, 1)
                    b = piece if j == 1 else pltpu.roll(piece, (SUB * (j - 1)) % LANES, 1)
                    keep = lane < SUB * (j + 1)
                    real = a if real is None else jnp.where(lane < SUB * j, real, a)
                    imag = b if imag is None else jnp.where(lane < SUB * j, imag, b)
                base = h * 2 * ncorr * LANES
                out_ref[g, :, base + e * LANES : base + (e + 1) * LANES] = real.astype(jnp.bfloat16)
                out_ref[g, :, base + (ncorr + e) * LANES : base + (ncorr + e + 1) * LANES] = imag.astype(jnp.bfloat16)
    near = station_ref[:, 0:1]
    far = station_ref[:, 1:2]
    facts = (tile_ref[...], offset_ref[:, 0:1], offset_ref[:, 1:2], near // 256, near % 256, far // 256, far % 256)
    table = jnp.zeros((step, LANES), jnp.int32)
    for i, fact in enumerate(facts):
        table = jnp.where(lane == i, fact, table)
    table = table.astype(jnp.float32).astype(jnp.bfloat16)
    for g in range(groups):
        out_ref[g, :, 2 * ncorr * halves * LANES :] = table


def make_images(visibilities, coords, stations, tile_ids, offsets, groups):
    count, fields, nvis = visibilities.shape
    ncorr = fields // 2
    step = 16
    width = fields * PIX // groups + LANES
    return pl.pallas_call(
        functools.partial(image_kernel, ncorr, groups),
        grid=(count // step,),
        in_specs=[
            pl.BlockSpec((step, fields, nvis), lambda i: (i, 0, 0)),
            pl.BlockSpec((step, 3, nvis), lambda i: (i, 0, 0)),
            pl.BlockSpec((step, 2), lambda i: (i, 0)),
            pl.BlockSpec((step, 1), lambda i: (i, 0)),
            pl.BlockSpec((step, 2), lambda i: (i, 0)),
        ],
        out_specs=pl.BlockSpec((groups, step, width), lambda i: (0, i, 0)),
        out_shape=jax.ShapeDtypeStruct((groups, count, width), jnp.bfloat16),
        scratch_shapes=[pltpu.VMEM((step * ncorr * SUB, LANES), jnp.float32)],
        compiler_params=pltpu.CompilerParams(vmem_limit_bytes=VMEM_LIMIT),
        cost_estimate=pl.CostEstimate(flops=count * 2 * 128 * 512 * 256, bytes_accessed=2 << 20, transcendentals=0),
        name="images",
    )(visibilities, coords, stations, tile_ids, offsets)


def send_rows(owners, per_owner, window, half, facts, block_ref, out_ref):
    first, rows = window
    n = facts.shape[0]
    ncorr = out_ref.shape[0]
    slots = rows - 1
    turned = jnp.transpose(facts)
    owner = jnp.floor(turned[0:1] * (1.0 / per_owner))
    mine = lax.broadcasted_iota(jnp.int32, (owners, n), 0).astype(jnp.float32) == owner
    hot = mine.astype(jnp.float32)
    before = lax.broadcasted_iota(jnp.int32, (n, n), 0) < lax.broadcasted_iota(jnp.int32, (n, n), 1)
    ahead = jnp.dot(
        hot.astype(jnp.bfloat16), before.astype(jnp.float32).astype(jnp.bfloat16), preferred_element_type=jnp.float32
    )
    rank = jnp.sum(hot * ahead, axis=0, keepdims=True) - first
    fits = (rank >= 0.0) & (rank < float(slots))

    def chosen(pitch):
        place = jnp.where(fits, owner * pitch + rank, -1.0)
        row = lax.broadcasted_iota(jnp.int32, (owners * pitch, n), 0).astype(jnp.float32)
        return (row == place).astype(jnp.float32).astype(jnp.bfloat16)

    facts_here = jnp.concatenate(
        [turned[1:3], turned[0:1] - owner * per_owner, jnp.zeros((5, n), jnp.float32)], axis=0
    ).astype(jnp.bfloat16)
    found = lax.dot_general(facts_here, chosen(LANES), (((1,), (1,)), ((), ())), preferred_element_type=jnp.float32)
    held = jnp.sum(hot, axis=1, keepdims=True)
    most = jnp.max(held, axis=0, keepdims=True)
    here = jnp.minimum(jnp.maximum(held - first, 0.0), float(slots))
    lane = lax.broadcasted_iota(jnp.int32, (1, LANES), 1)
    labels = []
    for o in range(owners):
        span = slice(o * LANES, (o + 1) * LANES)
        counts = jnp.where(lane == 0, here[o : o + 1], jnp.where(lane == 1, most, 0.0))
        left = jnp.where(half == 0, found[0:1, span], found[2:3, span])
        right = jnp.where(half == 0, found[1:2, span], counts)
        labels.append(jnp.concatenate([left, right], axis=1))
    move = chosen(rows)
    last = lax.broadcasted_iota(jnp.int32, (16, 2 * LANES), 0) == 15
    for e in range(ncorr):
        moved = jnp.dot(move, block_ref[:, 2 * e * LANES : 2 * (e + 1) * LANES], preferred_element_type=jnp.float32)
        out_ref[e] = moved.astype(jnp.bfloat16)
        for o in range(owners):
            end = (o + 1) * rows
            out_ref[e, end - 16 : end, :] = jnp.where(last, labels[o], moved[end - 16 : end]).astype(jnp.bfloat16)


def aterm_kernel(ncorr, owners, per_owner, window, facts_ref, taper_ref, image_ref, screen_ref, out_ref, block_ref, near_ref, far_ref):
    n = image_ref.shape[0]
    nst = screen_ref.shape[0]
    facts = facts_ref[...].astype(jnp.float32)
    number = lax.broadcasted_iota(jnp.int32, (n, nst), 1).astype(jnp.float32)
    for column, ref in ((3, near_ref), (5, far_ref)):
        station = facts[:, column : column + 1] * 256.0 + facts[:, column + 1 : column + 2]
        pick = (number == station).astype(jnp.float32).astype(jnp.bfloat16)
        ref[...] = jnp.dot(pick, screen_ref[...], preferred_element_type=jnp.float32)
    taper = taper_ref[0]
    chunk = 16

    def part(ref, rows, field):
        return ref[rows, field * LANES : (field + 1) * LANES].astype(jnp.float32)

    def body(i, carry):
        rows = pl.ds(pl.multiple_of(i * chunk, chunk), chunk)
        image_re = [part(image_ref, rows, e) for e in range(ncorr)]
        image_im = [part(image_ref, rows, ncorr + e) for e in range(ncorr)]
        for row_out in range(2):
            mid_re = []
            mid_im = []
            for inner in range(2):
                m_re = 0.0
                m_im = 0.0
                for first in range(2):
                    near_re = part(near_ref, rows, 2 * first + row_out)
                    near_im = part(near_ref, rows, ncorr + 2 * first + row_out)
                    vis_re = image_re[2 * first + inner]
                    vis_im = image_im[2 * first + inner]
                    m_re = m_re + near_re * vis_re + near_im * vis_im
                    m_im = m_im + near_re * vis_im - near_im * vis_re
                mid_re.append(m_re)
                mid_im.append(m_im)
            for col_out in range(2):
                t_re = 0.0
                t_im = 0.0
                for inner in range(2):
                    far_re = part(far_ref, rows, 2 * inner + col_out)
                    far_im = part(far_ref, rows, ncorr + 2 * inner + col_out)
                    t_re = t_re + mid_re[inner] * far_re - mid_im[inner] * far_im
                    t_im = t_im + mid_re[inner] * far_im + mid_im[inner] * far_re
                place = 2 * (2 * row_out + col_out) * LANES
                block_ref[rows, place : place + LANES] = (t_re * taper).astype(jnp.bfloat16)
                block_ref[rows, place + LANES : place + 2 * LANES] = (t_im * taper).astype(jnp.bfloat16)
        return carry

    lax.fori_loop(0, n // chunk, body, 0)
    send_rows(owners, per_owner, window, pl.program_id(0), facts, block_ref, out_ref)


def apply_aterms(images, screens, taper, ncorr, owners, per_owner, window):
    n = images.shape[0]
    nst = screens.shape[0]
    half = 2 * ncorr * LANES
    halves = screens.shape[1] // half
    rows = owners * window[1]
    return pl.pallas_call(
        functools.partial(aterm_kernel, ncorr, owners, per_owner, window),
        grid=(halves,),
        in_specs=[
            pl.BlockSpec((n, LANES), lambda h: (0, halves * 2 * ncorr)),
            pl.BlockSpec((1, 1, LANES), lambda h: (h, 0, 0)),
            pl.BlockSpec((n, half), lambda h: (0, h)),
            pl.BlockSpec((nst, half), lambda h: (0, h)),
        ],
        out_specs=[
            pl.BlockSpec((ncorr, rows, 2 * LANES), lambda h: (0, 0, h)),
            pl.BlockSpec((n, half), lambda h: (0, h)),
        ],
        out_shape=[
            jax.ShapeDtypeStruct((ncorr, rows, halves * 2 * LANES), jnp.bfloat16),
            jax.ShapeDtypeStruct((n, halves * half), jnp.bfloat16),
        ],
        scratch_shapes=[pltpu.VMEM((n, half), jnp.float32), pltpu.VMEM((n, half), jnp.float32)],
        compiler_params=pltpu.CompilerParams(vmem_limit_bytes=VMEM_LIMIT),
        name="aterms",
    )(images, taper, images, screens)


def rest_kernel(owners, per_owner, window, facts_ref, block_ref, out_ref):
    send_rows(owners, per_owner, window, pl.program_id(0), facts_ref[...].astype(jnp.float32), block_ref, out_ref)


def send_rest(images, blocks, ncorr, owners, per_owner, window):
    n = images.shape[0]
    half = 2 * ncorr * LANES
    halves = blocks.shape[1] // half
    rows = owners * window[1]
    return pl.pallas_call(
        functools.partial(rest_kernel, owners, per_owner, window),
        grid=(halves,),
        in_specs=[
            pl.BlockSpec((n, LANES), lambda h: (0, halves * 2 * ncorr)),
            pl.BlockSpec((n, half), lambda h: (0, h)),
        ],
        out_specs=pl.BlockSpec((ncorr, rows, 2 * LANES), lambda h: (0, 0, h)),
        out_shape=jax.ShapeDtypeStruct((ncorr, rows, halves * 2 * LANES), jnp.bfloat16),
        compiler_params=pltpu.CompilerParams(vmem_limit_bytes=VMEM_LIMIT),
        name="rest",
    )(images, blocks)


def grid_kernel(rows, block_ref, col_ref, row_ref, before_ref, out_ref, most_ref, half_ref, uv_ref, turned_ref, re_a, im_a, re_b, im_b, label_ref, place_ref, sem):
    groups, total, depth = block_ref.shape
    sources = total // rows
    per_slot = 2 * PIX // LANES
    quarters = depth // LANES
    for t in range(sources):
        end = (t + 1) * rows
        label_ref[t : t + 1, :] = block_ref[0, end - 16 : end, :].astype(jnp.float32)[15:16].astype(jnp.int32)
    fetch = pltpu.make_async_copy(label_ref, place_ref, sem)
    fetch.start()

    for g in range(groups):
        half_ref[g] = jnp.dot(block_ref[g], col_ref[...], preferred_element_type=jnp.float32).astype(jnp.bfloat16)
    for q in range(quarters):
        left = jnp.concatenate([half_ref[g, :, q * LANES : (q + 1) * LANES] for g in range(groups)], axis=1)
        uv = jnp.dot(left, row_ref[...], preferred_element_type=jnp.float32)
        for part in range(2):
            for i in range(2):
                j = part * 2 + i
                uv_ref[pl.ds(part * 8 + 2 * q + i, total, stride=per_slot), :] = uv[:, j * LANES : (j + 1) * LANES]
    for t in range(sources):
        uv_ref[((t + 1) * rows - 1) * per_slot : (t + 1) * rows * per_slot, :] = jnp.zeros((per_slot, LANES), jnp.float32)
    for ref in (re_a, im_a, re_b, im_b):
        ref[...] = jnp.zeros_like(ref)
    fetch.wait()

    lane = lax.broadcasted_iota(jnp.int32, (8, LANES), 1)
    pieces = LANES // SUB
    tall = 2 * pieces * 8
    batch = 8
    most = jnp.int32(0)
    for t in range(sources):
        count = place_ref[t, 3 * LANES]
        most = jnp.maximum(most, place_ref[t, 3 * LANES + 1])

        def turn(i, carry):
            for b in range(batch):
                j = i * batch + b
                y = place_ref[t, LANES + j]
                inside = (lane >= y) & (lane < y + SUB)
                slot = t * rows + j
                for part in range(2):
                    block = uv_ref[pl.ds(pl.multiple_of(slot * per_slot + part * 8, 8), 8), :]
                    for g in range(pieces):
                        moved = pltpu.roll(block, (y + (LANES - g * SUB)) & (LANES - 1), 1)
                        at = pl.multiple_of(slot * tall + (part * pieces + g) * 8, 8)
                        turned_ref[pl.ds(at, 8), :] = jnp.where(inside, moved, 0.0)
            return carry

        lax.fori_loop(0, (count + (batch - 1)) // batch, turn, 0)

        def add(i, carry):
            for b in range(4):
                j = i * 4 + b
                row = place_ref[t, 2 * LANES + j] * TILE_SIDE + place_ref[t, j]
                slot = t * rows + j
                for part, ref in enumerate((re_a, im_a) if b % 2 == 0 else (re_b, im_b)):
                    at = pl.multiple_of(slot * tall + part * pieces * 8, 8)
                    ref[pl.ds(row, SUB), :] = ref[pl.ds(row, SUB), :] + turned_ref[pl.ds(at, SUB), :]
            return carry

        lax.fori_loop(0, (count + 3) // 4, add, 0)

    most_ref[0] = most
    for k in range(out_ref.shape[0]):
        span = slice(k * TILE_SIDE, (k + 1) * TILE_SIDE)
        for part, (one, two) in enumerate(((re_a, re_b), (im_a, im_b))):
            value = one[span, :] + two[span, :]
            if before_ref is not None:
                value = value + before_ref[k, part]
            out_ref[k, part] = value


def first_grid_kernel(rows, block_ref, col_ref, row_ref, *refs):
    grid_kernel(rows, block_ref, col_ref, row_ref, None, *refs)


def place_on_grid(blocks, rows, tables, per_owner, before=None):
    groups, total, depth = blocks.shape
    sources = total // rows
    shape = (per_owner, 2, TILE_SIDE, TILE_SIDE)
    whole = pl.BlockSpec(memory_space=pltpu.VMEM)
    accumulator = pltpu.VMEM((per_owner * TILE_SIDE, TILE_SIDE), jnp.float32)
    given = (blocks,) + tables + (() if before is None else (before,))
    return pl.pallas_call(
        functools.partial(first_grid_kernel if before is None else grid_kernel, rows),
        in_specs=[whole] * len(given),
        out_specs=[whole, pl.BlockSpec(memory_space=pltpu.SMEM)],
        out_shape=[jax.ShapeDtypeStruct(shape, jnp.float32), jax.ShapeDtypeStruct((1,), jnp.int32)],
        scratch_shapes=[
            pltpu.VMEM((groups, total, depth), jnp.bfloat16),
            pltpu.VMEM((total * 2 * PIX // LANES, LANES), jnp.float32),
            pltpu.VMEM((total * 2 * PIX // SUB, LANES), jnp.float32),
            accumulator,
            accumulator,
            accumulator,
            accumulator,
            pltpu.VMEM((sources, depth), jnp.int32),
            pltpu.SMEM((sources, depth), jnp.int32),
            pltpu.SemaphoreType.DMA(()),
        ],
        compiler_params=pltpu.CompilerParams(vmem_limit_bytes=VMEM_LIMIT),
        name="grid",
    )(*given)


def uv_tables(groups):
    quad = LANES // SUB
    halves = SUB // (groups * quad)
    index = np.arange(SUB) - SUB // 2
    factor = np.exp(-2j * np.pi / SUB * ((index[:, None] * index[None, :]) % SUB))

    def parts(table, axis):
        upper = np.stack([table.real, table.imag], axis=axis)
        lower = np.stack([-table.imag, table.real], axis=axis)
        return upper, lower

    col = (factor / SUB).reshape(SUB, 4, 4, 2).transpose(2, 0, 3, 1)
    first = np.zeros((halves, 2, quad, SUB, 4, halves, 2, quad, 2, 4))
    for p, table in enumerate(parts(col, 0)):
        for h in range(halves):
            for r in range(quad):
                first[h, p, r, :, :, h, :, r] = table.transpose(2, 1, 0, 3, 4)
    second = np.zeros((groups, halves, 2, quad, 2, 4, 2, 2, 4, SUB))
    row = factor.reshape(groups, halves, quad, SUB)
    for p, table in enumerate(parts(row, 0)):
        for i in range(2):
            for g in range(4):
                second[:, :, p, :, i, g, :, i, g, :] = table.transpose(1, 2, 3, 0, 4)
    size = halves * 2 * LANES
    first = first.reshape(size, 4 * halves * 2 * quad * 8)
    second = second.reshape(groups * halves * 2 * quad * 8, 4 * LANES)
    return first.astype(jnp.bfloat16), second.astype(jnp.bfloat16)


def taper_table(scale):
    pos = (np.arange(SUB) - SUB / 2 + 0.5) / (SUB / 2)
    one = 1.0 - 0.8 * pos * pos
    return (one[:, None] * one[None, :] * scale).astype(np.float32)


def per_device(visibilities, coords, stations, tile_ids, offsets, screens):
    count, fields, nvis = visibilities.shape
    ncorr = fields // 2
    groups = lax.axis_size("corr")
    owners = lax.axis_size("tile")
    corr = lax.axis_index("corr")
    tile = lax.axis_index("tile")
    per_owner = NT // owners
    full = per_owner * groups * (2 * count // NT)
    rows = -(-full * 3 // 64) * 16
    local = PIX // groups
    halves = local // LANES

    part = lax.dynamic_slice_in_dim(screens, corr * local, local, axis=2)
    part = part.reshape(-1, fields, halves, LANES).transpose(0, 2, 1, 3).reshape(-1, fields * local)
    all_screens = lax.all_gather(part, "tile", axis=0, tiled=True)

    images = make_images(visibilities, coords, stations, tile_ids, offsets, groups)
    images = lax.all_to_all(images, "corr", split_axis=0, concat_axis=0, tiled=True)
    images = images.reshape(groups * count, -1)

    taper = jnp.asarray(taper_table(1.0 / nvis)).reshape(groups, halves, 1, LANES)
    taper = lax.dynamic_index_in_dim(taper, corr, axis=0, keepdims=False)
    tables = tuple(jnp.asarray(table) for table in uv_tables(groups))

    def exchange(sending, rows):
        received = lax.all_to_all(
            sending.reshape(groups * owners, rows, 2 * local), ("corr", "tile"), split_axis=0, concat_axis=0, tiled=True
        )
        return received.reshape(groups, owners * rows, 2 * local)

    sending, blocks = apply_aterms(images, all_screens, taper, ncorr, owners, per_owner, (0, rows))
    grid, most = place_on_grid(exchange(sending, rows), rows, tables, per_owner)
    slots = rows - 1
    if slots < full:
        more = -(-(full - slots + 1) // 16) * 16

        def overflow(grid):
            rest = send_rest(images, blocks, ncorr, owners, per_owner, (slots, more))
            return place_on_grid(exchange(rest, more), more, tables, per_owner, grid)[0]

        grid = lax.cond(most[0] > slots, overflow, lambda grid: grid, grid)
    return grid[None]


def solution(mesh):
    return jax.shard_map(
        per_device,
        mesh=mesh,
        in_specs=(
            P(("corr", "tile"), None, None),
            P(("corr", "tile"), None, None),
            P(("corr", "tile"), None),
            P(("corr", "tile"), None),
            P(("corr", "tile"), None),
            P("tile", None, None),
        ),
        out_specs=P("corr", "tile", None, None, None),
        check_vma=False,
    )
```

```python
import functools
import math

import jax
import jax.numpy as jnp
import numpy as np
from jax import lax
from jax.experimental import pallas as pl
from jax.experimental.pallas import tpu as pltpu
from jax.sharding import PartitionSpec as P

SUB = 32
NT = 64
TILE_SIDE = 128
PIX = SUB * SUB
LANES = 128
VMEM_LIMIT = 48 * 1024 * 1024

ROOT2 = math.sqrt(2.0)


def half_turn_series():
    grid = np.cos(np.pi * (np.arange(400) + 0.5) / 800.0) * 0.5
    z = grid * grid
    sine = np.polynomial.polynomial.Polynomial.fit(z, np.sin(np.pi * grid) / grid, 4, domain=[0, 0.25], window=[0, 0.25]).coef
    cosine = np.polynomial.polynomial.Polynomial.fit(z, np.cos(np.pi * grid), 4, domain=[0, 0.25], window=[0, 0.25]).coef
    return [float(x) * ROOT2 for x in sine], [float(x) * ROOT2 for x in cosine]


SINE, COSINE = half_turn_series()


def horner(coefficients, z):
    total = coefficients[-1]
    for value in coefficients[-2::-1]:
        total = total * z + value
    return total


def cis_turns(turns):
    t = turns - jnp.round(turns)
    z = t * t
    s = t * horner(SINE, z)
    c = horner(COSINE, z)
    return 1.0 - s * s, s * c


def image_kernel(ncorr, groups, vis_ref, coord_ref, station_ref, tile_ref, offset_ref, *refs):
    out_refs, square = refs[:-1], refs[-1]
    step = vis_ref.shape[0]
    nvis = vis_ref.shape[2]
    centred = (lax.broadcasted_iota(jnp.int32, (SUB, nvis), 0) - SUB // 2).astype(jnp.float32) * (1.0 / SUB)
    bend = 0.5 * centred * centred
    rows = ncorr * SUB

    def one(s):
        u = coord_ref[0, pl.ds(s, 1), :]
        v = coord_ref[1, pl.ds(s, 1), :]
        w = coord_ref[2, pl.ds(s, 1), :]
        sag = w * bend
        e_re, e_im = cis_turns(u * centred - sag)
        f_re, f_im = cis_turns(v * centred - sag)
        vis = vis_ref[s].astype(jnp.float32)
        g_re = []
        g_im = []
        for e in range(ncorr):
            vr = vis[e : e + 1]
            vi = vis[ncorr + e : ncorr + e + 1]
            g_re.append((vr * e_re - vi * e_im).astype(jnp.bfloat16))
            g_im.append((vr * e_im + vi * e_re).astype(jnp.bfloat16))
        left = jnp.concatenate([jnp.concatenate(g_re, axis=0), jnp.concatenate(g_im, axis=0)], axis=1)
        f_re = f_re.astype(jnp.bfloat16)
        f_im = f_im.astype(jnp.bfloat16)
        right = jnp.concatenate(
            [jnp.concatenate([f_re, f_im], axis=0), jnp.concatenate([-f_im, f_re], axis=0)], axis=1
        )
        image = lax.dot_general(left, right, (((1,), (1,)), ((), ())), preferred_element_type=jnp.float32)
        square[pl.ds(pl.multiple_of(s * rows, rows), rows), 0 : 2 * SUB] = image

    def several(i, carry):
        for j in range(4):
            one(i * 4 + j)
        return carry

    lax.fori_loop(0, step // 4, several, 0)

    lane = lax.broadcasted_iota(jnp.int32, (step, LANES), 1)
    per_tile = LANES // SUB
    halves = SUB // groups // per_tile
    for g in range(groups):
        for h in range(halves):
            for e in range(ncorr):
                real = None
                imag = None
                for j in range(per_tile):
                    r = (g * halves + h) * per_tile + j
                    piece = square[pl.ds(e * SUB + r, step, stride=rows), :]
                    a = piece if j == 0 else pltpu.roll(piece, SUB * j, 1)
                    b = piece if j == 1 else pltpu.roll(piece, (SUB * (j - 1)) % LANES, 1)
                    keep = lane < SUB * (j + 1)
                    real = a if real is None else jnp.where(lane < SUB * j, real, a)
                    imag = b if imag is None else jnp.where(lane < SUB * j, imag, b)
                out_refs[h][g, :, e * LANES : (e + 1) * LANES] = real.astype(jnp.bfloat16)
                out_refs[h][g, :, (ncorr + e) * LANES : (ncorr + e + 1) * LANES] = imag.astype(jnp.bfloat16)
    near = station_ref[0:1]
    far = station_ref[1:2]
    facts = (tile_ref[...], offset_ref[0:1], offset_ref[1:2], near // 256, near % 256, far // 256, far % 256)
    count = near.shape[1]
    field = lax.broadcasted_iota(jnp.int32, (LANES, count), 0)
    table = jnp.zeros((LANES, count), jnp.int32)
    for i, fact in enumerate(facts):
        table = jnp.where(field == i, fact, table)
    mine = lax.broadcasted_iota(jnp.int32, (step, count), 0) + pl.program_id(0) * step
    mine = (mine == lax.broadcasted_iota(jnp.int32, (step, count), 1)).astype(jnp.float32).astype(jnp.bfloat16)
    table = table.astype(jnp.float32).astype(jnp.bfloat16)
    table = lax.dot_general(mine, table, (((1,), (1,)), ((), ())), preferred_element_type=jnp.float32)
    for g in range(groups):
        out_refs[0][g, :, 2 * ncorr * LANES :] = table.astype(jnp.bfloat16)


def make_images(visibilities, coords, stations, tile_ids, offsets, groups):
    count, fields, nvis = visibilities.shape
    ncorr = fields // 2
    step = 16
    halves = PIX // (groups * LANES)
    widths = [fields * LANES + (LANES if h == 0 else 0) for h in range(halves)]
    return pl.pallas_call(
        functools.partial(image_kernel, ncorr, groups),
        grid=(count // step,),
        in_specs=[
            pl.BlockSpec((step, fields, nvis), lambda i: (i, 0, 0)),
            pl.BlockSpec((3, step, nvis), lambda i: (0, i, 0)),
            pl.BlockSpec((2, count), lambda i: (0, 0)),
            pl.BlockSpec((1, count), lambda i: (0, 0)),
            pl.BlockSpec((2, count), lambda i: (0, 0)),
        ],
        out_specs=[pl.BlockSpec((groups, step, width), lambda i: (0, i, 0)) for width in widths],
        out_shape=[jax.ShapeDtypeStruct((groups, count, width), jnp.bfloat16) for width in widths],
        scratch_shapes=[pltpu.VMEM((step * ncorr * SUB, LANES), jnp.float32)],
        compiler_params=pltpu.CompilerParams(vmem_limit_bytes=VMEM_LIMIT),
        cost_estimate=pl.CostEstimate(flops=count << 27, bytes_accessed=2 << 20, transcendentals=0),
        name="images",
    )(visibilities, jnp.transpose(coords, (1, 0, 2)), stations.T, tile_ids.T, offsets.T)


def send_rows(owners, per_owner, window, half, facts, block_ref, out_ref):
    first, rows = window
    n = facts.shape[0]
    ncorr = out_ref.shape[0]
    slots = rows - 1
    turned = jnp.transpose(facts)
    owner = jnp.floor(turned[0:1] * (1.0 / per_owner))
    mine = lax.broadcasted_iota(jnp.int32, (owners, n), 0).astype(jnp.float32) == owner
    hot = mine.astype(jnp.float32)
    before = lax.broadcasted_iota(jnp.int32, (n, n), 0) < lax.broadcasted_iota(jnp.int32, (n, n), 1)
    ahead = jnp.dot(
        hot.astype(jnp.bfloat16), before.astype(jnp.float32).astype(jnp.bfloat16), preferred_element_type=jnp.float32
    )
    rank = jnp.sum(hot * ahead, axis=0, keepdims=True) - first
    fits = (rank >= 0.0) & (rank < float(slots))

    def chosen(pitch):
        place = jnp.where(fits, owner * pitch + rank, -1.0)
        row = lax.broadcasted_iota(jnp.int32, (owners * pitch, n), 0).astype(jnp.float32)
        return (row == place).astype(jnp.float32).astype(jnp.bfloat16)

    facts_here = jnp.concatenate(
        [turned[1:3], turned[0:1] - owner * per_owner, jnp.zeros((5, n), jnp.float32)], axis=0
    ).astype(jnp.bfloat16)
    found = lax.dot_general(facts_here, chosen(LANES), (((1,), (1,)), ((), ())), preferred_element_type=jnp.float32)
    held = jnp.sum(hot, axis=1, keepdims=True)
    most = jnp.max(held, axis=0, keepdims=True)
    here = jnp.minimum(jnp.maximum(held - first, 0.0), float(slots))
    lane = lax.broadcasted_iota(jnp.int32, (1, LANES), 1)
    labels = []
    for o in range(owners):
        span = slice(o * LANES, (o + 1) * LANES)
        counts = jnp.where(lane == 0, here[o : o + 1], jnp.where(lane == 1, most, 0.0))
        both = [found[0:1, span], found[1:2, span]] if half == 0 else [found[2:3, span], counts]
        labels.append(jnp.concatenate(both, axis=1))
    move = chosen(rows)
    last = lax.broadcasted_iota(jnp.int32, (16, 2 * LANES), 0) == 15
    for e in range(ncorr):
        moved = jnp.dot(move, block_ref[:, 2 * e * LANES : 2 * (e + 1) * LANES], preferred_element_type=jnp.float32)
        out_ref[e] = moved.astype(jnp.bfloat16)
        for o in range(owners):
            end = (o + 1) * rows
            out_ref[e, end - 16 : end, :] = jnp.where(last, labels[o], moved[end - 16 : end]).astype(jnp.bfloat16)


def aterm_kernel(ncorr, owners, per_owner, window, half, facts_ref, taper_ref, image_ref, screen_ref, out_ref, block_ref, near_ref, far_ref):
    n = image_ref.shape[0]
    nst = screen_ref.shape[0]
    facts = facts_ref[...].astype(jnp.float32)
    number = lax.broadcasted_iota(jnp.int32, (n, nst), 1).astype(jnp.float32)
    for column, ref in ((3, near_ref), (5, far_ref)):
        station = facts[:, column : column + 1] * 256.0 + facts[:, column + 1 : column + 2]
        pick = (number == station).astype(jnp.float32).astype(jnp.bfloat16)
        ref[...] = jnp.dot(pick, screen_ref[...], preferred_element_type=jnp.float32)
    taper = taper_ref[...]
    chunk = 16

    def part(ref, rows, field):
        return ref[rows, field * LANES : (field + 1) * LANES].astype(jnp.float32)

    def body(i, carry):
        rows = pl.ds(pl.multiple_of(i * chunk, chunk), chunk)
        image_re = [part(image_ref, rows, e) for e in range(ncorr)]
        image_im = [part(image_ref, rows, ncorr + e) for e in range(ncorr)]
        for row_out in range(2):
            mid_re = []
            mid_im = []
            for inner in range(2):
                m_re = 0.0
                m_im = 0.0
                for first in range(2):
                    near_re = part(near_ref, rows, 2 * first + row_out)
                    near_im = part(near_ref, rows, ncorr + 2 * first + row_out)
                    vis_re = image_re[2 * first + inner]
                    vis_im = image_im[2 * first + inner]
                    m_re = m_re + near_re * vis_re + near_im * vis_im
                    m_im = m_im + near_re * vis_im - near_im * vis_re
                mid_re.append(m_re)
                mid_im.append(m_im)
            for col_out in range(2):
                t_re = 0.0
                t_im = 0.0
                for inner in range(2):
                    far_re = part(far_ref, rows, 2 * inner + col_out)
                    far_im = part(far_ref, rows, ncorr + 2 * inner + col_out)
                    t_re = t_re + mid_re[inner] * far_re - mid_im[inner] * far_im
                    t_im = t_im + mid_re[inner] * far_im + mid_im[inner] * far_re
                place = 2 * (2 * row_out + col_out) * LANES
                block_ref[rows, place : place + LANES] = (t_re * taper).astype(jnp.bfloat16)
                block_ref[rows, place + LANES : place + 2 * LANES] = (t_im * taper).astype(jnp.bfloat16)
        return carry

    lax.fori_loop(0, n // chunk, body, 0)
    send_rows(owners, per_owner, window, half, facts, block_ref, out_ref)


def apply_aterms(facts, images, screens, taper, ncorr, owners, per_owner, window, half):
    n = images.shape[0]
    nst, width = screens.shape
    rows = owners * window[1]
    whole = lambda shape: pl.BlockSpec(shape, lambda i: (0, 0))
    return pl.pallas_call(
        functools.partial(aterm_kernel, ncorr, owners, per_owner, window, half),
        grid=(1,),
        in_specs=[
            pl.BlockSpec((n, LANES), lambda i: (0, 2 * ncorr)),
            whole((1, LANES)),
            whole((n, width)),
            whole((nst, width)),
        ],
        out_specs=[pl.BlockSpec((ncorr, rows, 2 * LANES), lambda i: (0, 0, 0)), whole((n, width))],
        out_shape=[
            jax.ShapeDtypeStruct((ncorr, rows, 2 * LANES), jnp.bfloat16),
            jax.ShapeDtypeStruct((n, width), jnp.bfloat16),
        ],
        scratch_shapes=[pltpu.VMEM((n, width), jnp.float32), pltpu.VMEM((n, width), jnp.float32)],
        compiler_params=pltpu.CompilerParams(vmem_limit_bytes=VMEM_LIMIT),
        cost_estimate=pl.CostEstimate(flops=3 << 30, bytes_accessed=4 << 20, transcendentals=0),
        name="aterms",
    )(facts, taper, images, screens)


def rest_kernel(owners, per_owner, window, half, facts_ref, block_ref, out_ref):
    send_rows(owners, per_owner, window, half, facts_ref[...].astype(jnp.float32), block_ref, out_ref)


def send_rest(facts, block, ncorr, owners, per_owner, window, half):
    n, width = block.shape
    rows = owners * window[1]
    return pl.pallas_call(
        functools.partial(rest_kernel, owners, per_owner, window, half),
        grid=(1,),
        in_specs=[
            pl.BlockSpec((n, LANES), lambda i: (0, 2 * ncorr)),
            pl.BlockSpec((n, width), lambda i: (0, 0)),
        ],
        out_specs=pl.BlockSpec((ncorr, rows, 2 * LANES), lambda i: (0, 0, 0)),
        out_shape=jax.ShapeDtypeStruct((ncorr, rows, 2 * LANES), jnp.bfloat16),
        compiler_params=pltpu.CompilerParams(vmem_limit_bytes=VMEM_LIMIT),
        name="rest",
    )(facts, block)


def column_kernel(block_ref, col_ref, out_ref):
    for g in range(block_ref.shape[0]):
        out_ref[g] = jnp.dot(block_ref[g], col_ref[...], preferred_element_type=jnp.float32).astype(jnp.bfloat16)


def transform_columns(blocks, table):
    groups, total, depth = blocks.shape
    return pl.pallas_call(
        column_kernel,
        out_shape=jax.ShapeDtypeStruct((groups, total, table.shape[1]), jnp.bfloat16),
        compiler_params=pltpu.CompilerParams(vmem_limit_bytes=VMEM_LIMIT),
        cost_estimate=pl.CostEstimate(flops=2 << 30, bytes_accessed=4 << 20, transcendentals=0),
        name="columns",
    )(blocks, table)


def grid_kernel(rows, first_ref, done_ref, block_ref, col_ref, row_ref, before_ref, out_ref, most_ref, half_ref, uv_ref, turned_ref, re_a, im_a, re_b, im_b, label_ref, place_ref, sem):
    groups, total, depth = done_ref.shape
    sources = total // rows
    per_slot = 2 * PIX // LANES
    quarters = depth // LANES
    for t in range(sources):
        end = (t + 1) * rows
        for h, ref in enumerate((first_ref, block_ref)):
            label = ref[0, end - 16 : end, :].astype(jnp.float32)[15:16].astype(jnp.int32)
            label_ref[t : t + 1, 2 * h * LANES : 2 * (h + 1) * LANES] = label
    fetch = pltpu.make_async_copy(label_ref, place_ref, sem)
    fetch.start()

    for g in range(groups):
        rest = jnp.dot(block_ref[g], col_ref[...], preferred_element_type=jnp.float32).astype(jnp.bfloat16)
        half_ref[g] = done_ref[g] + rest
    for q in range(quarters):
        left = jnp.concatenate([half_ref[g, :, q * LANES : (q + 1) * LANES] for g in range(groups)], axis=1)
        uv = jnp.dot(left, row_ref[...], preferred_element_type=jnp.float32)
        for part in range(2):
            for i in range(2):
                j = part * 2 + i
                uv_ref[pl.ds(part * 8 + 2 * q + i, total, stride=per_slot), :] = uv[:, j * LANES : (j + 1) * LANES]
    for t in range(sources):
        uv_ref[((t + 1) * rows - 1) * per_slot : (t + 1) * rows * per_slot, :] = jnp.zeros((per_slot, LANES), jnp.float32)
    for ref in (re_a, im_a, re_b, im_b):
        ref[...] = jnp.zeros_like(ref)
    fetch.wait()

    lane = lax.broadcasted_iota(jnp.int32, (8, LANES), 1)
    pieces = LANES // SUB
    tall = 2 * pieces * 8
    batch = 8
    most = jnp.int32(0)
    for t in range(sources):
        count = place_ref[t, 3 * LANES]
        most = jnp.maximum(most, place_ref[t, 3 * LANES + 1])

        def turn(i, carry):
            for b in range(batch):
                j = i * batch + b
                y = place_ref[t, LANES + j]
                inside = (lane >= y) & (lane < y + SUB)
                slot = t * rows + j
                for part in range(2):
                    block = uv_ref[pl.ds(pl.multiple_of(slot * per_slot + part * 8, 8), 8), :]
                    for g in range(pieces):
                        moved = pltpu.roll(block, (y + (LANES - g * SUB)) & (LANES - 1), 1)
                        at = pl.multiple_of(slot * tall + (part * pieces + g) * 8, 8)
                        turned_ref[pl.ds(at, 8), :] = jnp.where(inside, moved, 0.0)
            return carry

        lax.fori_loop(0, (count + (batch - 1)) // batch, turn, 0)

        def add(i, carry):
            for b in range(4):
                j = i * 4 + b
                row = place_ref[t, 2 * LANES + j] * TILE_SIDE + place_ref[t, j]
                slot = t * rows + j
                for part, ref in enumerate((re_a, im_a) if b % 2 == 0 else (re_b, im_b)):
                    at = pl.multiple_of(slot * tall + part * pieces * 8, 8)
                    ref[pl.ds(row, SUB), :] = ref[pl.ds(row, SUB), :] + turned_ref[pl.ds(at, SUB), :]
            return carry

        lax.fori_loop(0, (count + 3) // 4, add, 0)

    most_ref[0] = most
    for k in range(out_ref.shape[0]):
        span = slice(k * TILE_SIDE, (k + 1) * TILE_SIDE)
        for part, (one, two) in enumerate(((re_a, re_b), (im_a, im_b))):
            value = one[span, :] + two[span, :]
            if before_ref is not None:
                value = value + before_ref[k, part]
            out_ref[k, part] = value


def first_grid_kernel(rows, first_ref, done_ref, block_ref, col_ref, row_ref, *refs):
    grid_kernel(rows, first_ref, done_ref, block_ref, col_ref, row_ref, None, *refs)


def place_on_grid(first, done, block, rows, tables, per_owner, before=None):
    groups, total, depth = done.shape
    sources = total // rows
    shape = (per_owner, 2, TILE_SIDE, TILE_SIDE)
    whole = pl.BlockSpec(memory_space=pltpu.VMEM)
    accumulator = pltpu.VMEM((per_owner * TILE_SIDE, TILE_SIDE), jnp.float32)
    given = (first, done, block) + tables + (() if before is None else (before,))
    return pl.pallas_call(
        functools.partial(first_grid_kernel if before is None else grid_kernel, rows),
        in_specs=[whole] * len(given),
        out_specs=[whole, pl.BlockSpec(memory_space=pltpu.SMEM)],
        out_shape=[jax.ShapeDtypeStruct(shape, jnp.float32), jax.ShapeDtypeStruct((1,), jnp.int32)],
        scratch_shapes=[
            pltpu.VMEM((groups, total, depth), jnp.bfloat16),
            pltpu.VMEM((total * 2 * PIX // LANES, LANES), jnp.float32),
            pltpu.VMEM((total * 2 * PIX // SUB, LANES), jnp.float32),
            accumulator,
            accumulator,
            accumulator,
            accumulator,
            pltpu.VMEM((sources, depth), jnp.int32),
            pltpu.SMEM((sources, depth), jnp.int32),
            pltpu.SemaphoreType.DMA(()),
        ],
        compiler_params=pltpu.CompilerParams(vmem_limit_bytes=VMEM_LIMIT),
        name="grid",
    )(*given)


def uv_tables(groups):
    quad = LANES // SUB
    halves = SUB // (groups * quad)
    index = np.arange(SUB) - SUB // 2
    factor = np.exp(-2j * np.pi / SUB * ((index[:, None] * index[None, :]) % SUB))

    def parts(table, axis):
        upper = np.stack([table.real, table.imag], axis=axis)
        lower = np.stack([-table.imag, table.real], axis=axis)
        return upper, lower

    col = (factor / SUB).reshape(SUB, 4, 4, 2).transpose(2, 0, 3, 1)
    first = np.zeros((halves, 2, quad, SUB, 4, halves, 2, quad, 2, 4))
    for p, table in enumerate(parts(col, 0)):
        for h in range(halves):
            for r in range(quad):
                first[h, p, r, :, :, h, :, r] = table.transpose(2, 1, 0, 3, 4)
    second = np.zeros((groups, halves, 2, quad, 2, 4, 2, 2, 4, SUB))
    row = factor.reshape(groups, halves, quad, SUB)
    for p, table in enumerate(parts(row, 0)):
        for i in range(2):
            for g in range(4):
                second[:, :, p, :, i, g, :, i, g, :] = table.transpose(1, 2, 3, 0, 4)
    size = halves * 2 * LANES
    first = first.reshape(size, 4 * halves * 2 * quad * 8)
    second = second.reshape(groups * halves * 2 * quad * 8, 4 * LANES)
    return first.astype(jnp.bfloat16), second.astype(jnp.bfloat16)


def taper_table(scale):
    pos = (np.arange(SUB) - SUB / 2 + 0.5) / (SUB / 2)
    one = 1.0 - 0.8 * pos * pos
    return (one[:, None] * one[None, :] * scale).astype(np.float32)


def per_device(visibilities, coords, stations, tile_ids, offsets, screens):
    count, fields, nvis = visibilities.shape
    ncorr = fields // 2
    groups = lax.axis_size("corr")
    owners = lax.axis_size("tile")
    corr = lax.axis_index("corr")
    tile = lax.axis_index("tile")
    per_owner = NT // owners
    full = per_owner * groups * (2 * count // NT)
    rows = -(-full * 3 // 64) * 16
    halves = PIX // (groups * LANES)

    screen_parts = []
    for h in range(halves):
        part = lax.dynamic_slice_in_dim(screens, (corr * halves + h) * LANES, LANES, axis=2)
        screen_parts.append(lax.all_gather(part.reshape(-1, fields * LANES), "tile", axis=0, tiled=True))

    images = make_images(visibilities, coords, stations, tile_ids, offsets, groups)
    images = [lax.all_to_all(part, "corr", split_axis=0, concat_axis=0, tiled=True) for part in images]
    images = [part.reshape(groups * count, -1) for part in images]
    facts = images[0]

    taper = jnp.asarray(taper_table(1.0 / nvis)).reshape(groups, halves, 1, LANES)
    taper = lax.dynamic_index_in_dim(taper, corr, axis=0, keepdims=False)
    col_table, row_table = uv_tables(groups)
    col_tables = [jnp.asarray(col_table[h * 2 * LANES : (h + 1) * 2 * LANES]) for h in range(halves)]
    row_table = jnp.asarray(row_table)

    def exchange(sending, rows):
        received = lax.all_to_all(
            sending.reshape(groups * owners, rows, -1), ("corr", "tile"), split_axis=0, concat_axis=0, tiled=True
        )
        return received.reshape(groups, owners * rows, -1)

    def finish(received, rows, before=None):
        done = transform_columns(received[0], col_tables[0])
        return place_on_grid(received[0], done, received[1], rows, (col_tables[1], row_table), per_owner, before)

    received = []
    blocks = []
    for h in range(halves):
        sending, block = apply_aterms(facts, images[h], screen_parts[h], taper[h], ncorr, owners, per_owner, (0, rows), h)
        received.append(exchange(sending, rows))
        blocks.append(block)
    grid, most = finish(received, rows)
    slots = rows - 1
    if slots < full:
        more = -(-(full - slots + 1) // 16) * 16

        def overflow(grid):
            rest = [send_rest(facts, blocks[h], ncorr, owners, per_owner, (slots, more), h) for h in range(halves)]
            return finish([exchange(part, more) for part in rest], more, grid)[0]

        grid = lax.cond(most[0] > slots, overflow, lambda grid: grid, grid)
    return grid[None]


def solution(mesh):
    return jax.shard_map(
        per_device,
        mesh=mesh,
        in_specs=(
            P(("corr", "tile"), None, None),
            P(("corr", "tile"), None, None),
            P(("corr", "tile"), None),
            P(("corr", "tile"), None),
            P(("corr", "tile"), None),
            P("tile", None, None),
        ),
        out_specs=P("corr", "tile", None, None, None),
        check_vma=False,
    )
```

```python
import functools
import math

import jax
import jax.numpy as jnp
import numpy as np
from jax import lax
from jax.experimental import pallas as pl
from jax.experimental.pallas import tpu as pltpu
from jax.sharding import PartitionSpec as P

SUB = 32
NT = 64
TILE_SIDE = 128
PIX = SUB * SUB
LANES = 128
VMEM_LIMIT = 36 * 1024 * 1024
VMEM_ALL = 63 * 1024 * 1024 + 512 * 1024

ROOT2 = math.sqrt(2.0)


def half_turn_series():
    grid = np.cos(np.pi * (np.arange(400) + 0.5) / 800.0) * 0.5
    z = grid * grid
    sine = np.polynomial.polynomial.Polynomial.fit(z, np.sin(np.pi * grid) / grid, 4, domain=[0, 0.25], window=[0, 0.25]).coef
    cosine = np.polynomial.polynomial.Polynomial.fit(z, np.cos(np.pi * grid), 4, domain=[0, 0.25], window=[0, 0.25]).coef
    return [float(x) * ROOT2 for x in sine], [float(x) * ROOT2 for x in cosine]


SINE, COSINE = half_turn_series()


def horner(coefficients, z):
    total = coefficients[-1]
    for value in coefficients[-2::-1]:
        total = total * z + value
    return total


def cis_turns(turns):
    t = turns - jnp.round(turns)
    z = t * t
    s = t * horner(SINE, z)
    c = horner(COSINE, z)
    return 1.0 - s * s, s * c


def image_kernel(ncorr, groups, begin, vis_ref, coord_ref, station_ref, tile_ref, offset_ref, *refs):
    out_refs, square = refs[:-1], refs[-1]
    me = lax.axis_index("corr")
    step = vis_ref.shape[0]
    nvis = vis_ref.shape[2]
    centred = (lax.broadcasted_iota(jnp.int32, (SUB, nvis), 0) - SUB // 2).astype(jnp.float32) * (1.0 / SUB)
    bend = 0.5 * centred * centred
    rows = ncorr * SUB

    def one(s):
        u = coord_ref[0, pl.ds(s, 1), :]
        v = coord_ref[1, pl.ds(s, 1), :]
        w = coord_ref[2, pl.ds(s, 1), :]
        sag = w * bend
        e_re, e_im = cis_turns(u * centred - sag)
        f_re, f_im = cis_turns(v * centred - sag)
        vis = vis_ref[s].astype(jnp.float32)
        g_re = []
        g_im = []
        for e in range(ncorr):
            vr = vis[e : e + 1]
            vi = vis[ncorr + e : ncorr + e + 1]
            g_re.append((vr * e_re - vi * e_im).astype(jnp.bfloat16))
            g_im.append((vr * e_im + vi * e_re).astype(jnp.bfloat16))
        left = jnp.concatenate([jnp.concatenate(g_re, axis=0), jnp.concatenate(g_im, axis=0)], axis=1)
        f_re = f_re.astype(jnp.bfloat16)
        f_im = f_im.astype(jnp.bfloat16)
        right = jnp.concatenate(
            [jnp.concatenate([f_re, f_im], axis=0), jnp.concatenate([-f_im, f_re], axis=0)], axis=1
        )
        image = lax.dot_general(left, right, (((1,), (1,)), ((), ())), preferred_element_type=jnp.float32)
        square[pl.ds(pl.multiple_of(s * rows, rows), rows), 0 : 2 * SUB] = image

    def several(i, carry):
        for j in range(4):
            one(i * 4 + j)
        return carry

    lax.fori_loop(0, step // 4, several, 0)

    lane = lax.broadcasted_iota(jnp.int32, (step, LANES), 1)
    per_tile = LANES // SUB
    halves = SUB // groups // per_tile
    for d in range(groups):
        first = (me ^ d) * (halves * per_tile)
        for h in range(halves):
            for e in range(ncorr):
                real = None
                imag = None
                for j in range(per_tile):
                    piece = square[pl.ds(first + (e * SUB + h * per_tile + j), step, stride=rows), :]
                    a = piece if j == 0 else pltpu.roll(piece, SUB * j, 1)
                    b = piece if j == 1 else pltpu.roll(piece, (SUB * (j - 1)) % LANES, 1)
                    keep = lane < SUB * (j + 1)
                    real = a if real is None else jnp.where(lane < SUB * j, real, a)
                    imag = b if imag is None else jnp.where(lane < SUB * j, imag, b)
                base = h * 2 * ncorr * LANES
                out_refs[d][:, base + e * LANES : base + (e + 1) * LANES] = real.astype(jnp.bfloat16)
                out_refs[d][:, base + (ncorr + e) * LANES : base + (ncorr + e + 1) * LANES] = imag.astype(jnp.bfloat16)
    near = station_ref[0:1]
    far = station_ref[1:2]
    facts = (tile_ref[...], offset_ref[0:1], offset_ref[1:2], near // 256, near % 256, far // 256, far % 256)
    count = near.shape[1]
    field = lax.broadcasted_iota(jnp.int32, (LANES, count), 0)
    table = jnp.zeros((LANES, count), jnp.int32)
    for i, fact in enumerate(facts):
        table = jnp.where(field == i, fact, table)
    mine = lax.broadcasted_iota(jnp.int32, (step, count), 0) + (pl.program_id(0) + begin) * step
    mine = (mine == lax.broadcasted_iota(jnp.int32, (step, count), 1)).astype(jnp.float32).astype(jnp.bfloat16)
    table = table.astype(jnp.float32).astype(jnp.bfloat16)
    table = lax.dot_general(mine, table, (((1,), (1,)), ((), ())), preferred_element_type=jnp.float32)
    for out_ref in out_refs:
        out_ref[:, 2 * ncorr * halves * LANES :] = table.astype(jnp.bfloat16)


def make_images(visibilities, coords, stations, tile_ids, offsets, groups, part, parts):
    count, fields, nvis = visibilities.shape
    ncorr = fields // 2
    step = 16
    width = fields * PIX // groups + LANES
    size = count // parts
    begin = part * size // step
    return pl.pallas_call(
        functools.partial(image_kernel, ncorr, groups, begin),
        grid=(size // step,),
        in_specs=[
            pl.BlockSpec((step, fields, nvis), lambda i: (i + begin, 0, 0)),
            pl.BlockSpec((3, step, nvis), lambda i: (0, i + begin, 0)),
            pl.BlockSpec((2, count), lambda i: (0, 0)),
            pl.BlockSpec((1, count), lambda i: (0, 0)),
            pl.BlockSpec((2, count), lambda i: (0, 0)),
        ],
        out_specs=[pl.BlockSpec((step, width), lambda i: (i, 0))] * groups,
        out_shape=[jax.ShapeDtypeStruct((size, width), jnp.bfloat16)] * groups,
        scratch_shapes=[pltpu.VMEM((step * ncorr * SUB, LANES), jnp.float32)],
        compiler_params=pltpu.CompilerParams(vmem_limit_bytes=VMEM_ALL),
        cost_estimate=pl.CostEstimate(flops=size << 27, bytes_accessed=2 << 20, transcendentals=0),
        name="images",
    )(visibilities, jnp.transpose(coords, (1, 0, 2)), stations.T, tile_ids.T, offsets.T)


def send_rows(owners, per_owner, window, half, facts, block_ref, out_ref):
    first, rows = window
    n = facts.shape[0]
    ncorr = out_ref.shape[0]
    slots = rows - 1
    turned = jnp.transpose(facts)
    owner = jnp.floor(turned[0:1] * (1.0 / per_owner))
    mine = lax.broadcasted_iota(jnp.int32, (owners, n), 0).astype(jnp.float32) == owner
    hot = mine.astype(jnp.float32)
    before = lax.broadcasted_iota(jnp.int32, (n, n), 0) < lax.broadcasted_iota(jnp.int32, (n, n), 1)
    ahead = jnp.dot(
        hot.astype(jnp.bfloat16), before.astype(jnp.float32).astype(jnp.bfloat16), preferred_element_type=jnp.float32
    )
    rank = jnp.sum(hot * ahead, axis=0, keepdims=True) - first
    fits = (rank >= 0.0) & (rank < float(slots))

    def chosen(pitch):
        place = jnp.where(fits, owner * pitch + rank, -1.0)
        row = lax.broadcasted_iota(jnp.int32, (owners * pitch, n), 0).astype(jnp.float32)
        return (row == place).astype(jnp.float32).astype(jnp.bfloat16)

    facts_here = jnp.concatenate(
        [turned[1:3], turned[0:1] - owner * per_owner, jnp.zeros((5, n), jnp.float32)], axis=0
    ).astype(jnp.bfloat16)
    found = lax.dot_general(facts_here, chosen(LANES), (((1,), (1,)), ((), ())), preferred_element_type=jnp.float32)
    held = jnp.sum(hot, axis=1, keepdims=True)
    most = jnp.max(held, axis=0, keepdims=True)
    here = jnp.minimum(jnp.maximum(held - first, 0.0), float(slots))
    lane = lax.broadcasted_iota(jnp.int32, (1, LANES), 1)
    labels = []
    for o in range(owners):
        span = slice(o * LANES, (o + 1) * LANES)
        counts = jnp.where(lane == 0, here[o : o + 1], jnp.where(lane == 1, most, 0.0))
        left = jnp.where(half == 0, found[0:1, span], found[2:3, span])
        right = jnp.where(half == 0, found[1:2, span], counts)
        labels.append(jnp.concatenate([left, right], axis=1))
    move = chosen(rows)
    last = lax.broadcasted_iota(jnp.int32, (16, 2 * LANES), 0) == 15
    for e in range(ncorr):
        moved = jnp.dot(move, block_ref[:, 2 * e * LANES : 2 * (e + 1) * LANES], preferred_element_type=jnp.float32)
        out_ref[e] = moved.astype(jnp.bfloat16)
        for o in range(owners):
            end = (o + 1) * rows
            out_ref[e, end - 16 : end, :] = jnp.where(last, labels[o], moved[end - 16 : end]).astype(jnp.bfloat16)


def aterm_kernel(ncorr, owners, per_owner, window, groups, *refs):
    pieces = (len(refs) - 8) // 2
    facts_refs, refs = refs[:pieces], refs[pieces:]
    image_refs, refs = refs[:pieces], refs[pieces:]
    taper_ref, mine_ref, other_ref, out_ref, block_ref, facts_ref, near_ref, far_ref = refs
    count = image_refs[0].shape[0]
    n = pieces * count
    share_of = n // groups
    nst = mine_ref.shape[0] + other_ref.shape[0]
    me = lax.axis_index("corr")
    for p in range(pieces):
        at = pl.multiple_of((me ^ (p % groups)) * share_of + p // groups * count, count)
        facts_ref[pl.ds(at, count), :] = facts_refs[p][...].astype(jnp.float32)
    facts = facts_ref[...]
    number = lax.broadcasted_iota(jnp.int32, (n, nst), 1).astype(jnp.float32)
    share = float(nst // owners)
    side = (lax.axis_index("tile") & 1).astype(jnp.float32)
    for column, ref in ((3, near_ref), (5, far_ref)):
        station = facts[:, column : column + 1] * 256.0 + facts[:, column + 1 : column + 2]
        holder = jnp.floor(station * (1.0 / share))
        pair = jnp.floor(holder * 0.5)
        station = station - (holder - pair) * share + jnp.where(holder - 2.0 * pair == side, 0.0, float(nst // 2))
        pick = (number == station).astype(jnp.float32).astype(jnp.bfloat16)
        screens = jnp.concatenate([mine_ref[...], other_ref[...]], axis=0)
        ref[...] = jnp.dot(pick, screens, preferred_element_type=jnp.float32)
    taper = taper_ref[0]
    chunk = 16

    def part(ref, rows, field):
        return ref[rows, field * LANES : (field + 1) * LANES].astype(jnp.float32)

    def body(p, i, carry):
        held = pl.ds(pl.multiple_of(i * chunk, chunk), chunk)
        at = (me ^ (p % groups)) * share_of + p // groups * count + i * chunk
        rows = pl.ds(pl.multiple_of(at, chunk), chunk)
        image_re = [part(image_refs[p], held, e) for e in range(ncorr)]
        image_im = [part(image_refs[p], held, ncorr + e) for e in range(ncorr)]
        for row_out in range(2):
            mid_re = []
            mid_im = []
            for inner in range(2):
                m_re = 0.0
                m_im = 0.0
                for first in range(2):
                    near_re = part(near_ref, rows, 2 * first + row_out)
                    near_im = part(near_ref, rows, ncorr + 2 * first + row_out)
                    vis_re = image_re[2 * first + inner]
                    vis_im = image_im[2 * first + inner]
                    m_re = m_re + near_re * vis_re + near_im * vis_im
                    m_im = m_im + near_re * vis_im - near_im * vis_re
                mid_re.append(m_re)
                mid_im.append(m_im)
            for col_out in range(2):
                t_re = 0.0
                t_im = 0.0
                for inner in range(2):
                    far_re = part(far_ref, rows, 2 * inner + col_out)
                    far_im = part(far_ref, rows, ncorr + 2 * inner + col_out)
                    t_re = t_re + mid_re[inner] * far_re - mid_im[inner] * far_im
                    t_im = t_im + mid_re[inner] * far_im + mid_im[inner] * far_re
                place = 2 * (2 * row_out + col_out) * LANES
                block_ref[rows, place : place + LANES] = (t_re * taper).astype(jnp.bfloat16)
                block_ref[rows, place + LANES : place + 2 * LANES] = (t_im * taper).astype(jnp.bfloat16)
        return carry

    for p in range(pieces):
        lax.fori_loop(0, count // chunk, functools.partial(body, p), 0)
    send_rows(owners, per_owner, window, pl.program_id(0), facts, block_ref, out_ref)


def apply_aterms(images, groups, mine, other, taper, ncorr, owners, per_owner, window):
    count = images[0].shape[0]
    n = count * len(images)
    half = 2 * ncorr * LANES
    halves = mine.shape[1] // half
    rows = owners * window[1]
    return pl.pallas_call(
        functools.partial(aterm_kernel, ncorr, owners, per_owner, window, groups),
        grid=(halves,),
        in_specs=[pl.BlockSpec((count, LANES), lambda h: (0, halves * 2 * ncorr))] * len(images)
        + [pl.BlockSpec((count, half), lambda h: (0, h))] * len(images)
        + [
            pl.BlockSpec((1, 1, LANES), lambda h: (h, 0, 0)),
            pl.BlockSpec((mine.shape[0], half), lambda h: (0, h)),
            pl.BlockSpec((other.shape[0], half), lambda h: (0, h)),
        ],
        out_specs=[
            pl.BlockSpec((ncorr, rows, 2 * LANES), lambda h: (0, 0, h)),
            pl.BlockSpec((n, half), lambda h: (0, h)),
            pl.BlockSpec((n, LANES), lambda h: (0, 0)),
        ],
        out_shape=[
            jax.ShapeDtypeStruct((ncorr, rows, halves * 2 * LANES), jnp.bfloat16),
            jax.ShapeDtypeStruct((n, halves * half), jnp.bfloat16),
            jax.ShapeDtypeStruct((n, LANES), jnp.float32),
        ],
        scratch_shapes=[pltpu.VMEM((n, half), jnp.float32), pltpu.VMEM((n, half), jnp.float32)],
        compiler_params=pltpu.CompilerParams(vmem_limit_bytes=VMEM_LIMIT),
        cost_estimate=pl.CostEstimate(flops=6 << 30, bytes_accessed=8 << 20, transcendentals=0),
        name="aterms",
    )(*images, *images, taper, mine, other)


def rest_kernel(owners, per_owner, window, facts_ref, block_ref, out_ref):
    send_rows(owners, per_owner, window, pl.program_id(0), facts_ref[...], block_ref, out_ref)


def send_rest(facts, blocks, ncorr, owners, per_owner, window):
    n = blocks.shape[0]
    half = 2 * ncorr * LANES
    halves = blocks.shape[1] // half
    rows = owners * window[1]
    return pl.pallas_call(
        functools.partial(rest_kernel, owners, per_owner, window),
        grid=(halves,),
        in_specs=[
            pl.BlockSpec((n, LANES), lambda h: (0, 0)),
            pl.BlockSpec((n, half), lambda h: (0, h)),
        ],
        out_specs=pl.BlockSpec((ncorr, rows, 2 * LANES), lambda h: (0, 0, h)),
        out_shape=jax.ShapeDtypeStruct((ncorr, rows, halves * 2 * LANES), jnp.bfloat16),
        compiler_params=pltpu.CompilerParams(vmem_limit_bytes=VMEM_LIMIT),
        name="rest",
    )(facts, blocks)


def grid_kernel(rows, block_ref, col_ref, row_ref, before_ref, out_ref, most_ref, half_ref, uv_ref, turned_ref, re_a, im_a, re_b, im_b, label_ref, place_ref, sem):
    groups, total, depth = block_ref.shape
    sources = total // rows
    per_slot = 2 * PIX // LANES
    quarters = depth // LANES
    for t in range(sources):
        end = (t + 1) * rows
        label_ref[t : t + 1, :] = block_ref[0, end - 16 : end, :].astype(jnp.float32)[15:16].astype(jnp.int32)
    fetch = pltpu.make_async_copy(label_ref, place_ref, sem)
    fetch.start()

    for g in range(groups):
        half_ref[g] = jnp.dot(block_ref[g], col_ref[...], preferred_element_type=jnp.float32).astype(jnp.bfloat16)
    for q in range(quarters):
        left = jnp.concatenate([half_ref[g, :, q * LANES : (q + 1) * LANES] for g in range(groups)], axis=1)
        uv = jnp.dot(left, row_ref[...], preferred_element_type=jnp.float32)
        for part in range(2):
            for i in range(2):
                j = part * 2 + i
                uv_ref[pl.ds(part * 8 + 2 * q + i, total, stride=per_slot), :] = uv[:, j * LANES : (j + 1) * LANES]
    for t in range(sources):
        uv_ref[((t + 1) * rows - 1) * per_slot : (t + 1) * rows * per_slot, :] = jnp.zeros((per_slot, LANES), jnp.float32)
    for ref in (re_a, im_a, re_b, im_b):
        ref[...] = jnp.zeros_like(ref)
    fetch.wait()

    lane = lax.broadcasted_iota(jnp.int32, (8, LANES), 1)
    pieces = LANES // SUB
    tall = 2 * pieces * 8
    batch = 8
    most = jnp.int32(0)
    for t in range(sources):
        count = place_ref[t, 3 * LANES]
        most = jnp.maximum(most, place_ref[t, 3 * LANES + 1])

        def turn(i, carry):
            for b in range(batch):
                j = i * batch + b
                y = place_ref[t, LANES + j]
                inside = (lane >= y) & (lane < y + SUB)
                slot = t * rows + j
                for part in range(2):
                    block = uv_ref[pl.ds(pl.multiple_of(slot * per_slot + part * 8, 8), 8), :]
                    for g in range(pieces):
                        moved = pltpu.roll(block, (y + (LANES - g * SUB)) & (LANES - 1), 1)
                        at = pl.multiple_of(slot * tall + (part * pieces + g) * 8, 8)
                        turned_ref[pl.ds(at, 8), :] = jnp.where(inside, moved, 0.0)
            return carry

        lax.fori_loop(0, (count + (batch - 1)) // batch, turn, 0)

        def add(i, carry):
            for b in range(4):
                j = i * 4 + b
                row = place_ref[t, 2 * LANES + j] * TILE_SIDE + place_ref[t, j]
                slot = t * rows + j
                for part, ref in enumerate((re_a, im_a) if b % 2 == 0 else (re_b, im_b)):
                    at = pl.multiple_of(slot * tall + part * pieces * 8, 8)
                    ref[pl.ds(row, SUB), :] = ref[pl.ds(row, SUB), :] + turned_ref[pl.ds(at, SUB), :]
            return carry

        lax.fori_loop(0, (count + 3) // 4, add, 0)

    most_ref[0] = most
    for k in range(out_ref.shape[0]):
        span = slice(k * TILE_SIDE, (k + 1) * TILE_SIDE)
        for part, (one, two) in enumerate(((re_a, re_b), (im_a, im_b))):
            value = one[span, :] + two[span, :]
            if before_ref is not None:
                value = value + before_ref[k, part]
            out_ref[k, part] = value


def first_grid_kernel(rows, block_ref, col_ref, row_ref, *refs):
    grid_kernel(rows, block_ref, col_ref, row_ref, None, *refs)


def place_on_grid(blocks, rows, tables, per_owner, before=None):
    groups, total, depth = blocks.shape
    sources = total // rows
    shape = (per_owner, 2, TILE_SIDE, TILE_SIDE)
    whole = pl.BlockSpec(memory_space=pltpu.VMEM)
    accumulator = pltpu.VMEM((per_owner * TILE_SIDE, TILE_SIDE), jnp.float32)
    given = (blocks,) + tables + (() if before is None else (before,))
    return pl.pallas_call(
        functools.partial(first_grid_kernel if before is None else grid_kernel, rows),
        in_specs=[whole] * len(given),
        out_specs=[whole, pl.BlockSpec(memory_space=pltpu.SMEM)],
        out_shape=[jax.ShapeDtypeStruct(shape, jnp.float32), jax.ShapeDtypeStruct((1,), jnp.int32)],
        scratch_shapes=[
            pltpu.VMEM((groups, total, depth), jnp.bfloat16),
            pltpu.VMEM((total * 2 * PIX // LANES, LANES), jnp.float32),
            pltpu.VMEM((total * 2 * PIX // SUB, LANES), jnp.float32),
            accumulator,
            accumulator,
            accumulator,
            accumulator,
            pltpu.VMEM((sources, depth), jnp.int32),
            pltpu.SMEM((sources, depth), jnp.int32),
            pltpu.SemaphoreType.DMA(()),
        ],
        compiler_params=pltpu.CompilerParams(vmem_limit_bytes=VMEM_LIMIT),
        name="grid",
    )(*given)


def uv_tables(groups):
    quad = LANES // SUB
    halves = SUB // (groups * quad)
    index = np.arange(SUB) - SUB // 2
    factor = np.exp(-2j * np.pi / SUB * ((index[:, None] * index[None, :]) % SUB))

    def parts(table, axis):
        upper = np.stack([table.real, table.imag], axis=axis)
        lower = np.stack([-table.imag, table.real], axis=axis)
        return upper, lower

    col = (factor / SUB).reshape(SUB, 4, 4, 2).transpose(2, 0, 3, 1)
    first = np.zeros((halves, 2, quad, SUB, 4, halves, 2, quad, 2, 4))
    for p, table in enumerate(parts(col, 0)):
        for h in range(halves):
            for r in range(quad):
                first[h, p, r, :, :, h, :, r] = table.transpose(2, 1, 0, 3, 4)
    second = np.zeros((groups, halves, 2, quad, 2, 4, 2, 2, 4, SUB))
    row = factor.reshape(groups, halves, quad, SUB)
    for p, table in enumerate(parts(row, 0)):
        for i in range(2):
            for g in range(4):
                second[:, :, p, :, i, g, :, i, g, :] = table.transpose(1, 2, 3, 0, 4)
    size = halves * 2 * LANES
    first = first.reshape(size, 4 * halves * 2 * quad * 8)
    second = second.reshape(groups * halves * 2 * quad * 8, 4 * LANES)
    return first.astype(jnp.bfloat16), second.astype(jnp.bfloat16)


def taper_table(scale):
    pos = (np.arange(SUB) - SUB / 2 + 0.5) / (SUB / 2)
    one = 1.0 - 0.8 * pos * pos
    return (one[:, None] * one[None, :] * scale).astype(np.float32)


def per_device(visibilities, coords, stations, tile_ids, offsets, screens):
    count, fields, nvis = visibilities.shape
    ncorr = fields // 2
    groups = lax.axis_size("corr")
    owners = lax.axis_size("tile")
    corr = lax.axis_index("corr")
    tile = lax.axis_index("tile")
    per_owner = NT // owners
    full = per_owner * groups * (2 * count // NT)
    rows = -(-full * 3 // 64) * 16
    local = PIX // groups
    halves = local // LANES

    part = lax.dynamic_slice_in_dim(screens, corr * local, local, axis=2)
    part = part.reshape(-1, fields, halves, LANES).transpose(0, 2, 1, 3).reshape(-1, fields * local)
    sides = [[i for i in range(owners) if i % 2 == side] for side in range(2)]
    mine = lax.all_gather(part, "tile", axis=0, tiled=True, axis_index_groups=sides)

    images = []
    for half in range(2):
        made = make_images(visibilities, coords, stations, tile_ids, offsets, groups, half, 2)
        for d, piece in enumerate(made):
            images.append(lax.ppermute(piece, "corr", [(i, i ^ d) for i in range(groups)]) if d else piece)
    mine, *images = lax.optimization_barrier((mine, *images))
    other = lax.ppermute(mine, "tile", [(i, i ^ 1) for i in range(owners)])

    taper = jnp.asarray(taper_table(1.0 / nvis)).reshape(groups, halves, 1, LANES)
    taper = lax.dynamic_index_in_dim(taper, corr, axis=0, keepdims=False)
    tables = tuple(jnp.asarray(table) for table in uv_tables(groups))

    def exchange(sending, rows):
        received = lax.all_to_all(
            sending.reshape(groups * owners, rows, 2 * local), ("corr", "tile"), split_axis=0, concat_axis=0, tiled=True
        )
        return received.reshape(groups, owners * rows, 2 * local)

    sending, blocks, facts = apply_aterms(images, groups, mine, other, taper, ncorr, owners, per_owner, (0, rows))
    grid, most = place_on_grid(exchange(sending, rows), rows, tables, per_owner)
    slots = rows - 1
    if slots < full:
        more = -(-(full - slots + 1) // 16) * 16

        def overflow(grid):
            rest = send_rest(facts, blocks, ncorr, owners, per_owner, (slots, more))
            return place_on_grid(exchange(rest, more), more, tables, per_owner, grid)[0]

        grid = lax.cond(most[0] > slots, overflow, lambda grid: grid, grid)
    return grid[None]


def solution(mesh):
    return jax.shard_map(
        per_device,
        mesh=mesh,
        in_specs=(
            P(("corr", "tile"), None, None),
            P(("corr", "tile"), None, None),
            P(("corr", "tile"), None),
            P(("corr", "tile"), None),
            P(("corr", "tile"), None),
            P("tile", None, None),
        ),
        out_specs=P("corr", "tile", None, None, None),
        check_vma=False,
    )
```

```python
import functools
import math

import jax
import jax.numpy as jnp
import numpy as np
from jax import lax
from jax.experimental import pallas as pl
from jax.experimental.pallas import tpu as pltpu
from jax.sharding import PartitionSpec as P

SUB = 32
NT = 64
TILE_SIDE = 128
PIX = SUB * SUB
LANES = 128
VMEM_LIMIT = 36 * 1024 * 1024
VMEM_ALL = 63 * 1024 * 1024 + 512 * 1024

ROOT2 = math.sqrt(2.0)


def half_turn_series():
    grid = np.cos(np.pi * (np.arange(400) + 0.5) / 800.0) * 0.5
    z = grid * grid
    sine = np.polynomial.polynomial.Polynomial.fit(z, np.sin(np.pi * grid) / grid, 4, domain=[0, 0.25], window=[0, 0.25]).coef
    cosine = np.polynomial.polynomial.Polynomial.fit(z, np.cos(np.pi * grid), 4, domain=[0, 0.25], window=[0, 0.25]).coef
    return [float(x) * ROOT2 for x in sine], [float(x) * ROOT2 for x in cosine]


SINE, COSINE = half_turn_series()


def horner(coefficients, z):
    total = coefficients[-1]
    for value in coefficients[-2::-1]:
        total = total * z + value
    return total


def cis_turns(turns):
    t = turns - jnp.round(turns)
    z = t * t
    s = t * horner(SINE, z)
    c = horner(COSINE, z)
    return 1.0 - s * s, s * c


def image_kernel(ncorr, groups, begin, vis_ref, coord_ref, station_ref, tile_ref, offset_ref, *refs):
    out_refs, square = refs[:-1], refs[-1]
    me = lax.axis_index("corr")
    step = vis_ref.shape[0]
    nvis = vis_ref.shape[2]
    centred = (lax.broadcasted_iota(jnp.int32, (SUB, nvis), 0) - SUB // 2).astype(jnp.float32) * (1.0 / SUB)
    bend = 0.5 * centred * centred
    rows = ncorr * SUB

    def one(s):
        u = coord_ref[0, pl.ds(s, 1), :]
        v = coord_ref[1, pl.ds(s, 1), :]
        w = coord_ref[2, pl.ds(s, 1), :]
        sag = w * bend
        e_re, e_im = cis_turns(u * centred - sag)
        f_re, f_im = cis_turns(v * centred - sag)
        vis = vis_ref[s].astype(jnp.float32)
        g_re = []
        g_im = []
        for e in range(ncorr):
            vr = vis[e : e + 1]
            vi = vis[ncorr + e : ncorr + e + 1]
            g_re.append((vr * e_re - vi * e_im).astype(jnp.bfloat16))
            g_im.append((vr * e_im + vi * e_re).astype(jnp.bfloat16))
        left = jnp.concatenate([jnp.concatenate(g_re, axis=0), jnp.concatenate(g_im, axis=0)], axis=1)
        f_re = f_re.astype(jnp.bfloat16)
        f_im = f_im.astype(jnp.bfloat16)
        right = jnp.concatenate(
            [jnp.concatenate([f_re, f_im], axis=0), jnp.concatenate([-f_im, f_re], axis=0)], axis=1
        )
        image = lax.dot_general(left, right, (((1,), (1,)), ((), ())), preferred_element_type=jnp.float32)
        square[pl.ds(pl.multiple_of(s * rows, rows), rows), 0 : 2 * SUB] = image

    def several(i, carry):
        for j in range(4):
            one(i * 4 + j)
        return carry

    lax.fori_loop(0, step // 4, several, 0)

    lane = lax.broadcasted_iota(jnp.int32, (step, LANES), 1)
    per_tile = LANES // SUB
    halves = SUB // groups // per_tile
    for d in range(groups):
        first = (me ^ d) * (halves * per_tile)
        for h in range(halves):
            for e in range(ncorr):
                real = None
                imag = None
                for j in range(per_tile):
                    piece = square[pl.ds(first + (e * SUB + h * per_tile + j), step, stride=rows), :]
                    a = piece if j == 0 else pltpu.roll(piece, SUB * j, 1)
                    b = piece if j == 1 else pltpu.roll(piece, (SUB * (j - 1)) % LANES, 1)
                    keep = lane < SUB * (j + 1)
                    real = a if real is None else jnp.where(lane < SUB * j, real, a)
                    imag = b if imag is None else jnp.where(lane < SUB * j, imag, b)
                base = h * 2 * ncorr * LANES
                out_refs[d][:, base + e * LANES : base + (e + 1) * LANES] = real.astype(jnp.bfloat16)
                out_refs[d][:, base + (ncorr + e) * LANES : base + (ncorr + e + 1) * LANES] = imag.astype(jnp.bfloat16)
    near = station_ref[0:1]
    far = station_ref[1:2]
    facts = (tile_ref[...], offset_ref[0:1], offset_ref[1:2], near // 256, near % 256, far // 256, far % 256)
    count = near.shape[1]
    field = lax.broadcasted_iota(jnp.int32, (LANES, count), 0)
    table = jnp.zeros((LANES, count), jnp.int32)
    for i, fact in enumerate(facts):
        table = jnp.where(field == i, fact, table)
    mine = lax.broadcasted_iota(jnp.int32, (step, count), 0) + (pl.program_id(0) + begin) * step
    mine = (mine == lax.broadcasted_iota(jnp.int32, (step, count), 1)).astype(jnp.float32).astype(jnp.bfloat16)
    table = table.astype(jnp.float32).astype(jnp.bfloat16)
    table = lax.dot_general(mine, table, (((1,), (1,)), ((), ())), preferred_element_type=jnp.float32)
    for out_ref in out_refs:
        out_ref[:, 2 * ncorr * halves * LANES :] = table.astype(jnp.bfloat16)


def make_images(visibilities, coords, stations, tile_ids, offsets, groups, part, parts):
    count, fields, nvis = visibilities.shape
    ncorr = fields // 2
    step = 16
    width = fields * PIX // groups + LANES
    size = count // parts
    begin = part * size // step
    return pl.pallas_call(
        functools.partial(image_kernel, ncorr, groups, begin),
        grid=(size // step,),
        in_specs=[
            pl.BlockSpec((step, fields, nvis), lambda i: (i + begin, 0, 0)),
            pl.BlockSpec((3, step, nvis), lambda i: (0, i + begin, 0)),
            pl.BlockSpec((2, count), lambda i: (0, 0)),
            pl.BlockSpec((1, count), lambda i: (0, 0)),
            pl.BlockSpec((2, count), lambda i: (0, 0)),
        ],
        out_specs=[pl.BlockSpec((step, width), lambda i: (i, 0))] * groups,
        out_shape=[jax.ShapeDtypeStruct((size, width), jnp.bfloat16)] * groups,
        scratch_shapes=[pltpu.VMEM((step * ncorr * SUB, LANES), jnp.float32)],
        compiler_params=pltpu.CompilerParams(vmem_limit_bytes=VMEM_ALL),
        cost_estimate=pl.CostEstimate(flops=size << 27, bytes_accessed=2 << 20, transcendentals=0),
        name="images",
    )(visibilities, jnp.transpose(coords, (1, 0, 2)), stations.T, tile_ids.T, offsets.T)


def plan_rows(owners, per_owner, window, facts):
    first, rows = window
    n = facts.shape[0]
    slots = rows - 1
    turned = jnp.transpose(facts)
    owner = jnp.floor(turned[0:1] * (1.0 / per_owner))
    mine = lax.broadcasted_iota(jnp.int32, (owners, n), 0).astype(jnp.float32) == owner
    hot = mine.astype(jnp.float32)
    before = lax.broadcasted_iota(jnp.int32, (n, n), 0) < lax.broadcasted_iota(jnp.int32, (n, n), 1)
    ahead = jnp.dot(
        hot.astype(jnp.bfloat16), before.astype(jnp.float32).astype(jnp.bfloat16), preferred_element_type=jnp.float32
    )
    rank = jnp.sum(hot * ahead, axis=0, keepdims=True) - first
    fits = (rank >= 0.0) & (rank < float(slots))

    def chosen(pitch):
        place = jnp.where(fits, owner * pitch + rank, -1.0)
        row = lax.broadcasted_iota(jnp.int32, (owners * pitch, n), 0).astype(jnp.float32)
        return (row == place).astype(jnp.float32).astype(jnp.bfloat16)

    facts_here = jnp.concatenate(
        [turned[1:3], turned[0:1] - owner * per_owner, jnp.zeros((5, n), jnp.float32)], axis=0
    ).astype(jnp.bfloat16)
    found = lax.dot_general(facts_here, chosen(LANES), (((1,), (1,)), ((), ())), preferred_element_type=jnp.float32)
    held = jnp.sum(hot, axis=1, keepdims=True)
    most = jnp.max(held, axis=0, keepdims=True)
    here = jnp.minimum(jnp.maximum(held - first, 0.0), float(slots))
    lane = lax.broadcasted_iota(jnp.int32, (1, LANES), 1)
    labels = ([], [])
    for o in range(owners):
        span = slice(o * LANES, (o + 1) * LANES)
        counts = jnp.where(lane == 0, here[o : o + 1], jnp.where(lane == 1, most, 0.0))
        labels[0].append(jnp.concatenate([found[0:1, span], found[1:2, span]], axis=1))
        labels[1].append(jnp.concatenate([found[2:3, span], counts], axis=1))
    return chosen(rows), labels


def send_rows(owners, rows, move_ref, label_ref, block_ref, out_ref):
    last = lax.broadcasted_iota(jnp.int32, (16, 2 * LANES), 0) == 15
    for e in range(out_ref.shape[0]):
        block = block_ref[:, 2 * e * LANES : 2 * (e + 1) * LANES]
        moved = jnp.dot(move_ref[...], block, preferred_element_type=jnp.float32)
        out_ref[e] = moved.astype(jnp.bfloat16)
        for o in range(owners):
            end = (o + 1) * rows
            label = label_ref[0, o : o + 1, :]
            out_ref[e, end - 16 : end, :] = jnp.where(last, label, moved[end - 16 : end]).astype(jnp.bfloat16)


def plan_kernel(owners, per_owner, window, groups, *refs):
    facts_refs, (facts_ref, near_ref, far_ref, move_ref, label_ref) = refs[:-5], refs[-5:]
    pieces = len(facts_refs)
    count = facts_refs[0].shape[0]
    n, nst = near_ref.shape
    share = n // groups
    me = lax.axis_index("corr")
    for p in range(pieces):
        at = pl.multiple_of((me ^ (p % groups)) * share + p // groups * count, count)
        facts_ref[pl.ds(at, count), :] = facts_refs[p][...].astype(jnp.float32)
    facts = facts_ref[...]
    number = lax.broadcasted_iota(jnp.int32, (n, nst), 1).astype(jnp.float32)
    for column, ref in ((3, near_ref), (5, far_ref)):
        station = facts[:, column : column + 1] * 256.0 + facts[:, column + 1 : column + 2]
        ref[...] = (number == station).astype(jnp.float32).astype(jnp.bfloat16)
    move, labels = plan_rows(owners, per_owner, window, facts)
    move_ref[...] = move
    for h, rows in enumerate(labels):
        label_ref[h] = jnp.concatenate(rows, axis=0)


def make_plan(images, groups, nst, ncorr, owners, per_owner, window):
    count, width = images[0].shape
    n = count * len(images)
    halves = 2
    return pl.pallas_call(
        functools.partial(plan_kernel, owners, per_owner, window, groups),
        grid=(1,),
        in_specs=[pl.BlockSpec((count, LANES), lambda i: (0, width // LANES - 1))] * len(images),
        out_specs=[
            pl.BlockSpec((n, LANES), lambda i: (0, 0)),
            pl.BlockSpec((n, nst), lambda i: (0, 0)),
            pl.BlockSpec((n, nst), lambda i: (0, 0)),
            pl.BlockSpec((owners * window[1], n), lambda i: (0, 0)),
            pl.BlockSpec((halves, owners, 2 * LANES), lambda i: (0, 0, 0)),
        ],
        out_shape=[
            jax.ShapeDtypeStruct((n, LANES), jnp.float32),
            jax.ShapeDtypeStruct((n, nst), jnp.bfloat16),
            jax.ShapeDtypeStruct((n, nst), jnp.bfloat16),
            jax.ShapeDtypeStruct((owners * window[1], n), jnp.bfloat16),
            jax.ShapeDtypeStruct((halves, owners, 2 * LANES), jnp.float32),
        ],
        compiler_params=pltpu.CompilerParams(vmem_limit_bytes=VMEM_ALL),
        cost_estimate=pl.CostEstimate(flops=1 << 30, bytes_accessed=1 << 20, transcendentals=0),
        name="plan",
    )(*images)


def aterm_kernel(ncorr, owners, rows_of, groups, *refs):
    pieces = len(refs) - 10
    image_refs, refs = refs[:pieces], refs[pieces:]
    taper_ref, screen_ref, near_pick, far_pick, move_ref, label_ref, out_ref, block_ref, near_ref, far_ref = refs
    count = image_refs[0].shape[0]
    share_of = pieces * count // groups
    me = lax.axis_index("corr")
    for pick, ref in ((near_pick, near_ref), (far_pick, far_ref)):
        ref[...] = jnp.dot(pick[...], screen_ref[...], preferred_element_type=jnp.float32)
    taper = taper_ref[0]
    chunk = 16

    def part(ref, rows, field):
        return ref[rows, field * LANES : (field + 1) * LANES].astype(jnp.float32)

    def body(p, i, carry):
        held = pl.ds(pl.multiple_of(i * chunk, chunk), chunk)
        at = (me ^ (p % groups)) * share_of + p // groups * count + i * chunk
        rows = pl.ds(pl.multiple_of(at, chunk), chunk)
        image_re = [part(image_refs[p], held, e) for e in range(ncorr)]
        image_im = [part(image_refs[p], held, ncorr + e) for e in range(ncorr)]
        for row_out in range(2):
            mid_re = []
            mid_im = []
            for inner in range(2):
                m_re = 0.0
                m_im = 0.0
                for first in range(2):
                    near_re = part(near_ref, rows, 2 * first + row_out)
                    near_im = part(near_ref, rows, ncorr + 2 * first + row_out)
                    vis_re = image_re[2 * first + inner]
                    vis_im = image_im[2 * first + inner]
                    m_re = m_re + near_re * vis_re + near_im * vis_im
                    m_im = m_im + near_re * vis_im - near_im * vis_re
                mid_re.append(m_re)
                mid_im.append(m_im)
            for col_out in range(2):
                t_re = 0.0
                t_im = 0.0
                for inner in range(2):
                    far_re = part(far_ref, rows, 2 * inner + col_out)
                    far_im = part(far_ref, rows, ncorr + 2 * inner + col_out)
                    t_re = t_re + mid_re[inner] * far_re - mid_im[inner] * far_im
                    t_im = t_im + mid_re[inner] * far_im + mid_im[inner] * far_re
                place = 2 * (2 * row_out + col_out) * LANES
                block_ref[rows, place : place + LANES] = (t_re * taper).astype(jnp.bfloat16)
                block_ref[rows, place + LANES : place + 2 * LANES] = (t_im * taper).astype(jnp.bfloat16)
        return carry

    for p in range(pieces):
        lax.fori_loop(0, count // chunk, functools.partial(body, p), 0)
    send_rows(owners, rows_of, move_ref, label_ref, block_ref, out_ref)


def apply_aterms(images, groups, screens, plan, taper, ncorr, owners, rows):
    near, far, move, label = plan
    count = images[0].shape[0]
    n = count * len(images)
    nst = screens.shape[0]
    half = 2 * ncorr * LANES
    halves = screens.shape[1] // half
    fixed = lambda array: pl.BlockSpec(array.shape, lambda h: (0, 0))
    return pl.pallas_call(
        functools.partial(aterm_kernel, ncorr, owners, rows, groups),
        grid=(halves,),
        in_specs=[pl.BlockSpec((count, half), lambda h: (0, h))] * len(images)
        + [
            pl.BlockSpec((1, 1, LANES), lambda h: (h, 0, 0)),
            pl.BlockSpec((nst, half), lambda h: (0, h)),
            fixed(near),
            fixed(far),
            fixed(move),
            pl.BlockSpec((1, owners, 2 * LANES), lambda h: (h, 0, 0)),
        ],
        out_specs=[
            pl.BlockSpec((ncorr, owners * rows, 2 * LANES), lambda h: (0, 0, h)),
            pl.BlockSpec((n, half), lambda h: (0, h)),
        ],
        out_shape=[
            jax.ShapeDtypeStruct((ncorr, owners * rows, halves * 2 * LANES), jnp.bfloat16),
            jax.ShapeDtypeStruct((n, halves * half), jnp.bfloat16),
        ],
        scratch_shapes=[pltpu.VMEM((n, half), jnp.float32), pltpu.VMEM((n, half), jnp.float32)],
        compiler_params=pltpu.CompilerParams(vmem_limit_bytes=VMEM_ALL),
        cost_estimate=pl.CostEstimate(flops=6 << 30, bytes_accessed=8 << 20, transcendentals=0),
        name="aterms",
    )(*images, taper, screens, near, far, move, label)


def rest_kernel(owners, per_owner, window, facts_ref, block_ref, out_ref, move_ref, label_ref):
    move, labels = plan_rows(owners, per_owner, window, facts_ref[...])
    move_ref[...] = move
    for o in range(owners):
        label_ref[0, o : o + 1, :] = jnp.where(pl.program_id(0) == 0, labels[0][o], labels[1][o])
    send_rows(owners, window[1], move_ref, label_ref, block_ref, out_ref)


def send_rest(facts, blocks, ncorr, owners, per_owner, window):
    n = blocks.shape[0]
    half = 2 * ncorr * LANES
    halves = blocks.shape[1] // half
    rows = owners * window[1]
    return pl.pallas_call(
        functools.partial(rest_kernel, owners, per_owner, window),
        grid=(halves,),
        in_specs=[pl.BlockSpec((n, LANES), lambda h: (0, 0)), pl.BlockSpec((n, half), lambda h: (0, h))],
        out_specs=pl.BlockSpec((ncorr, rows, 2 * LANES), lambda h: (0, 0, h)),
        out_shape=jax.ShapeDtypeStruct((ncorr, rows, halves * 2 * LANES), jnp.bfloat16),
        scratch_shapes=[pltpu.VMEM((rows, n), jnp.bfloat16), pltpu.VMEM((1, owners, 2 * LANES), jnp.float32)],
        compiler_params=pltpu.CompilerParams(vmem_limit_bytes=VMEM_LIMIT),
        name="rest",
    )(facts, blocks)


def grid_kernel(rows, block_ref, col_ref, row_ref, before_ref, out_ref, most_ref, half_ref, uv_ref, turned_ref, re_a, im_a, re_b, im_b, label_ref, place_ref, sem):
    groups, total, depth = block_ref.shape
    sources = total // rows
    per_slot = 2 * PIX // LANES
    quarters = depth // LANES
    for t in range(sources):
        end = (t + 1) * rows
        label_ref[t : t + 1, :] = block_ref[0, end - 16 : end, :].astype(jnp.float32)[15:16].astype(jnp.int32)
    fetch = pltpu.make_async_copy(label_ref, place_ref, sem)
    fetch.start()

    for g in range(groups):
        half_ref[g] = jnp.dot(block_ref[g], col_ref[...], preferred_element_type=jnp.float32).astype(jnp.bfloat16)
    for q in range(quarters):
        left = jnp.concatenate([half_ref[g, :, q * LANES : (q + 1) * LANES] for g in range(groups)], axis=1)
        uv = jnp.dot(left, row_ref[...], preferred_element_type=jnp.float32)
        for part in range(2):
            for i in range(2):
                j = part * 2 + i
                uv_ref[pl.ds(part * 8 + 2 * q + i, total, stride=per_slot), :] = uv[:, j * LANES : (j + 1) * LANES]
    for t in range(sources):
        uv_ref[((t + 1) * rows - 1) * per_slot : (t + 1) * rows * per_slot, :] = jnp.zeros((per_slot, LANES), jnp.float32)
    for ref in (re_a, im_a, re_b, im_b):
        ref[...] = jnp.zeros_like(ref)
    fetch.wait()

    lane = lax.broadcasted_iota(jnp.int32, (8, LANES), 1)
    pieces = LANES // SUB
    tall = 2 * pieces * 8
    batch = 8
    most = jnp.int32(0)
    for t in range(sources):
        count = place_ref[t, 3 * LANES]
        most = jnp.maximum(most, place_ref[t, 3 * LANES + 1])

        def turn(i, carry):
            for b in range(batch):
                j = i * batch + b
                y = place_ref[t, LANES + j]
                inside = (lane >= y) & (lane < y + SUB)
                slot = t * rows + j
                for part in range(2):
                    block = uv_ref[pl.ds(pl.multiple_of(slot * per_slot + part * 8, 8), 8), :]
                    for g in range(pieces):
                        moved = pltpu.roll(block, (y + (LANES - g * SUB)) & (LANES - 1), 1)
                        at = pl.multiple_of(slot * tall + (part * pieces + g) * 8, 8)
                        turned_ref[pl.ds(at, 8), :] = jnp.where(inside, moved, 0.0)
            return carry

        lax.fori_loop(0, (count + (batch - 1)) // batch, turn, 0)

        def add(i, carry):
            for b in range(batch):
                j = i * batch + b
                row = place_ref[t, 2 * LANES + j] * TILE_SIDE + place_ref[t, j]
                slot = t * rows + j
                for part, ref in enumerate((re_a, im_a) if b % 2 == 0 else (re_b, im_b)):
                    at = pl.multiple_of(slot * tall + part * pieces * 8, 8)
                    ref[pl.ds(row, SUB), :] = ref[pl.ds(row, SUB), :] + turned_ref[pl.ds(at, SUB), :]
            return carry

        lax.fori_loop(0, (count + (batch - 1)) // batch, add, 0)

    most_ref[0] = most
    for k in range(out_ref.shape[0]):
        span = slice(k * TILE_SIDE, (k + 1) * TILE_SIDE)
        for part, (one, two) in enumerate(((re_a, re_b), (im_a, im_b))):
            value = one[span, :] + two[span, :]
            if before_ref is not None:
                value = value + before_ref[k, part]
            out_ref[k, part] = value


def first_grid_kernel(rows, block_ref, col_ref, row_ref, *refs):
    grid_kernel(rows, block_ref, col_ref, row_ref, None, *refs)


def place_on_grid(blocks, rows, tables, per_owner, before=None):
    groups, total, depth = blocks.shape
    sources = total // rows
    shape = (per_owner, 2, TILE_SIDE, TILE_SIDE)
    whole = pl.BlockSpec(memory_space=pltpu.VMEM)
    accumulator = pltpu.VMEM((per_owner * TILE_SIDE, TILE_SIDE), jnp.float32)
    given = (blocks,) + tables + (() if before is None else (before,))
    return pl.pallas_call(
        functools.partial(first_grid_kernel if before is None else grid_kernel, rows),
        in_specs=[whole] * len(given),
        out_specs=[whole, pl.BlockSpec(memory_space=pltpu.SMEM)],
        out_shape=[jax.ShapeDtypeStruct(shape, jnp.float32), jax.ShapeDtypeStruct((1,), jnp.int32)],
        scratch_shapes=[
            pltpu.VMEM((groups, total, depth), jnp.bfloat16),
            pltpu.VMEM((total * 2 * PIX // LANES, LANES), jnp.float32),
            pltpu.VMEM((total * 2 * PIX // SUB, LANES), jnp.float32),
            accumulator,
            accumulator,
            accumulator,
            accumulator,
            pltpu.VMEM((sources, depth), jnp.int32),
            pltpu.SMEM((sources, depth), jnp.int32),
            pltpu.SemaphoreType.DMA(()),
        ],
        compiler_params=pltpu.CompilerParams(vmem_limit_bytes=VMEM_LIMIT),
        name="grid",
    )(*given)


def uv_tables(groups):
    quad = LANES // SUB
    halves = SUB // (groups * quad)
    index = np.arange(SUB) - SUB // 2
    factor = np.exp(-2j * np.pi / SUB * ((index[:, None] * index[None, :]) % SUB))

    def parts(table, axis):
        upper = np.stack([table.real, table.imag], axis=axis)
        lower = np.stack([-table.imag, table.real], axis=axis)
        return upper, lower

    col = (factor / SUB).reshape(SUB, 4, 4, 2).transpose(2, 0, 3, 1)
    first = np.zeros((halves, 2, quad, SUB, 4, halves, 2, quad, 2, 4))
    for p, table in enumerate(parts(col, 0)):
        for h in range(halves):
            for r in range(quad):
                first[h, p, r, :, :, h, :, r] = table.transpose(2, 1, 0, 3, 4)
    second = np.zeros((groups, halves, 2, quad, 2, 4, 2, 2, 4, SUB))
    row = factor.reshape(groups, halves, quad, SUB)
    for p, table in enumerate(parts(row, 0)):
        for i in range(2):
            for g in range(4):
                second[:, :, p, :, i, g, :, i, g, :] = table.transpose(1, 2, 3, 0, 4)
    size = halves * 2 * LANES
    first = first.reshape(size, 4 * halves * 2 * quad * 8)
    second = second.reshape(groups * halves * 2 * quad * 8, 4 * LANES)
    return first.astype(jnp.bfloat16), second.astype(jnp.bfloat16)


def taper_table(scale):
    pos = (np.arange(SUB) - SUB / 2 + 0.5) / (SUB / 2)
    one = 1.0 - 0.8 * pos * pos
    return (one[:, None] * one[None, :] * scale).astype(np.float32)


def per_device(visibilities, coords, stations, tile_ids, offsets, screens):
    count, fields, nvis = visibilities.shape
    ncorr = fields // 2
    groups = lax.axis_size("corr")
    owners = lax.axis_size("tile")
    corr = lax.axis_index("corr")
    tile = lax.axis_index("tile")
    per_owner = NT // owners
    full = per_owner * groups * (2 * count // NT)
    rows = -(-full * 3 // 64) * 16
    local = PIX // groups
    halves = local // LANES

    part = lax.dynamic_slice_in_dim(screens, corr * local, local, axis=2)
    part = part.reshape(-1, fields, halves, LANES).transpose(0, 2, 1, 3).reshape(-1, fields * local)
    all_screens = lax.all_gather(part, "tile", axis=0, tiled=True)

    images = []
    for half in range(2):
        made = make_images(visibilities, coords, stations, tile_ids, offsets, groups, half, 2)
        for d, piece in enumerate(made):
            images.append(lax.ppermute(piece, "corr", [(i, i ^ d) for i in range(groups)]) if d else piece)
    taper = jnp.asarray(taper_table(1.0 / nvis)).reshape(groups, halves, 1, LANES)
    taper = lax.dynamic_index_in_dim(taper, corr, axis=0, keepdims=False)
    tables = tuple(jnp.asarray(table) for table in uv_tables(groups))

    def exchange(sending, rows):
        received = lax.all_to_all(
            sending.reshape(groups * owners, rows, 2 * local), ("corr", "tile"), split_axis=0, concat_axis=0, tiled=True
        )
        return received.reshape(groups, owners * rows, 2 * local)

    nst = all_screens.shape[0]
    facts, *plan = make_plan(images, groups, nst, ncorr, owners, per_owner, (0, rows))
    all_screens, *plan = lax.optimization_barrier((all_screens, *plan))
    sending, blocks = apply_aterms(images, groups, all_screens, plan, taper, ncorr, owners, rows)
    grid, most = place_on_grid(exchange(sending, rows), rows, tables, per_owner)
    slots = rows - 1
    if slots < full:
        more = -(-(full - slots + 1) // 16) * 16

        def overflow(grid):
            rest = send_rest(facts, blocks, ncorr, owners, per_owner, (slots, more))
            return place_on_grid(exchange(rest, more), more, tables, per_owner, grid)[0]

        grid = lax.cond(most[0] > slots, overflow, lambda grid: grid, grid)
    return grid[None]


def solution(mesh):
    return jax.shard_map(
        per_device,
        mesh=mesh,
        in_specs=(
            P(("corr", "tile"), None, None),
            P(("corr", "tile"), None, None),
            P(("corr", "tile"), None),
            P(("corr", "tile"), None),
            P(("corr", "tile"), None),
            P("tile", None, None),
        ),
        out_specs=P("corr", "tile", None, None, None),
        check_vma=False,
    )
```

```python
import functools
import math

import jax
import jax.numpy as jnp
import numpy as np
from jax import lax
from jax.experimental import pallas as pl
from jax.experimental.pallas import tpu as pltpu
from jax.sharding import PartitionSpec as P

SUB = 32
NT = 64
TILE_SIDE = 128
PIX = SUB * SUB
LANES = 128
VMEM_LIMIT = 36 * 1024 * 1024
VMEM_ALL = 63 * 1024 * 1024 + 512 * 1024

ROOT2 = math.sqrt(2.0)


def half_turn_series():
    grid = np.cos(np.pi * (np.arange(400) + 0.5) / 800.0) * 0.5
    z = grid * grid
    sine = np.polynomial.polynomial.Polynomial.fit(z, np.sin(np.pi * grid) / grid, 4, domain=[0, 0.25], window=[0, 0.25]).coef
    cosine = np.polynomial.polynomial.Polynomial.fit(z, np.cos(np.pi * grid), 4, domain=[0, 0.25], window=[0, 0.25]).coef
    return [float(x) * ROOT2 for x in sine], [float(x) * ROOT2 for x in cosine]


SINE, COSINE = half_turn_series()


def horner(coefficients, z):
    total = coefficients[-1]
    for value in coefficients[-2::-1]:
        total = total * z + value
    return total


def cis_turns(turns):
    t = turns - jnp.round(turns)
    z = t * t
    s = t * horner(SINE, z)
    c = horner(COSINE, z)
    return 1.0 - s * s, s * c


def image_kernel(ncorr, groups, vis_ref, coord_ref, *refs):
    out_refs, square = refs[:-1], refs[-1]
    me = lax.axis_index("corr")
    step = vis_ref.shape[0]
    nvis = vis_ref.shape[2]
    centred = (lax.broadcasted_iota(jnp.int32, (SUB, nvis), 0) - SUB // 2).astype(jnp.float32) * (1.0 / SUB)
    bend = 0.5 * centred * centred
    rows = ncorr * SUB

    def one(s):
        u = coord_ref[0, pl.ds(s, 1), :]
        v = coord_ref[1, pl.ds(s, 1), :]
        w = coord_ref[2, pl.ds(s, 1), :]
        sag = w * bend
        e_re, e_im = cis_turns(u * centred - sag)
        f_re, f_im = cis_turns(v * centred - sag)
        vis = vis_ref[s].astype(jnp.float32)
        g_re = []
        g_im = []
        for e in range(ncorr):
            vr = vis[e : e + 1]
            vi = vis[ncorr + e : ncorr + e + 1]
            g_re.append((vr * e_re - vi * e_im).astype(jnp.bfloat16))
            g_im.append((vr * e_im + vi * e_re).astype(jnp.bfloat16))
        left = jnp.concatenate([jnp.concatenate(g_re, axis=0), jnp.concatenate(g_im, axis=0)], axis=1)
        f_re = f_re.astype(jnp.bfloat16)
        f_im = f_im.astype(jnp.bfloat16)
        right = jnp.concatenate(
            [jnp.concatenate([f_re, f_im], axis=0), jnp.concatenate([-f_im, f_re], axis=0)], axis=1
        )
        image = lax.dot_general(left, right, (((1,), (1,)), ((), ())), preferred_element_type=jnp.float32)
        square[pl.ds(pl.multiple_of(s * rows, rows), rows), 0 : 2 * SUB] = image

    def several(i, carry):
        for j in range(4):
            one(i * 4 + j)
        return carry

    lax.fori_loop(0, step // 4, several, 0)

    lane = lax.broadcasted_iota(jnp.int32, (step, LANES), 1)
    per_tile = LANES // SUB
    halves = SUB // groups // per_tile
    for d in range(groups):
        first = (me ^ d) * (halves * per_tile)
        for h in range(halves):
            for e in range(ncorr):
                real = None
                imag = None
                for j in range(per_tile):
                    piece = square[pl.ds(first + (e * SUB + h * per_tile + j), step, stride=rows), :]
                    a = piece if j == 0 else pltpu.roll(piece, SUB * j, 1)
                    b = piece if j == 1 else pltpu.roll(piece, (SUB * (j - 1)) % LANES, 1)
                    keep = lane < SUB * (j + 1)
                    real = a if real is None else jnp.where(lane < SUB * j, real, a)
                    imag = b if imag is None else jnp.where(lane < SUB * j, imag, b)
                base = h * 2 * ncorr * LANES
                out_refs[d][:, base + e * LANES : base + (e + 1) * LANES] = real.astype(jnp.bfloat16)
                out_refs[d][:, base + (ncorr + e) * LANES : base + (ncorr + e + 1) * LANES] = imag.astype(jnp.bfloat16)


def make_images(visibilities, coords, groups):
    count, fields, nvis = visibilities.shape
    ncorr = fields // 2
    step = 16
    width = fields * PIX // groups
    return pl.pallas_call(
        functools.partial(image_kernel, ncorr, groups),
        grid=(count // step,),
        in_specs=[
            pl.BlockSpec((step, fields, nvis), lambda i: (i, 0, 0)),
            pl.BlockSpec((3, step, nvis), lambda i: (0, i, 0)),
        ],
        out_specs=[pl.BlockSpec((step, width), lambda i: (i, 0))] * groups,
        out_shape=[jax.ShapeDtypeStruct((count, width), jnp.bfloat16)] * groups,
        scratch_shapes=[pltpu.VMEM((step * ncorr * SUB, LANES), jnp.float32)],
        compiler_params=pltpu.CompilerParams(vmem_limit_bytes=VMEM_ALL),
        cost_estimate=pl.CostEstimate(flops=count << 27, bytes_accessed=2 << 20, transcendentals=0),
        name="images",
    )(visibilities, jnp.transpose(coords, (1, 0, 2)))


def plan_kernel(groups, owners, per_owner, count, every_ref, pick_ref, order_ref, place_ref, most_ref):
    nst = pick_ref.shape[1]
    n = groups * count
    together = LANES // count
    me = lax.axis_index("tile")
    lane = lax.broadcasted_iota(jnp.int32, (8, LANES), 1)
    number = lax.broadcasted_iota(jnp.int32, (count, nst), 1).astype(jnp.float32)
    before = lax.broadcasted_iota(jnp.int32, (n, n), 0) < lax.broadcasted_iota(jnp.int32, (n, n), 1)
    before = before.astype(jnp.float32).astype(jnp.bfloat16)
    owner_row = lax.broadcasted_iota(jnp.int32, (owners, n), 0).astype(jnp.float32)
    slot = lax.broadcasted_iota(jnp.int32, (LANES, n), 0).astype(jnp.float32)
    row = lax.broadcasted_iota(jnp.int32, (8, LANES), 0)

    def group(t):
        tiles = []
        for g in range(0, groups, together):
            joined = None
            for k in range(together):
                facts = every_ref[(g + k) * owners + t].astype(jnp.float32)
                facts = facts if k == 0 else pltpu.roll(facts, k * count, 1)
                joined = facts if k == 0 else jnp.where(lane < k * count, joined, facts)
            tiles.append(joined)
        return jnp.concatenate(tiles, axis=1)

    def ranks(facts):
        owner = jnp.floor(facts[0:1] * (1.0 / per_owner))
        hot = (owner_row == owner).astype(jnp.float32)
        ahead = jnp.dot(hot.astype(jnp.bfloat16), before, preferred_element_type=jnp.float32)
        return owner, jnp.sum(hot * ahead, axis=0, keepdims=True), jnp.sum(hot, axis=1, keepdims=True)

    for g in range(groups):
        columns = jnp.transpose(every_ref[g * owners + me].astype(jnp.float32))
        for which in range(2):
            at = which * n + g * count
            station = columns[:count, 3 + which : 4 + which]
            pick_ref[at : at + count, :] = (number == station).astype(jnp.float32).astype(jnp.bfloat16)
    owner, rank, held = ranks(group(me))
    order_ref[0:1, :] = owner
    order_ref[1:2, :] = rank

    most = jnp.zeros((owners, 1), jnp.float32)
    for t in range(owners):
        facts = group(t)
        owner, rank, held = ranks(facts)
        most = jnp.maximum(most, held)
        here = jnp.where(owner == me.astype(jnp.float32), 1.0, 0.0)
        hit = jnp.where(slot == jnp.where(here > 0.0, rank, -1.0), 1.0, 0.0).astype(jnp.bfloat16)
        local = facts[0:1] - owner * per_owner
        values = jnp.concatenate([facts[1:3], local, jnp.zeros((5, n), jnp.float32)], axis=0).astype(jnp.bfloat16)
        found = lax.dot_general(values, hit, (((1,), (1,)), ((), ())), preferred_element_type=jnp.float32)
        total = jnp.sum(here, axis=1, keepdims=True)
        place_ref[t] = jnp.where(row == 4, total, found).astype(jnp.int32)
    most_ref[...] = jnp.broadcast_to(jnp.max(most, axis=0, keepdims=True), most_ref.shape).astype(jnp.int32)


def make_plan(every, groups, owners, per_owner, count, nst):
    n = groups * count
    return pl.pallas_call(
        functools.partial(plan_kernel, groups, owners, per_owner, count),
        out_shape=[
            jax.ShapeDtypeStruct((2 * n, nst), jnp.bfloat16),
            jax.ShapeDtypeStruct((8, n), jnp.float32),
            jax.ShapeDtypeStruct((owners, 8, LANES), jnp.int32),
            jax.ShapeDtypeStruct((8, LANES), jnp.int32),
        ],
        compiler_params=pltpu.CompilerParams(vmem_limit_bytes=VMEM_LIMIT),
        cost_estimate=pl.CostEstimate(flops=1 << 30, bytes_accessed=1 << 20, transcendentals=0),
        name="plan",
    )(every)


def aterm_kernel(ncorr, owners, rows_of, *refs):
    groups = len(refs) - 7
    image_refs, refs = refs[:groups], refs[groups:]
    taper_ref, screen_ref, pick_ref, order_ref, out_ref, block_ref, jones_ref = refs
    count = image_refs[0].shape[0]
    n = groups * count
    me = lax.axis_index("corr")
    jones_ref[...] = jnp.dot(pick_ref[...], screen_ref[...], preferred_element_type=jnp.float32)
    taper = taper_ref[0]
    chunk = 16

    def part(ref, rows, field):
        return ref[rows, field * LANES : (field + 1) * LANES].astype(jnp.float32)

    def body(d, i, carry):
        held = pl.ds(pl.multiple_of(i * chunk, chunk), chunk)
        at = (me ^ d) * count + i * chunk
        rows = pl.ds(pl.multiple_of(at, chunk), chunk)
        far_rows = pl.ds(pl.multiple_of(at + n, chunk), chunk)
        image_re = [part(image_refs[d], held, e) for e in range(ncorr)]
        image_im = [part(image_refs[d], held, ncorr + e) for e in range(ncorr)]
        for row_out in range(2):
            mid_re = []
            mid_im = []
            for inner in range(2):
                m_re = 0.0
                m_im = 0.0
                for first in range(2):
                    near_re = part(jones_ref, rows, 2 * first + row_out)
                    near_im = part(jones_ref, rows, ncorr + 2 * first + row_out)
                    vis_re = image_re[2 * first + inner]
                    vis_im = image_im[2 * first + inner]
                    m_re = m_re + near_re * vis_re + near_im * vis_im
                    m_im = m_im + near_re * vis_im - near_im * vis_re
                mid_re.append(m_re)
                mid_im.append(m_im)
            for col_out in range(2):
                t_re = 0.0
                t_im = 0.0
                for inner in range(2):
                    far_re = part(jones_ref, far_rows, 2 * inner + col_out)
                    far_im = part(jones_ref, far_rows, ncorr + 2 * inner + col_out)
                    t_re = t_re + mid_re[inner] * far_re - mid_im[inner] * far_im
                    t_im = t_im + mid_re[inner] * far_im + mid_im[inner] * far_re
                place = 2 * (2 * row_out + col_out) * LANES
                block_ref[rows, place : place + LANES] = (t_re * taper).astype(jnp.bfloat16)
                block_ref[rows, place + LANES : place + 2 * LANES] = (t_im * taper).astype(jnp.bfloat16)
        return carry

    for d in range(groups):
        lax.fori_loop(0, count // chunk, functools.partial(body, d), 0)
    target = order_ref[0:1, :] * float(rows_of) + order_ref[1:2, :]
    row = lax.broadcasted_iota(jnp.int32, (owners * rows_of, n), 0).astype(jnp.float32)
    move = (row == target).astype(jnp.float32).astype(jnp.bfloat16)
    for e in range(ncorr):
        block = block_ref[:, 2 * e * LANES : 2 * (e + 1) * LANES]
        out_ref[e] = jnp.dot(move, block, preferred_element_type=jnp.float32).astype(jnp.bfloat16)


def apply_aterms(images, screens, pick, order, taper, ncorr, owners, rows):
    count = images[0].shape[0]
    n = count * len(images)
    nst = screens.shape[0]
    half = 2 * ncorr * LANES
    halves = screens.shape[1] // half
    return pl.pallas_call(
        functools.partial(aterm_kernel, ncorr, owners, rows),
        grid=(halves,),
        in_specs=[pl.BlockSpec((count, half), lambda h: (0, h))] * len(images)
        + [
            pl.BlockSpec((1, 1, LANES), lambda h: (h, 0, 0)),
            pl.BlockSpec((nst, half), lambda h: (0, h)),
            pl.BlockSpec(pick.shape, lambda h: (0, 0)),
            pl.BlockSpec(order.shape, lambda h: (0, 0)),
        ],
        out_specs=pl.BlockSpec((ncorr, owners * rows, 2 * LANES), lambda h: (0, 0, h)),
        out_shape=jax.ShapeDtypeStruct((ncorr, owners * rows, halves * 2 * LANES), jnp.bfloat16),
        scratch_shapes=[pltpu.VMEM((n, half), jnp.bfloat16), pltpu.VMEM((2 * n, half), jnp.float32)],
        compiler_params=pltpu.CompilerParams(vmem_limit_bytes=VMEM_ALL),
        cost_estimate=pl.CostEstimate(flops=6 << 30, bytes_accessed=8 << 20, transcendentals=0),
        name="aterms",
    )(*images, taper, screens, pick, order)


def grid_kernel(rows, place_ref, block_ref, col_ref, row_ref, out_ref, half_ref, uv_ref, turned_ref, re_a, im_a, re_b, im_b):
    groups, total, depth = block_ref.shape
    sources = total // rows
    per_slot = 2 * PIX // LANES
    quarters = depth // LANES
    for g in range(groups):
        half_ref[g] = jnp.dot(block_ref[g], col_ref[...], preferred_element_type=jnp.float32).astype(jnp.bfloat16)
    for q in range(quarters):
        left = jnp.concatenate([half_ref[g, :, q * LANES : (q + 1) * LANES] for g in range(groups)], axis=1)
        uv = jnp.dot(left, row_ref[...], preferred_element_type=jnp.float32)
        for part in range(2):
            for i in range(2):
                j = part * 2 + i
                uv_ref[pl.ds(part * 8 + 2 * q + i, total, stride=per_slot), :] = uv[:, j * LANES : (j + 1) * LANES]
    for ref in (re_a, im_a, re_b, im_b):
        ref[...] = jnp.zeros_like(ref)

    lane = lax.broadcasted_iota(jnp.int32, (8, LANES), 1)
    pieces = LANES // SUB
    tall = 2 * pieces * 8
    wide = 16
    batch = 8
    for t in range(sources):
        count = place_ref[t, 4, 0]

        def turn(i, carry):
            for b in range(wide):
                j = i * wide + b
                y = place_ref[t, 1, j]
                inside = (lane >= y) & (lane < y + SUB)
                slot = t * rows + j
                for part in range(2):
                    block = uv_ref[pl.ds(pl.multiple_of(slot * per_slot + part * 8, 8), 8), :]
                    for g in range(pieces):
                        moved = pltpu.roll(block, (y + (LANES - g * SUB)) & (LANES - 1), 1)
                        at = pl.multiple_of(slot * tall + (part * pieces + g) * 8, 8)
                        turned_ref[pl.ds(at, 8), :] = jnp.where(inside, moved, 0.0)
            return carry

        lax.fori_loop(0, (count + (wide - 1)) // wide, turn, 0)

        def add(i, carry):
            for b in range(batch):
                j = i * batch + b
                row = place_ref[t, 2, j] * TILE_SIDE + place_ref[t, 0, j]
                slot = t * rows + j
                for part, ref in enumerate((re_a, im_a) if b % 2 == 0 else (re_b, im_b)):
                    at = pl.multiple_of(slot * tall + part * pieces * 8, 8)
                    ref[pl.ds(row, SUB), :] = ref[pl.ds(row, SUB), :] + turned_ref[pl.ds(at, SUB), :]
            return carry

        lax.fori_loop(0, (count + (batch - 1)) // batch, add, 0)

    for k in range(out_ref.shape[0]):
        span = slice(k * TILE_SIDE, (k + 1) * TILE_SIDE)
        for part, (one, two) in enumerate(((re_a, re_b), (im_a, im_b))):
            out_ref[k, part] = one[span, :] + two[span, :]


def place_on_grid(places, blocks, rows, tables, per_owner):
    groups, total, depth = blocks.shape
    whole = pl.BlockSpec(memory_space=pltpu.VMEM)
    accumulator = pltpu.VMEM((per_owner * TILE_SIDE, TILE_SIDE), jnp.float32)
    spare = 16
    return pl.pallas_call(
        functools.partial(grid_kernel, rows),
        in_specs=[pl.BlockSpec(memory_space=pltpu.SMEM), whole, whole, whole],
        out_specs=whole,
        out_shape=jax.ShapeDtypeStruct((per_owner, 2, TILE_SIDE, TILE_SIDE), jnp.float32),
        scratch_shapes=[
            pltpu.VMEM((groups, total, depth), jnp.bfloat16),
            pltpu.VMEM(((total + spare) * 2 * PIX // LANES, LANES), jnp.float32),
            pltpu.VMEM(((total + spare) * 2 * PIX // SUB, LANES), jnp.float32),
            accumulator,
            accumulator,
            accumulator,
            accumulator,
        ],
        compiler_params=pltpu.CompilerParams(vmem_limit_bytes=VMEM_LIMIT),
        name="grid",
    )(places, blocks, *tables)


def uv_tables(groups):
    quad = LANES // SUB
    halves = SUB // (groups * quad)
    index = np.arange(SUB) - SUB // 2
    factor = np.exp(-2j * np.pi / SUB * ((index[:, None] * index[None, :]) % SUB))

    def parts(table, axis):
        upper = np.stack([table.real, table.imag], axis=axis)
        lower = np.stack([-table.imag, table.real], axis=axis)
        return upper, lower

    col = (factor / SUB).reshape(SUB, 4, 4, 2).transpose(2, 0, 3, 1)
    first = np.zeros((halves, 2, quad, SUB, 4, halves, 2, quad, 2, 4))
    for p, table in enumerate(parts(col, 0)):
        for h in range(halves):
            for r in range(quad):
                first[h, p, r, :, :, h, :, r] = table.transpose(2, 1, 0, 3, 4)
    second = np.zeros((groups, halves, 2, quad, 2, 4, 2, 2, 4, SUB))
    row = factor.reshape(groups, halves, quad, SUB)
    for p, table in enumerate(parts(row, 0)):
        for i in range(2):
            for g in range(4):
                second[:, :, p, :, i, g, :, i, g, :] = table.transpose(1, 2, 3, 0, 4)
    size = halves * 2 * LANES
    first = first.reshape(size, 4 * halves * 2 * quad * 8)
    second = second.reshape(groups * halves * 2 * quad * 8, 4 * LANES)
    return first.astype(jnp.bfloat16), second.astype(jnp.bfloat16)


def taper_table(scale):
    pos = (np.arange(SUB) - SUB / 2 + 0.5) / (SUB / 2)
    one = 1.0 - 0.8 * pos * pos
    return (one[:, None] * one[None, :] * scale).astype(np.float32)


def per_device(visibilities, coords, stations, tile_ids, offsets, screens):
    count, fields, nvis = visibilities.shape
    ncorr = fields // 2
    groups = lax.axis_size("corr")
    owners = lax.axis_size("tile")
    corr = lax.axis_index("corr")
    tile = lax.axis_index("tile")
    per_owner = NT // owners
    full = per_owner * groups * (2 * count // NT)
    halves = PIX // (groups * LANES)
    local = PIX // groups

    part = lax.dynamic_slice_in_dim(screens, corr * local, local, axis=2)
    part = part.reshape(-1, fields, halves, LANES).transpose(0, 2, 1, 3).reshape(-1, fields * local)
    all_screens = lax.all_gather(part, "tile", axis=0, tiled=True)

    facts = jnp.concatenate([tile_ids.T, offsets.T, stations.T], axis=0)
    facts = jnp.pad(facts, ((0, 8 - facts.shape[0]), (0, LANES - count)))
    every = jnp.broadcast_to(facts[None], (groups * owners, 8, LANES))
    every = lax.all_to_all(every, ("corr", "tile"), split_axis=0, concat_axis=0, tiled=True)

    images = make_images(visibilities, coords, groups)
    images = [
        lax.ppermute(piece, "corr", [(i, i ^ d) for i in range(groups)]) if d else piece for d, piece in enumerate(images)
    ]
    pick, order, places, most = make_plan(every, groups, owners, per_owner, count, all_screens.shape[0])

    taper = jnp.asarray(taper_table(1.0 / nvis)).reshape(groups, halves, 1, LANES)
    taper = lax.dynamic_index_in_dim(taper, corr, axis=0, keepdims=False)
    tables = tuple(jnp.asarray(table) for table in uv_tables(groups))

    def finish(rows, images, screens, pick, order, places):
        sending = apply_aterms(images, screens, pick, order, taper, ncorr, owners, rows)
        received = lax.all_to_all(
            sending.reshape(groups * owners, rows, 2 * local), ("corr", "tile"), split_axis=0, concat_axis=0, tiled=True
        )
        return place_on_grid(places, received.reshape(groups, owners * rows, 2 * local), rows, tables, per_owner)

    heights = sorted({min(full, -(-full * share // 64) * 8) for share in (5, 6, 8)})
    branches = [functools.partial(finish, rows) for rows in heights]
    if len(heights) == 1:
        grid = branches[0](images, all_screens, pick, order, places)
    else:
        index = sum((most[0, 0] > rows).astype(jnp.int32) for rows in heights[:-1])
        grid = lax.switch(index, branches, images, all_screens, pick, order, places)
    return grid[None]


def solution(mesh):
    return jax.shard_map(
        per_device,
        mesh=mesh,
        in_specs=(
            P(("corr", "tile"), None, None),
            P(("corr", "tile"), None, None),
            P(("corr", "tile"), None),
            P(("corr", "tile"), None),
            P(("corr", "tile"), None),
            P("tile", None, None),
        ),
        out_specs=P("corr", "tile", None, None, None),
        check_vma=False,
    )
```

```python
import functools
import math

import jax
import jax.numpy as jnp
import numpy as np
from jax import lax
from jax.experimental import pallas as pl
from jax.experimental.pallas import tpu as pltpu
from jax.sharding import PartitionSpec as P

SUB = 32
NT = 64
TILE_SIDE = 128
PIX = SUB * SUB
LANES = 128
VMEM_LIMIT = 36 * 1024 * 1024
VMEM_ALL = 63 * 1024 * 1024 + 512 * 1024

ROOT2 = math.sqrt(2.0)


def half_turn_series():
    grid = np.cos(np.pi * (np.arange(400) + 0.5) / 800.0) * 0.5
    z = grid * grid
    sine = np.polynomial.polynomial.Polynomial.fit(z, np.sin(np.pi * grid) / grid, 4, domain=[0, 0.25], window=[0, 0.25]).coef
    cosine = np.polynomial.polynomial.Polynomial.fit(z, np.cos(np.pi * grid), 4, domain=[0, 0.25], window=[0, 0.25]).coef
    return [float(x) * ROOT2 for x in sine], [float(x) * ROOT2 for x in cosine]


SINE, COSINE = half_turn_series()


def horner(coefficients, z):
    total = coefficients[-1]
    for value in coefficients[-2::-1]:
        total = total * z + value
    return total


def cis_turns(turns):
    t = turns - jnp.round(turns)
    z = t * t
    s = t * horner(SINE, z)
    c = horner(COSINE, z)
    return 1.0 - s * s, s * c


def image_kernel(ncorr, groups, vis_ref, coord_ref, *refs):
    out_refs, square = refs[:-1], refs[-1]
    me = lax.axis_index("corr")
    step = vis_ref.shape[0]
    nvis = vis_ref.shape[2]
    centred = (lax.broadcasted_iota(jnp.int32, (SUB, nvis), 0) - SUB // 2).astype(jnp.float32) * (1.0 / SUB)
    bend = 0.5 * centred * centred
    rows = ncorr * SUB

    def one(s):
        u = coord_ref[0, pl.ds(s, 1), :]
        v = coord_ref[1, pl.ds(s, 1), :]
        w = coord_ref[2, pl.ds(s, 1), :]
        sag = w * bend
        e_re, e_im = cis_turns(u * centred - sag)
        f_re, f_im = cis_turns(v * centred - sag)
        vis = vis_ref[s].astype(jnp.float32)
        g_re = []
        g_im = []
        for e in range(ncorr):
            vr = vis[e : e + 1]
            vi = vis[ncorr + e : ncorr + e + 1]
            g_re.append((vr * e_re - vi * e_im).astype(jnp.bfloat16))
            g_im.append((vr * e_im + vi * e_re).astype(jnp.bfloat16))
        left = jnp.concatenate([jnp.concatenate(g_re, axis=0), jnp.concatenate(g_im, axis=0)], axis=1)
        f_re = f_re.astype(jnp.bfloat16)
        f_im = f_im.astype(jnp.bfloat16)
        right = jnp.concatenate(
            [jnp.concatenate([f_re, f_im], axis=0), jnp.concatenate([-f_im, f_re], axis=0)], axis=1
        )
        image = lax.dot_general(left, right, (((1,), (1,)), ((), ())), preferred_element_type=jnp.float32)
        square[pl.ds(pl.multiple_of(s * rows, rows), rows), 0 : 2 * SUB] = image

    def several(i, carry):
        for j in range(4):
            one(i * 4 + j)
        return carry

    lax.fori_loop(0, step // 4, several, 0)

    lane = lax.broadcasted_iota(jnp.int32, (step, LANES), 1)
    per_tile = LANES // SUB
    halves = SUB // groups // per_tile
    for d in range(groups):
        first = (me ^ d) * (halves * per_tile)
        for h in range(halves):
            for e in range(ncorr):
                real = None
                imag = None
                for j in range(per_tile):
                    piece = square[pl.ds(first + (e * SUB + h * per_tile + j), step, stride=rows), :]
                    a = piece if j == 0 else pltpu.roll(piece, SUB * j, 1)
                    b = piece if j == 1 else pltpu.roll(piece, (SUB * (j - 1)) % LANES, 1)
                    keep = lane < SUB * (j + 1)
                    real = a if real is None else jnp.where(lane < SUB * j, real, a)
                    imag = b if imag is None else jnp.where(lane < SUB * j, imag, b)
                base = h * 2 * ncorr * LANES
                out_refs[d][:, base + e * LANES : base + (e + 1) * LANES] = real.astype(jnp.bfloat16)
                out_refs[d][:, base + (ncorr + e) * LANES : base + (ncorr + e + 1) * LANES] = imag.astype(jnp.bfloat16)


def make_images(visibilities, coords, groups):
    count, fields, nvis = visibilities.shape
    ncorr = fields // 2
    step = 16
    width = fields * PIX // groups
    return pl.pallas_call(
        functools.partial(image_kernel, ncorr, groups),
        grid=(count // step,),
        in_specs=[
            pl.BlockSpec((step, fields, nvis), lambda i: (i, 0, 0)),
            pl.BlockSpec((3, step, nvis), lambda i: (0, i, 0)),
        ],
        out_specs=[pl.BlockSpec((step, width), lambda i: (i, 0))] * groups,
        out_shape=[jax.ShapeDtypeStruct((count, width), jnp.bfloat16)] * groups,
        scratch_shapes=[pltpu.VMEM((step * ncorr * SUB, LANES), jnp.float32)],
        compiler_params=pltpu.CompilerParams(vmem_limit_bytes=VMEM_ALL),
        cost_estimate=pl.CostEstimate(flops=count << 27, bytes_accessed=2 << 20, transcendentals=0),
        name="images",
    )(visibilities, jnp.transpose(coords, (1, 0, 2)))


def plan_kernel(groups, owners, per_owner, count, every_ref, pick_ref, order_ref, place_ref, most_ref):
    nst = pick_ref.shape[1]
    n = groups * count
    together = LANES // count
    me = lax.axis_index("tile")
    lane = lax.broadcasted_iota(jnp.int32, (8, LANES), 1)
    number = lax.broadcasted_iota(jnp.int32, (count, nst), 1).astype(jnp.float32)
    before = lax.broadcasted_iota(jnp.int32, (n, n), 0) < lax.broadcasted_iota(jnp.int32, (n, n), 1)
    before = before.astype(jnp.float32).astype(jnp.bfloat16)
    owner_row = lax.broadcasted_iota(jnp.int32, (owners, n), 0).astype(jnp.float32)
    slot = lax.broadcasted_iota(jnp.int32, (LANES, n), 0).astype(jnp.float32)
    row = lax.broadcasted_iota(jnp.int32, (8, LANES), 0)

    def group(t):
        tiles = []
        for g in range(0, groups, together):
            joined = None
            for k in range(together):
                facts = every_ref[(g + k) * owners + t].astype(jnp.float32)
                facts = facts if k == 0 else pltpu.roll(facts, k * count, 1)
                joined = facts if k == 0 else jnp.where(lane < k * count, joined, facts)
            tiles.append(joined)
        return jnp.concatenate(tiles, axis=1)

    def ranks(facts):
        owner = jnp.floor(facts[0:1] * (1.0 / per_owner))
        hot = (owner_row == owner).astype(jnp.float32)
        ahead = jnp.dot(hot.astype(jnp.bfloat16), before, preferred_element_type=jnp.float32)
        return owner, jnp.sum(hot * ahead, axis=0, keepdims=True), jnp.sum(hot, axis=1, keepdims=True)

    for g in range(groups):
        columns = jnp.transpose(every_ref[g * owners + me].astype(jnp.float32))
        for which in range(2):
            at = which * n + g * count
            station = columns[:count, 3 + which : 4 + which]
            pick_ref[at : at + count, :] = (number == station).astype(jnp.float32).astype(jnp.bfloat16)
    owner, rank, held = ranks(group(me))
    order_ref[0:1, :] = owner
    order_ref[1:2, :] = rank

    most = jnp.zeros((owners, 1), jnp.float32)
    for t in range(owners):
        facts = group(t)
        owner, rank, held = ranks(facts)
        most = jnp.maximum(most, held)
        here = jnp.where(owner == me.astype(jnp.float32), 1.0, 0.0)
        hit = jnp.where(slot == jnp.where(here > 0.0, rank, -1.0), 1.0, 0.0).astype(jnp.bfloat16)
        local = facts[0:1] - owner * per_owner
        values = jnp.concatenate([facts[1:3], local, jnp.zeros((5, n), jnp.float32)], axis=0).astype(jnp.bfloat16)
        found = lax.dot_general(values, hit, (((1,), (1,)), ((), ())), preferred_element_type=jnp.float32)
        total = jnp.sum(here, axis=1, keepdims=True)
        place_ref[t] = jnp.where(row == 4, total, found).astype(jnp.int32)
    most_ref[...] = jnp.broadcast_to(jnp.max(most, axis=0, keepdims=True), most_ref.shape).astype(jnp.int32)


def make_plan(every, groups, owners, per_owner, count, nst):
    n = groups * count
    return pl.pallas_call(
        functools.partial(plan_kernel, groups, owners, per_owner, count),
        out_shape=[
            jax.ShapeDtypeStruct((2 * n, nst), jnp.bfloat16),
            jax.ShapeDtypeStruct((8, n), jnp.float32),
            jax.ShapeDtypeStruct((owners, 8, LANES), jnp.int32),
            jax.ShapeDtypeStruct((8, LANES), jnp.int32),
        ],
        compiler_params=pltpu.CompilerParams(vmem_limit_bytes=VMEM_LIMIT),
        cost_estimate=pl.CostEstimate(flops=1 << 30, bytes_accessed=1 << 20, transcendentals=0),
        name="plan",
    )(every)


def aterm_kernel(ncorr, owners, rows_of, *refs):
    groups = len(refs) - 7
    image_refs, refs = refs[:groups], refs[groups:]
    taper_ref, screen_ref, pick_ref, order_ref, out_ref, block_ref, jones_ref = refs
    count = image_refs[0].shape[0]
    n = groups * count
    me = lax.axis_index("corr")
    jones_ref[...] = jnp.dot(pick_ref[...], screen_ref[...], preferred_element_type=jnp.float32)
    taper = taper_ref[0]
    chunk = 16

    def part(ref, rows, field):
        return ref[rows, field * LANES : (field + 1) * LANES].astype(jnp.float32)

    def body(d, i, carry):
        held = pl.ds(pl.multiple_of(i * chunk, chunk), chunk)
        at = (me ^ d) * count + i * chunk
        rows = pl.ds(pl.multiple_of(at, chunk), chunk)
        far_rows = pl.ds(pl.multiple_of(at + n, chunk), chunk)
        image_re = [part(image_refs[d], held, e) for e in range(ncorr)]
        image_im = [part(image_refs[d], held, ncorr + e) for e in range(ncorr)]
        for row_out in range(2):
            mid_re = []
            mid_im = []
            for inner in range(2):
                m_re = 0.0
                m_im = 0.0
                for first in range(2):
                    near_re = part(jones_ref, rows, 2 * first + row_out)
                    near_im = part(jones_ref, rows, ncorr + 2 * first + row_out)
                    vis_re = image_re[2 * first + inner]
                    vis_im = image_im[2 * first + inner]
                    m_re = m_re + near_re * vis_re + near_im * vis_im
                    m_im = m_im + near_re * vis_im - near_im * vis_re
                mid_re.append(m_re)
                mid_im.append(m_im)
            for col_out in range(2):
                t_re = 0.0
                t_im = 0.0
                for inner in range(2):
                    far_re = part(jones_ref, far_rows, 2 * inner + col_out)
                    far_im = part(jones_ref, far_rows, ncorr + 2 * inner + col_out)
                    t_re = t_re + mid_re[inner] * far_re - mid_im[inner] * far_im
                    t_im = t_im + mid_re[inner] * far_im + mid_im[inner] * far_re
                place = 2 * (2 * row_out + col_out) * LANES
                block_ref[rows, place : place + LANES] = (t_re * taper).astype(jnp.bfloat16)
                block_ref[rows, place + LANES : place + 2 * LANES] = (t_im * taper).astype(jnp.bfloat16)
        return carry

    for d in range(groups):
        lax.fori_loop(0, count // chunk, functools.partial(body, d), 0)
    target = order_ref[0:1, :] * float(rows_of) + order_ref[1:2, :]
    row = lax.broadcasted_iota(jnp.int32, (owners * rows_of, n), 0).astype(jnp.float32)
    move = (row == target).astype(jnp.float32).astype(jnp.bfloat16)
    for e in range(ncorr):
        block = block_ref[:, 2 * e * LANES : 2 * (e + 1) * LANES]
        out_ref[e] = jnp.dot(move, block, preferred_element_type=jnp.float32).astype(jnp.bfloat16)


def apply_aterms(images, screens, pick, order, taper, ncorr, owners, rows):
    count = images[0].shape[0]
    n = count * len(images)
    nst = screens.shape[0]
    half = 2 * ncorr * LANES
    halves = screens.shape[1] // half
    return pl.pallas_call(
        functools.partial(aterm_kernel, ncorr, owners, rows),
        grid=(halves,),
        in_specs=[pl.BlockSpec((count, half), lambda h: (0, h))] * len(images)
        + [
            pl.BlockSpec((1, 1, LANES), lambda h: (h, 0, 0)),
            pl.BlockSpec((nst, half), lambda h: (0, h)),
            pl.BlockSpec(pick.shape, lambda h: (0, 0)),
            pl.BlockSpec(order.shape, lambda h: (0, 0)),
        ],
        out_specs=pl.BlockSpec((ncorr, owners * rows, 2 * LANES), lambda h: (0, 0, h)),
        out_shape=jax.ShapeDtypeStruct((ncorr, owners * rows, halves * 2 * LANES), jnp.bfloat16),
        scratch_shapes=[pltpu.VMEM((n, half), jnp.bfloat16), pltpu.VMEM((2 * n, half), jnp.float32)],
        compiler_params=pltpu.CompilerParams(vmem_limit_bytes=VMEM_ALL),
        cost_estimate=pl.CostEstimate(flops=6 << 30, bytes_accessed=8 << 20, transcendentals=0),
        name="aterms",
    )(*images, taper, screens, pick, order)


def grid_kernel(rows, place_ref, block_ref, col_ref, row_ref, out_ref, half_ref, uv_ref, turned_a, turned_b, re_a, im_a, re_b, im_b):
    groups, total, depth = block_ref.shape
    sources = total // rows
    per_slot = 2 * PIX // LANES
    quarters = depth // LANES
    for g in range(groups):
        half_ref[g] = jnp.dot(block_ref[g], col_ref[...], preferred_element_type=jnp.float32).astype(jnp.bfloat16)
    for q in range(quarters):
        left = jnp.concatenate([half_ref[g, :, q * LANES : (q + 1) * LANES] for g in range(groups)], axis=1)
        uv = jnp.dot(left, row_ref[...], preferred_element_type=jnp.float32)
        for part in range(2):
            for i in range(2):
                j = part * 2 + i
                uv_ref[pl.ds(part * 8 + 2 * q + i, total, stride=per_slot), :] = uv[:, j * LANES : (j + 1) * LANES]
    for ref in (re_a, im_a, re_b, im_b):
        ref[...] = jnp.zeros_like(ref)

    lane = lax.broadcasted_iota(jnp.int32, (8, LANES), 1)
    pieces = LANES // SUB
    tall = 2 * pieces * 8
    batch = 8
    longest = place_ref[0, 4, 0]
    for t in range(1, sources):
        longest = jnp.maximum(longest, place_ref[t, 4, 0])
    trips = (longest + (batch - 1)) // batch
    turned = (turned_a, turned_b)

    def turn(t, i):
        for b in range(batch):
            j = i * batch + b
            y = place_ref[t, 1, j]
            inside = (lane >= y) & (lane < y + SUB)
            for part in range(2):
                at = pl.multiple_of((t * rows + j) * per_slot + part * 8, 8)
                block = uv_ref[pl.ds(at, 8), :]
                for g in range(pieces):
                    moved = pltpu.roll(block, (y + (LANES - g * SUB)) & (LANES - 1), 1)
                    at = pl.multiple_of(j * tall + (part * pieces + g) * 8, 8)
                    turned[t % 2][pl.ds(at, 8), :] = jnp.where(inside, moved, 0.0)

    def add(t, i):
        for b in range(batch):
            j = i * batch + b
            row = place_ref[t, 2, j] * TILE_SIDE + place_ref[t, 0, j]
            for part, ref in enumerate((re_a, im_a) if b % 2 == 0 else (re_b, im_b)):
                at = pl.multiple_of(j * tall + part * pieces * 8, 8)
                ref[pl.ds(row, SUB), :] = ref[pl.ds(row, SUB), :] + turned[t % 2][pl.ds(at, SUB), :]

    for t in range(sources + 1):

        def both(i, carry):
            if t < sources:
                turn(t, i)
            if t > 0:
                add(t - 1, i)
            return carry

        lax.fori_loop(0, trips, both, 0)

    for k in range(out_ref.shape[0]):
        span = slice(k * TILE_SIDE, (k + 1) * TILE_SIDE)
        for part, (one, two) in enumerate(((re_a, re_b), (im_a, im_b))):
            out_ref[k, part] = one[span, :] + two[span, :]


def place_on_grid(places, blocks, rows, tables, per_owner):
    groups, total, depth = blocks.shape
    whole = pl.BlockSpec(memory_space=pltpu.VMEM)
    accumulator = pltpu.VMEM((per_owner * TILE_SIDE, TILE_SIDE), jnp.float32)
    return pl.pallas_call(
        functools.partial(grid_kernel, rows),
        in_specs=[pl.BlockSpec(memory_space=pltpu.SMEM), whole, whole, whole],
        out_specs=whole,
        out_shape=jax.ShapeDtypeStruct((per_owner, 2, TILE_SIDE, TILE_SIDE), jnp.float32),
        scratch_shapes=[
            pltpu.VMEM((groups, total, depth), jnp.bfloat16),
            pltpu.VMEM((total * 2 * PIX // LANES, LANES), jnp.float32),
            pltpu.VMEM((rows * 2 * PIX // SUB, LANES), jnp.float32),
            pltpu.VMEM((rows * 2 * PIX // SUB, LANES), jnp.float32),
            accumulator,
            accumulator,
            accumulator,
            accumulator,
        ],
        compiler_params=pltpu.CompilerParams(vmem_limit_bytes=VMEM_LIMIT),
        name="grid",
    )(places, blocks, *tables)


def uv_tables(groups):
    quad = LANES // SUB
    halves = SUB // (groups * quad)
    index = np.arange(SUB) - SUB // 2
    factor = np.exp(-2j * np.pi / SUB * ((index[:, None] * index[None, :]) % SUB))

    def parts(table, axis):
        upper = np.stack([table.real, table.imag], axis=axis)
        lower = np.stack([-table.imag, table.real], axis=axis)
        return upper, lower

    col = (factor / SUB).reshape(SUB, 4, 4, 2).transpose(2, 0, 3, 1)
    first = np.zeros((halves, 2, quad, SUB, 4, halves, 2, quad, 2, 4))
    for p, table in enumerate(parts(col, 0)):
        for h in range(halves):
            for r in range(quad):
                first[h, p, r, :, :, h, :, r] = table.transpose(2, 1, 0, 3, 4)
    second = np.zeros((groups, halves, 2, quad, 2, 4, 2, 2, 4, SUB))
    row = factor.reshape(groups, halves, quad, SUB)
    for p, table in enumerate(parts(row, 0)):
        for i in range(2):
            for g in range(4):
                second[:, :, p, :, i, g, :, i, g, :] = table.transpose(1, 2, 3, 0, 4)
    size = halves * 2 * LANES
    first = first.reshape(size, 4 * halves * 2 * quad * 8)
    second = second.reshape(groups * halves * 2 * quad * 8, 4 * LANES)
    return first.astype(jnp.bfloat16), second.astype(jnp.bfloat16)


def taper_table(scale):
    pos = (np.arange(SUB) - SUB / 2 + 0.5) / (SUB / 2)
    one = 1.0 - 0.8 * pos * pos
    return (one[:, None] * one[None, :] * scale).astype(np.float32)


def per_device(visibilities, coords, stations, tile_ids, offsets, screens):
    count, fields, nvis = visibilities.shape
    ncorr = fields // 2
    groups = lax.axis_size("corr")
    owners = lax.axis_size("tile")
    corr = lax.axis_index("corr")
    tile = lax.axis_index("tile")
    per_owner = NT // owners
    full = per_owner * groups * (2 * count // NT)
    halves = PIX // (groups * LANES)
    local = PIX // groups

    part = lax.dynamic_slice_in_dim(screens, corr * local, local, axis=2)
    part = part.reshape(-1, fields, halves, LANES).transpose(0, 2, 1, 3).reshape(-1, fields * local)
    all_screens = lax.all_gather(part, "tile", axis=0, tiled=True)

    images = list(make_images(visibilities, coords, groups))
    tile_ids, offsets, stations, images[0] = lax.optimization_barrier((tile_ids, offsets, stations, images[0]))
    facts = jnp.concatenate([tile_ids.T, offsets.T, stations.T], axis=0)
    facts = jnp.pad(facts, ((0, 8 - facts.shape[0]), (0, LANES - count)))
    every = jnp.broadcast_to(facts[None], (groups * owners, 8, LANES))
    every = lax.all_to_all(every, ("corr", "tile"), split_axis=0, concat_axis=0, tiled=True)

    images = [
        lax.ppermute(piece, "corr", [(i, i ^ d) for i in range(groups)]) if d else piece for d, piece in enumerate(images)
    ]
    pick, order, places, most = make_plan(every, groups, owners, per_owner, count, all_screens.shape[0])

    taper = jnp.asarray(taper_table(1.0 / nvis)).reshape(groups, halves, 1, LANES)
    taper = lax.dynamic_index_in_dim(taper, corr, axis=0, keepdims=False)
    tables = tuple(jnp.asarray(table) for table in uv_tables(groups))

    def finish(rows, images, screens, pick, order, places, taper):
        sending = apply_aterms(images, screens, pick, order, taper, ncorr, owners, rows)
        received = lax.all_to_all(
            sending.reshape(groups * owners, rows, 2 * local), ("corr", "tile"), split_axis=0, concat_axis=0, tiled=True
        )
        return place_on_grid(places, received.reshape(groups, owners * rows, 2 * local), rows, tables, per_owner)

    heights = sorted({min(full, -(-full * share // 64) * 8) for share in (5, 6, 8)})
    branches = [functools.partial(finish, rows) for rows in heights]
    if len(heights) == 1:
        grid = branches[0](images, all_screens, pick, order, places, taper)
    else:
        index = sum((most[0, 0] > rows).astype(jnp.int32) for rows in heights[:-1])
        grid = lax.switch(index, branches, images, all_screens, pick, order, places, taper)
    return grid[None]


def solution(mesh):
    return jax.shard_map(
        per_device,
        mesh=mesh,
        in_specs=(
            P(("corr", "tile"), None, None),
            P(("corr", "tile"), None, None),
            P(("corr", "tile"), None),
            P(("corr", "tile"), None),
            P(("corr", "tile"), None),
            P("tile", None, None),
        ),
        out_specs=P("corr", "tile", None, None, None),
        check_vma=False,
    )
```

```python
import functools
import math

import jax
import jax.numpy as jnp
import numpy as np
from jax import lax
from jax.experimental import pallas as pl
from jax.experimental.pallas import tpu as pltpu
from jax.sharding import PartitionSpec as P

SUB = 32
NT = 64
TILE_SIDE = 128
PIX = SUB * SUB
LANES = 128
VMEM_LIMIT = 36 * 1024 * 1024
VMEM_ALL = 63 * 1024 * 1024 + 512 * 1024

ROOT2 = math.sqrt(2.0)


def half_turn_series():
    grid = np.cos(np.pi * (np.arange(400) + 0.5) / 800.0) * 0.5
    z = grid * grid
    sine = np.polynomial.polynomial.Polynomial.fit(z, np.sin(np.pi * grid) / grid, 3, domain=[0, 0.25], window=[0, 0.25]).coef
    cosine = np.polynomial.polynomial.Polynomial.fit(z, np.cos(np.pi * grid), 4, domain=[0, 0.25], window=[0, 0.25]).coef
    return [float(x) * ROOT2 for x in sine], [float(x) * ROOT2 for x in cosine]


SINE, COSINE = half_turn_series()


def horner(coefficients, z):
    total = coefficients[-1]
    for value in coefficients[-2::-1]:
        total = total * z + value
    return total


def cis_turns(turns):
    t = turns - jnp.round(turns)
    z = t * t
    s = t * horner(SINE, z)
    c = horner(COSINE, z)
    return 1.0 - s * s, s * c


def image_kernel(ncorr, groups, vis_ref, coord_ref, *refs):
    out_refs, square = refs[:-1], refs[-1]
    me = lax.axis_index("corr")
    step = vis_ref.shape[0]
    nvis = vis_ref.shape[2]
    centred = (lax.broadcasted_iota(jnp.int32, (SUB, nvis), 0) - SUB // 2).astype(jnp.float32) * (1.0 / SUB)
    bend = 0.5 * centred * centred
    rows = ncorr * SUB
    pitch = rows + 1

    def one(s):
        u = coord_ref[0, pl.ds(s, 1), :]
        v = coord_ref[1, pl.ds(s, 1), :]
        w = coord_ref[2, pl.ds(s, 1), :]
        sag = w * bend
        e_re, e_im = cis_turns(u * centred - sag)
        f_re, f_im = cis_turns(v * centred - sag)
        vis = vis_ref[s].astype(jnp.float32)
        g_re = []
        g_im = []
        for e in range(ncorr):
            vr = vis[e : e + 1]
            vi = vis[ncorr + e : ncorr + e + 1]
            g_re.append((vr * e_re - vi * e_im).astype(jnp.bfloat16))
            g_im.append((vr * e_im + vi * e_re).astype(jnp.bfloat16))
        left = jnp.concatenate([jnp.concatenate(g_re, axis=0), jnp.concatenate(g_im, axis=0)], axis=1)
        f_re = f_re.astype(jnp.bfloat16)
        f_im = f_im.astype(jnp.bfloat16)
        right = jnp.concatenate(
            [jnp.concatenate([f_re, f_im], axis=0), jnp.concatenate([-f_im, f_re], axis=0)], axis=1
        )
        image = lax.dot_general(left, right, (((1,), (1,)), ((), ())), preferred_element_type=jnp.float32)
        square[pl.ds(s * pitch, rows), 0 : 2 * SUB] = image

    def several(i, carry):
        for j in range(4):
            one(i * 4 + j)
        return carry

    lax.fori_loop(0, step // 4, several, 0)

    lane = lax.broadcasted_iota(jnp.int32, (step, LANES), 1)
    per_tile = LANES // SUB
    halves = SUB // groups // per_tile
    for d in range(groups):
        first = (me ^ d) * (halves * per_tile)
        for h in range(halves):
            for e in range(ncorr):
                real = None
                imag = None
                for j in range(per_tile):
                    piece = square[pl.ds(first + (e * SUB + h * per_tile + j), step, stride=pitch), :]
                    a = piece if j == 0 else pltpu.roll(piece, SUB * j, 1)
                    b = piece if j == 1 else pltpu.roll(piece, (SUB * (j - 1)) % LANES, 1)
                    keep = lane < SUB * (j + 1)
                    real = a if real is None else jnp.where(lane < SUB * j, real, a)
                    imag = b if imag is None else jnp.where(lane < SUB * j, imag, b)
                base = h * 2 * ncorr * LANES
                out_refs[d][:, base + e * LANES : base + (e + 1) * LANES] = real.astype(jnp.bfloat16)
                out_refs[d][:, base + (ncorr + e) * LANES : base + (ncorr + e + 1) * LANES] = imag.astype(jnp.bfloat16)


def make_images(visibilities, coords, groups):
    count, fields, nvis = visibilities.shape
    ncorr = fields // 2
    step = 16
    width = fields * PIX // groups
    return pl.pallas_call(
        functools.partial(image_kernel, ncorr, groups),
        grid=(count // step,),
        in_specs=[
            pl.BlockSpec((step, fields, nvis), lambda i: (i, 0, 0)),
            pl.BlockSpec((3, step, nvis), lambda i: (0, i, 0)),
        ],
        out_specs=[pl.BlockSpec((step, width), lambda i: (i, 0))] * groups,
        out_shape=[jax.ShapeDtypeStruct((count, width), jnp.bfloat16)] * groups,
        scratch_shapes=[pltpu.VMEM((step * (ncorr * SUB + 1), LANES), jnp.float32)],
        compiler_params=pltpu.CompilerParams(vmem_limit_bytes=VMEM_ALL),
        cost_estimate=pl.CostEstimate(flops=count << 27, bytes_accessed=2 << 20, transcendentals=0),
        name="images",
    )(visibilities, jnp.transpose(coords, (1, 0, 2)))


def plan_kernel(groups, owners, per_owner, count, every_ref, pick_ref, order_ref, place_ref, most_ref):
    nst = pick_ref.shape[1]
    n = groups * count
    together = LANES // count
    me = lax.axis_index("tile")
    lane = lax.broadcasted_iota(jnp.int32, (8, LANES), 1)
    number = lax.broadcasted_iota(jnp.int32, (count, nst), 1).astype(jnp.float32)
    before = lax.broadcasted_iota(jnp.int32, (n, n), 0) < lax.broadcasted_iota(jnp.int32, (n, n), 1)
    before = before.astype(jnp.float32).astype(jnp.bfloat16)
    owner_row = lax.broadcasted_iota(jnp.int32, (owners, n), 0).astype(jnp.float32)
    slot = lax.broadcasted_iota(jnp.int32, (LANES, n), 0).astype(jnp.float32)
    row = lax.broadcasted_iota(jnp.int32, (8, LANES), 0)

    def group(t):
        tiles = []
        for g in range(0, groups, together):
            joined = None
            for k in range(together):
                facts = every_ref[(g + k) * owners + t].astype(jnp.float32)
                facts = facts if k == 0 else pltpu.roll(facts, k * count, 1)
                joined = facts if k == 0 else jnp.where(lane < k * count, joined, facts)
            tiles.append(joined)
        return jnp.concatenate(tiles, axis=1)

    def ranks(facts):
        owner = jnp.floor(facts[0:1] * (1.0 / per_owner))
        hot = (owner_row == owner).astype(jnp.float32)
        ahead = jnp.dot(hot.astype(jnp.bfloat16), before, preferred_element_type=jnp.float32)
        return owner, jnp.sum(hot * ahead, axis=0, keepdims=True), jnp.sum(hot, axis=1, keepdims=True)

    for g in range(groups):
        columns = jnp.transpose(every_ref[g * owners + me].astype(jnp.float32))
        for which in range(2):
            at = which * n + g * count
            station = columns[:count, 3 + which : 4 + which]
            pick_ref[at : at + count, :] = (number == station).astype(jnp.float32).astype(jnp.bfloat16)
    owner, rank, held = ranks(group(me))
    order_ref[0:1, :] = owner
    order_ref[1:2, :] = rank

    most = jnp.zeros((owners, 1), jnp.float32)
    for t in range(owners):
        facts = group(t)
        owner, rank, held = ranks(facts)
        most = jnp.maximum(most, held)
        here = jnp.where(owner == me.astype(jnp.float32), 1.0, 0.0)
        hit = jnp.where(slot == jnp.where(here > 0.0, rank, -1.0), 1.0, 0.0).astype(jnp.bfloat16)
        local = facts[0:1] - owner * per_owner
        values = jnp.concatenate([facts[1:3], local, jnp.zeros((5, n), jnp.float32)], axis=0).astype(jnp.bfloat16)
        found = lax.dot_general(values, hit, (((1,), (1,)), ((), ())), preferred_element_type=jnp.float32)
        total = jnp.sum(here, axis=1, keepdims=True)
        place_ref[t] = jnp.where(row == 4, total, found).astype(jnp.int32)
    most_ref[...] = jnp.broadcast_to(jnp.max(most, axis=0, keepdims=True), most_ref.shape).astype(jnp.int32)


def make_plan(every, groups, owners, per_owner, count, nst):
    n = groups * count
    return pl.pallas_call(
        functools.partial(plan_kernel, groups, owners, per_owner, count),
        out_shape=[
            jax.ShapeDtypeStruct((2 * n, nst), jnp.bfloat16),
            jax.ShapeDtypeStruct((8, n), jnp.float32),
            jax.ShapeDtypeStruct((owners, 8, LANES), jnp.int32),
            jax.ShapeDtypeStruct((8, LANES), jnp.int32),
        ],
        compiler_params=pltpu.CompilerParams(vmem_limit_bytes=VMEM_LIMIT),
        cost_estimate=pl.CostEstimate(flops=1 << 30, bytes_accessed=1 << 20, transcendentals=0),
        name="plan",
    )(every)


def aterm_kernel(ncorr, owners, rows_of, scale, *refs):
    groups = len(refs) - 6
    image_refs, refs = refs[:groups], refs[groups:]
    screen_ref, pick_ref, order_ref, out_ref, block_ref, jones_ref = refs
    count = image_refs[0].shape[0]
    n = groups * count
    me = lax.axis_index("corr")
    jones_ref[...] = jnp.dot(pick_ref[...], screen_ref[...], preferred_element_type=jnp.float32)
    pixel = lax.broadcasted_iota(jnp.int32, (1, LANES), 1) + (me * pl.num_programs(0) + pl.program_id(0)) * LANES
    row_at = ((pixel // SUB).astype(jnp.float32) - (SUB - 1) / 2.0) * (2.0 / SUB)
    col_at = ((pixel % SUB).astype(jnp.float32) - (SUB - 1) / 2.0) * (2.0 / SUB)
    taper = (1.0 - 0.8 * row_at * row_at) * (1.0 - 0.8 * col_at * col_at) * scale
    chunk = 16

    def part(ref, rows, field):
        return ref[rows, field * LANES : (field + 1) * LANES].astype(jnp.float32)

    def body(d, i, carry):
        held = pl.ds(pl.multiple_of(i * chunk, chunk), chunk)
        at = (me ^ d) * count + i * chunk
        rows = pl.ds(pl.multiple_of(at, chunk), chunk)
        far_rows = pl.ds(pl.multiple_of(at + n, chunk), chunk)
        image_re = [part(image_refs[d], held, e) for e in range(ncorr)]
        image_im = [part(image_refs[d], held, ncorr + e) for e in range(ncorr)]
        for row_out in range(2):
            mid_re = []
            mid_im = []
            for inner in range(2):
                m_re = 0.0
                m_im = 0.0
                for first in range(2):
                    near_re = part(jones_ref, rows, 2 * first + row_out)
                    near_im = part(jones_ref, rows, ncorr + 2 * first + row_out)
                    vis_re = image_re[2 * first + inner]
                    vis_im = image_im[2 * first + inner]
                    m_re = m_re + near_re * vis_re + near_im * vis_im
                    m_im = m_im + near_re * vis_im - near_im * vis_re
                mid_re.append(m_re)
                mid_im.append(m_im)
            for col_out in range(2):
                t_re = 0.0
                t_im = 0.0
                for inner in range(2):
                    far_re = part(jones_ref, far_rows, 2 * inner + col_out)
                    far_im = part(jones_ref, far_rows, ncorr + 2 * inner + col_out)
                    t_re = t_re + mid_re[inner] * far_re - mid_im[inner] * far_im
                    t_im = t_im + mid_re[inner] * far_im + mid_im[inner] * far_re
                place = 2 * (2 * row_out + col_out) * LANES
                block_ref[rows, place : place + LANES] = (t_re * taper).astype(jnp.bfloat16)
                block_ref[rows, place + LANES : place + 2 * LANES] = (t_im * taper).astype(jnp.bfloat16)
        return carry

    for d in range(groups):
        lax.fori_loop(0, count // chunk, functools.partial(body, d), 0)
    target = order_ref[0:1, :] * float(rows_of) + order_ref[1:2, :]
    row = lax.broadcasted_iota(jnp.int32, (owners * rows_of, n), 0).astype(jnp.float32)
    move = (row == target).astype(jnp.float32).astype(jnp.bfloat16)
    for e in range(ncorr):
        block = block_ref[:, 2 * e * LANES : 2 * (e + 1) * LANES]
        out_ref[e] = jnp.dot(move, block, preferred_element_type=jnp.float32).astype(jnp.bfloat16)


def apply_aterms(images, screens, pick, order, scale, ncorr, owners, rows):
    count = images[0].shape[0]
    n = count * len(images)
    nst = screens.shape[0]
    half = 2 * ncorr * LANES
    halves = screens.shape[1] // half
    return pl.pallas_call(
        functools.partial(aterm_kernel, ncorr, owners, rows, scale),
        grid=(halves,),
        in_specs=[pl.BlockSpec((count, half), lambda h: (0, h))] * len(images)
        + [
            pl.BlockSpec((nst, half), lambda h: (0, h)),
            pl.BlockSpec(pick.shape, lambda h: (0, 0)),
            pl.BlockSpec(order.shape, lambda h: (0, 0)),
        ],
        out_specs=pl.BlockSpec((ncorr, owners * rows, 2 * LANES), lambda h: (0, 0, h)),
        out_shape=jax.ShapeDtypeStruct((ncorr, owners * rows, halves * 2 * LANES), jnp.bfloat16),
        scratch_shapes=[pltpu.VMEM((n, half), jnp.bfloat16), pltpu.VMEM((2 * n, half), jnp.float32)],
        compiler_params=pltpu.CompilerParams(vmem_limit_bytes=VMEM_ALL),
        cost_estimate=pl.CostEstimate(flops=6 << 30, bytes_accessed=8 << 20, transcendentals=0),
        name="aterms",
    )(*images, screens, pick, order)


def grid_kernel(rows, place_ref, block_ref, col_ref, row_ref, out_ref, half_ref, uv_ref, turned_a, turned_b, re_a, im_a, re_b, im_b):
    groups, total, depth = block_ref.shape
    sources = total // rows
    per_slot = 2 * PIX // LANES + 1
    quarters = depth // LANES
    for g in range(groups):
        half_ref[g] = jnp.dot(block_ref[g], col_ref[...], preferred_element_type=jnp.float32).astype(jnp.bfloat16)
    for q in range(quarters):
        left = jnp.concatenate([half_ref[g, :, q * LANES : (q + 1) * LANES] for g in range(groups)], axis=1)
        uv = jnp.dot(left, row_ref[...], preferred_element_type=jnp.float32)
        for part in range(2):
            for i in range(2):
                j = part * 2 + i
                uv_ref[pl.ds(part * 8 + 2 * q + i, total, stride=per_slot), :] = uv[:, j * LANES : (j + 1) * LANES]
    for ref in (re_a, im_a, re_b, im_b):
        ref[...] = jnp.zeros_like(ref)

    lane = lax.broadcasted_iota(jnp.int32, (8, LANES), 1)
    pieces = LANES // SUB
    tall = 2 * pieces * 8
    batch = 8
    longest = place_ref[0, 4, 0]
    for t in range(1, sources):
        longest = jnp.maximum(longest, place_ref[t, 4, 0])
    trips = (longest + (batch - 1)) // batch
    turned = (turned_a, turned_b)

    def turn(t, i):
        for b in range(batch):
            j = i * batch + b
            y = place_ref[t, 1, j]
            inside = (lane >= y) & (lane < y + SUB)
            for part in range(2):
                at = (t * rows + j) * per_slot + part * 8
                block = uv_ref[pl.ds(at, 8), :]
                for g in range(pieces):
                    moved = pltpu.roll(block, (y + (LANES - g * SUB)) & (LANES - 1), 1)
                    at = pl.multiple_of(j * tall + (part * pieces + g) * 8, 8)
                    turned[t % 2][pl.ds(at, 8), :] = jnp.where(inside, moved, 0.0)

    def add(t, i):
        for b in range(batch):
            j = i * batch + b
            row = place_ref[t, 2, j] * TILE_SIDE + place_ref[t, 0, j]
            for part, ref in enumerate((re_a, im_a) if b % 2 == 0 else (re_b, im_b)):
                at = pl.multiple_of(j * tall + part * pieces * 8, 8)
                ref[pl.ds(row, SUB), :] = ref[pl.ds(row, SUB), :] + turned[t % 2][pl.ds(at, SUB), :]

    for t in range(sources + 1):

        def both(i, carry):
            if t < sources:
                turn(t, i)
            if t > 0:
                add(t - 1, i)
            return carry

        lax.fori_loop(0, trips, both, 0)

    for k in range(out_ref.shape[0]):
        span = slice(k * TILE_SIDE, (k + 1) * TILE_SIDE)
        for part, (one, two) in enumerate(((re_a, re_b), (im_a, im_b))):
            out_ref[k, part] = one[span, :] + two[span, :]


def place_on_grid(places, blocks, rows, tables, per_owner):
    groups, total, depth = blocks.shape
    whole = pl.BlockSpec(memory_space=pltpu.VMEM)
    accumulator = pltpu.VMEM((per_owner * TILE_SIDE, TILE_SIDE), jnp.float32)
    return pl.pallas_call(
        functools.partial(grid_kernel, rows),
        in_specs=[pl.BlockSpec(memory_space=pltpu.SMEM), whole, whole, whole],
        out_specs=whole,
        out_shape=jax.ShapeDtypeStruct((per_owner, 2, TILE_SIDE, TILE_SIDE), jnp.float32),
        scratch_shapes=[
            pltpu.VMEM((groups, total, depth), jnp.bfloat16),
            pltpu.VMEM((total * (2 * PIX // LANES + 1), LANES), jnp.float32),
            pltpu.VMEM((rows * 2 * PIX // SUB, LANES), jnp.float32),
            pltpu.VMEM((rows * 2 * PIX // SUB, LANES), jnp.float32),
            accumulator,
            accumulator,
            accumulator,
            accumulator,
        ],
        compiler_params=pltpu.CompilerParams(vmem_limit_bytes=VMEM_LIMIT),
        name="grid",
    )(places, blocks, *tables)


def uv_tables(groups):
    quad = LANES // SUB
    halves = SUB // (groups * quad)
    index = np.arange(SUB) - SUB // 2
    factor = np.exp(-2j * np.pi / SUB * ((index[:, None] * index[None, :]) % SUB))

    def parts(table, axis):
        upper = np.stack([table.real, table.imag], axis=axis)
        lower = np.stack([-table.imag, table.real], axis=axis)
        return upper, lower

    col = (factor / SUB).reshape(SUB, 4, 4, 2).transpose(2, 0, 3, 1)
    first = np.zeros((halves, 2, quad, SUB, 4, halves, 2, quad, 2, 4))
    for p, table in enumerate(parts(col, 0)):
        for h in range(halves):
            for r in range(quad):
                first[h, p, r, :, :, h, :, r] = table.transpose(2, 1, 0, 3, 4)
    second = np.zeros((groups, halves, 2, quad, 2, 4, 2, 2, 4, SUB))
    row = factor.reshape(groups, halves, quad, SUB)
    for p, table in enumerate(parts(row, 0)):
        for i in range(2):
            for g in range(4):
                second[:, :, p, :, i, g, :, i, g, :] = table.transpose(1, 2, 3, 0, 4)
    size = halves * 2 * LANES
    first = first.reshape(size, 4 * halves * 2 * quad * 8)
    second = second.reshape(groups * halves * 2 * quad * 8, 4 * LANES)
    return first.astype(jnp.bfloat16), second.astype(jnp.bfloat16)


def per_device(visibilities, coords, stations, tile_ids, offsets, screens):
    count, fields, nvis = visibilities.shape
    ncorr = fields // 2
    groups = lax.axis_size("corr")
    owners = lax.axis_size("tile")
    corr = lax.axis_index("corr")
    tile = lax.axis_index("tile")
    per_owner = NT // owners
    full = per_owner * groups * (2 * count // NT)
    halves = PIX // (groups * LANES)
    local = PIX // groups

    part = lax.dynamic_slice_in_dim(screens, corr * local, local, axis=2)
    part = part.reshape(-1, fields, halves, LANES).transpose(0, 2, 1, 3).reshape(-1, fields * local)
    all_screens = lax.all_gather(part, "tile", axis=0, tiled=True)

    facts = jnp.concatenate([tile_ids.T, offsets.T, stations.T], axis=0)
    facts = jnp.pad(facts, ((0, 8 - facts.shape[0]), (0, LANES - count)))
    every = jnp.broadcast_to(facts[None], (groups * owners, 8, LANES))
    every = lax.all_to_all(every, ("corr", "tile"), split_axis=0, concat_axis=0, tiled=True)

    images = make_images(visibilities, coords, groups)
    images = [
        lax.ppermute(piece, "corr", [(i, i ^ d) for i in range(groups)]) if d else piece for d, piece in enumerate(images)
    ]
    pick, order, places, most = make_plan(every, groups, owners, per_owner, count, all_screens.shape[0])

    tables = tuple(jnp.asarray(table) for table in uv_tables(groups))

    def finish(rows, images, screens, pick, order, places):
        sending = apply_aterms(images, screens, pick, order, 1.0 / nvis, ncorr, owners, rows)
        received = lax.all_to_all(
            sending.reshape(groups * owners, rows, 2 * local), ("corr", "tile"), split_axis=0, concat_axis=0, tiled=True
        )
        return place_on_grid(places, received.reshape(groups, owners * rows, 2 * local), rows, tables, per_owner)

    heights = sorted({min(full, -(-full * share // 64) * 8) for share in (5, 6, 8)})
    branches = [functools.partial(finish, rows) for rows in heights]
    if len(heights) == 1:
        grid = branches[0](images, all_screens, pick, order, places)
    else:
        index = sum((most[0, 0] > rows).astype(jnp.int32) for rows in heights[:-1])
        grid = lax.switch(index, branches, images, all_screens, pick, order, places)
    return grid[None]


def solution(mesh):
    return jax.shard_map(
        per_device,
        mesh=mesh,
        in_specs=(
            P(("corr", "tile"), None, None),
            P(("corr", "tile"), None, None),
            P(("corr", "tile"), None),
            P(("corr", "tile"), None),
            P(("corr", "tile"), None),
            P("tile", None, None),
        ),
        out_specs=P("corr", "tile", None, None, None),
        check_vma=False,
    )
```

```python
import functools
import math

import jax
import jax.numpy as jnp
import numpy as np
from jax import lax
from jax.experimental import pallas as pl
from jax.experimental.pallas import tpu as pltpu
from jax.sharding import PartitionSpec as P

SUB = 32
NT = 64
TILE_SIDE = 128
PIX = SUB * SUB
LANES = 128
VMEM_LIMIT = 36 * 1024 * 1024
VMEM_ALL = 63 * 1024 * 1024 + 512 * 1024

ROOT2 = math.sqrt(2.0)
NEAREST = 1.5 * 2.0**23


def half_turn_series():
    grid = np.cos(np.pi * (np.arange(400) + 0.5) / 800.0) * 0.5
    z = grid * grid
    sine = np.polynomial.polynomial.Polynomial.fit(z, np.sin(np.pi * grid) / grid, 3, domain=[0, 0.25], window=[0, 0.25]).coef
    cosine = np.polynomial.polynomial.Polynomial.fit(z, np.cos(np.pi * grid), 3, domain=[0, 0.25], window=[0, 0.25]).coef
    return [float(x) * ROOT2 for x in sine], [float(x) * ROOT2 for x in cosine]


SINE, COSINE = half_turn_series()


def horner(coefficients, z):
    total = coefficients[-1]
    for value in coefficients[-2::-1]:
        total = total * z + value
    return total


def cis_turns(turns):
    t = turns - ((turns + NEAREST) - NEAREST)
    z = t * t
    s = t * horner(SINE, z)
    c = horner(COSINE, z)
    return 1.0 - s * s, s * c


def image_kernel(ncorr, groups, vis_ref, coord_ref, *refs):
    out_refs, square = refs[:-1], refs[-1]
    me = lax.axis_index("corr")
    step = vis_ref.shape[0]
    nvis = vis_ref.shape[2]
    centred = (lax.broadcasted_iota(jnp.int32, (SUB, nvis), 0) - SUB // 2).astype(jnp.float32) * (1.0 / SUB)
    bend = 0.5 * centred * centred
    rows = ncorr * SUB
    pitch = rows + 1

    def one(s):
        u = coord_ref[0, pl.ds(s, 1), :]
        v = coord_ref[1, pl.ds(s, 1), :]
        w = coord_ref[2, pl.ds(s, 1), :]
        sag = w * bend
        e_re, e_im = cis_turns(u * centred - sag)
        f_re, f_im = cis_turns(v * centred - sag)
        vis = vis_ref[s].astype(jnp.float32)
        g_re = []
        g_im = []
        for e in range(ncorr):
            vr = vis[e : e + 1]
            vi = vis[ncorr + e : ncorr + e + 1]
            g_re.append((vr * e_re - vi * e_im).astype(jnp.bfloat16))
            g_im.append((vr * e_im + vi * e_re).astype(jnp.bfloat16))
        left = jnp.concatenate([jnp.concatenate(g_re, axis=0), jnp.concatenate(g_im, axis=0)], axis=1)
        f_re = f_re.astype(jnp.bfloat16)
        f_im = f_im.astype(jnp.bfloat16)
        right = jnp.concatenate(
            [jnp.concatenate([f_re, f_im], axis=0), jnp.concatenate([-f_im, f_re], axis=0)], axis=1
        )
        image = lax.dot_general(left, right, (((1,), (1,)), ((), ())), preferred_element_type=jnp.float32)
        square[pl.ds(s * pitch, rows), 0 : 2 * SUB] = image

    def several(i, carry):
        for j in range(4):
            one(i * 4 + j)
        return carry

    lax.fori_loop(0, step // 4, several, 0)

    lane = lax.broadcasted_iota(jnp.int32, (step, LANES), 1)
    low = lane < 2 * SUB
    even = (lane // SUB) % 2 == 0
    per_tile = LANES // SUB
    halves = SUB // groups // per_tile
    for d in range(groups):
        first = (me ^ d) * (halves * per_tile)
        for h in range(halves):
            for e in range(ncorr):
                p0, p1, p2, p3 = [
                    square[pl.ds(first + (e * SUB + h * per_tile + j), step, stride=pitch), :] for j in range(per_tile)
                ]
                evens = jnp.where(low, p0, pltpu.roll(p2, 2 * SUB, 1))
                odds = jnp.where(low, p1, pltpu.roll(p3, 2 * SUB, 1))
                real = jnp.where(even, evens, pltpu.roll(odds, SUB, 1))
                imag = jnp.where(even, pltpu.roll(evens, LANES - SUB, 1), odds)
                base = h * 2 * ncorr * LANES
                out_refs[d][:, base + e * LANES : base + (e + 1) * LANES] = real.astype(jnp.bfloat16)
                out_refs[d][:, base + (ncorr + e) * LANES : base + (ncorr + e + 1) * LANES] = imag.astype(jnp.bfloat16)


def make_images(visibilities, coords, groups):
    count, fields, nvis = visibilities.shape
    ncorr = fields // 2
    step = 16
    width = fields * PIX // groups
    return pl.pallas_call(
        functools.partial(image_kernel, ncorr, groups),
        grid=(count // step,),
        in_specs=[
            pl.BlockSpec((step, fields, nvis), lambda i: (i, 0, 0)),
            pl.BlockSpec((3, step, nvis), lambda i: (0, i, 0)),
        ],
        out_specs=[pl.BlockSpec((step, width), lambda i: (i, 0))] * groups,
        out_shape=[jax.ShapeDtypeStruct((count, width), jnp.bfloat16)] * groups,
        scratch_shapes=[pltpu.VMEM((step * (ncorr * SUB + 1), LANES), jnp.float32)],
        compiler_params=pltpu.CompilerParams(vmem_limit_bytes=VMEM_LIMIT),
        cost_estimate=pl.CostEstimate(flops=count << 27, bytes_accessed=2 << 20, transcendentals=0),
        name="images",
    )(visibilities, jnp.transpose(coords, (1, 0, 2)))


def plan_kernel(groups, owners, per_owner, count, every_ref, pick_ref, order_ref, place_ref, most_ref):
    nst = pick_ref.shape[1]
    n = groups * count
    together = LANES // count
    me = lax.axis_index("tile")
    lane = lax.broadcasted_iota(jnp.int32, (8, LANES), 1)
    number = lax.broadcasted_iota(jnp.int32, (count, nst), 1).astype(jnp.float32)
    before = lax.broadcasted_iota(jnp.int32, (n, n), 0) < lax.broadcasted_iota(jnp.int32, (n, n), 1)
    before = before.astype(jnp.float32).astype(jnp.bfloat16)
    owner_row = lax.broadcasted_iota(jnp.int32, (owners, n), 0).astype(jnp.float32)
    slot = lax.broadcasted_iota(jnp.int32, (LANES, n), 0).astype(jnp.float32)
    row = lax.broadcasted_iota(jnp.int32, (8, LANES), 0)

    def group(t):
        tiles = []
        for g in range(0, groups, together):
            joined = None
            for k in range(together):
                facts = every_ref[(g + k) * owners + t].astype(jnp.float32)
                facts = facts if k == 0 else pltpu.roll(facts, k * count, 1)
                joined = facts if k == 0 else jnp.where(lane < k * count, joined, facts)
            tiles.append(joined)
        return jnp.concatenate(tiles, axis=1)

    def ranks(facts):
        owner = jnp.floor(facts[0:1] * (1.0 / per_owner))
        hot = (owner_row == owner).astype(jnp.float32)
        ahead = jnp.dot(hot.astype(jnp.bfloat16), before, preferred_element_type=jnp.float32)
        return owner, jnp.sum(hot * ahead, axis=0, keepdims=True), jnp.sum(hot, axis=1, keepdims=True)

    for g in range(groups):
        columns = jnp.transpose(every_ref[g * owners + me].astype(jnp.float32))
        for which in range(2):
            at = which * n + g * count
            station = columns[:count, 3 + which : 4 + which]
            pick_ref[at : at + count, :] = (number == station).astype(jnp.float32).astype(jnp.bfloat16)
    owner, rank, held = ranks(group(me))
    order_ref[0:1, :] = owner
    order_ref[1:2, :] = rank

    most = jnp.zeros((owners, 1), jnp.float32)
    for t in range(owners):
        facts = group(t)
        owner, rank, held = ranks(facts)
        most = jnp.maximum(most, held)
        here = jnp.where(owner == me.astype(jnp.float32), 1.0, 0.0)
        hit = jnp.where(slot == jnp.where(here > 0.0, rank, -1.0), 1.0, 0.0).astype(jnp.bfloat16)
        local = facts[0:1] - owner * per_owner
        values = jnp.concatenate([facts[1:3], local, jnp.zeros((5, n), jnp.float32)], axis=0).astype(jnp.bfloat16)
        found = lax.dot_general(values, hit, (((1,), (1,)), ((), ())), preferred_element_type=jnp.float32)
        total = jnp.sum(here, axis=1, keepdims=True)
        place_ref[t] = jnp.where(row == 4, total, found).astype(jnp.int32)
    most_ref[...] = jnp.broadcast_to(jnp.max(most, axis=0, keepdims=True), most_ref.shape).astype(jnp.int32)


def make_plan(every, groups, owners, per_owner, count, nst):
    n = groups * count
    return pl.pallas_call(
        functools.partial(plan_kernel, groups, owners, per_owner, count),
        out_shape=[
            jax.ShapeDtypeStruct((2 * n, nst), jnp.bfloat16),
            jax.ShapeDtypeStruct((8, n), jnp.float32),
            jax.ShapeDtypeStruct((owners, 8, LANES), jnp.int32),
            jax.ShapeDtypeStruct((8, LANES), jnp.int32),
        ],
        compiler_params=pltpu.CompilerParams(vmem_limit_bytes=VMEM_LIMIT),
        cost_estimate=pl.CostEstimate(flops=1 << 30, bytes_accessed=1 << 20, transcendentals=0),
        name="plan",
    )(every)


def aterm_kernel(ncorr, owners, rows_of, scale, *refs):
    groups = len(refs) - 6
    image_refs, refs = refs[:groups], refs[groups:]
    screen_ref, pick_ref, order_ref, out_ref, block_ref, jones_ref = refs
    count = image_refs[0].shape[0]
    n = groups * count
    me = lax.axis_index("corr")
    jones_ref[...] = jnp.dot(pick_ref[...], screen_ref[...], preferred_element_type=jnp.float32)
    pixel = lax.broadcasted_iota(jnp.int32, (1, LANES), 1) + (me * pl.num_programs(0) + pl.program_id(0)) * LANES
    row_at = ((pixel // SUB).astype(jnp.float32) - (SUB - 1) / 2.0) * (2.0 / SUB)
    col_at = ((pixel % SUB).astype(jnp.float32) - (SUB - 1) / 2.0) * (2.0 / SUB)
    taper = (1.0 - 0.8 * row_at * row_at) * (1.0 - 0.8 * col_at * col_at) * scale
    chunk = 16

    def part(ref, rows, field):
        return ref[rows, field * LANES : (field + 1) * LANES].astype(jnp.float32)

    def body(d, i, carry):
        held = pl.ds(pl.multiple_of(i * chunk, chunk), chunk)
        at = (me ^ d) * count + i * chunk
        rows = pl.ds(pl.multiple_of(at, chunk), chunk)
        far_rows = pl.ds(pl.multiple_of(at + n, chunk), chunk)
        image_re = [part(image_refs[d], held, e) for e in range(ncorr)]
        image_im = [part(image_refs[d], held, ncorr + e) for e in range(ncorr)]
        for row_out in range(2):
            mid_re = []
            mid_im = []
            for inner in range(2):
                m_re = 0.0
                m_im = 0.0
                for first in range(2):
                    near_re = part(jones_ref, rows, 2 * first + row_out)
                    near_im = part(jones_ref, rows, ncorr + 2 * first + row_out)
                    vis_re = image_re[2 * first + inner]
                    vis_im = image_im[2 * first + inner]
                    m_re = m_re + near_re * vis_re + near_im * vis_im
                    m_im = m_im + near_re * vis_im - near_im * vis_re
                mid_re.append(m_re)
                mid_im.append(m_im)
            for col_out in range(2):
                t_re = 0.0
                t_im = 0.0
                for inner in range(2):
                    far_re = part(jones_ref, far_rows, 2 * inner + col_out)
                    far_im = part(jones_ref, far_rows, ncorr + 2 * inner + col_out)
                    t_re = t_re + mid_re[inner] * far_re - mid_im[inner] * far_im
                    t_im = t_im + mid_re[inner] * far_im + mid_im[inner] * far_re
                place = 2 * (2 * row_out + col_out) * LANES
                block_ref[rows, place : place + LANES] = (t_re * taper).astype(jnp.bfloat16)
                block_ref[rows, place + LANES : place + 2 * LANES] = (t_im * taper).astype(jnp.bfloat16)
        return carry

    for d in range(groups):
        lax.fori_loop(0, count // chunk, functools.partial(body, d), 0)
    target = order_ref[0:1, :] * float(rows_of) + order_ref[1:2, :]
    row = lax.broadcasted_iota(jnp.int32, (owners * rows_of, n), 0).astype(jnp.float32)
    move = (row == target).astype(jnp.float32).astype(jnp.bfloat16)
    for e in range(ncorr):
        block = block_ref[:, 2 * e * LANES : 2 * (e + 1) * LANES]
        out_ref[e] = jnp.dot(move, block, preferred_element_type=jnp.float32).astype(jnp.bfloat16)


def apply_aterms(images, screens, pick, order, scale, ncorr, owners, rows):
    count = images[0].shape[0]
    n = count * len(images)
    nst = screens.shape[0]
    half = 2 * ncorr * LANES
    halves = screens.shape[1] // half
    return pl.pallas_call(
        functools.partial(aterm_kernel, ncorr, owners, rows, scale),
        grid=(halves,),
        in_specs=[pl.BlockSpec((count, half), lambda h: (0, h))] * len(images)
        + [
            pl.BlockSpec((nst, half), lambda h: (0, h)),
            pl.BlockSpec(pick.shape, lambda h: (0, 0)),
            pl.BlockSpec(order.shape, lambda h: (0, 0)),
        ],
        out_specs=pl.BlockSpec((ncorr, owners * rows, 2 * LANES), lambda h: (0, 0, h)),
        out_shape=jax.ShapeDtypeStruct((ncorr, owners * rows, halves * 2 * LANES), jnp.bfloat16),
        scratch_shapes=[pltpu.VMEM((n, half), jnp.bfloat16), pltpu.VMEM((2 * n, half), jnp.float32)],
        compiler_params=pltpu.CompilerParams(vmem_limit_bytes=VMEM_ALL),
        cost_estimate=pl.CostEstimate(flops=6 << 30, bytes_accessed=8 << 20, transcendentals=0),
        name="aterms",
    )(*images, screens, pick, order)


def grid_kernel(rows, place_ref, block_ref, col_ref, row_ref, out_ref, half_ref, uv_ref, turned_a, turned_b, re_a, im_a, re_b, im_b):
    groups, total, depth = block_ref.shape
    sources = total // rows
    per_slot = 2 * PIX // LANES + 1
    quarters = depth // LANES
    for g in range(groups):
        half_ref[g] = jnp.dot(block_ref[g], col_ref[...], preferred_element_type=jnp.float32).astype(jnp.bfloat16)
    for q in range(quarters):
        left = jnp.concatenate([half_ref[g, :, q * LANES : (q + 1) * LANES] for g in range(groups)], axis=1)
        uv = jnp.dot(left, row_ref[...], preferred_element_type=jnp.float32)
        for part in range(2):
            for i in range(2):
                j = part * 2 + i
                uv_ref[pl.ds(part * 8 + 2 * q + i, total, stride=per_slot), :] = uv[:, j * LANES : (j + 1) * LANES]
    for ref in (re_a, im_a, re_b, im_b):
        ref[...] = jnp.zeros_like(ref)

    lane = lax.broadcasted_iota(jnp.int32, (8, LANES), 1)
    pieces = LANES // SUB
    tall = 2 * pieces * 8
    batch = 8
    longest = place_ref[0, 4, 0]
    for t in range(1, sources):
        longest = jnp.maximum(longest, place_ref[t, 4, 0])
    trips = (longest + (batch - 1)) // batch
    turned = (turned_a, turned_b)

    def turn(t, i):
        for b in range(batch):
            j = i * batch + b
            y = place_ref[t, 1, j]
            inside = (lane >= y) & (lane < y + SUB)
            for part in range(2):
                at = (t * rows + j) * per_slot + part * 8
                block = uv_ref[pl.ds(at, 8), :]
                for g in range(pieces):
                    moved = pltpu.roll(block, (y + (LANES - g * SUB)) & (LANES - 1), 1)
                    at = pl.multiple_of(j * tall + (part * pieces + g) * 8, 8)
                    turned[t % 2][pl.ds(at, 8), :] = jnp.where(inside, moved, 0.0)

    def add(t, i):
        for b in range(batch):
            j = i * batch + b
            row = place_ref[t, 2, j] * TILE_SIDE + place_ref[t, 0, j]
            for part, ref in enumerate((re_a, im_a) if b % 2 == 0 else (re_b, im_b)):
                at = pl.multiple_of(j * tall + part * pieces * 8, 8)
                ref[pl.ds(row, SUB), :] = ref[pl.ds(row, SUB), :] + turned[t % 2][pl.ds(at, SUB), :]

    for t in range(sources + 1):

        def both(i, carry):
            if t < sources:
                turn(t, i)
            if t > 0:
                add(t - 1, i)
            return carry

        lax.fori_loop(0, trips, both, 0)

    for k in range(out_ref.shape[0]):
        span = slice(k * TILE_SIDE, (k + 1) * TILE_SIDE)
        for part, (one, two) in enumerate(((re_a, re_b), (im_a, im_b))):
            out_ref[k, part] = one[span, :] + two[span, :]


def place_on_grid(places, blocks, rows, tables, per_owner):
    groups, total, depth = blocks.shape
    whole = pl.BlockSpec(memory_space=pltpu.VMEM)
    accumulator = pltpu.VMEM((per_owner * TILE_SIDE, TILE_SIDE), jnp.float32)
    return pl.pallas_call(
        functools.partial(grid_kernel, rows),
        in_specs=[pl.BlockSpec(memory_space=pltpu.SMEM), whole, whole, whole],
        out_specs=whole,
        out_shape=jax.ShapeDtypeStruct((per_owner, 2, TILE_SIDE, TILE_SIDE), jnp.float32),
        scratch_shapes=[
            pltpu.VMEM((groups, total, depth), jnp.bfloat16),
            pltpu.VMEM((total * (2 * PIX // LANES + 1), LANES), jnp.float32),
            pltpu.VMEM((rows * 2 * PIX // SUB, LANES), jnp.float32),
            pltpu.VMEM((rows * 2 * PIX // SUB, LANES), jnp.float32),
            accumulator,
            accumulator,
            accumulator,
            accumulator,
        ],
        compiler_params=pltpu.CompilerParams(vmem_limit_bytes=VMEM_LIMIT),
        name="grid",
    )(places, blocks, *tables)


def uv_tables(groups):
    quad = LANES // SUB
    halves = SUB // (groups * quad)
    index = np.arange(SUB) - SUB // 2
    factor = np.exp(-2j * np.pi / SUB * ((index[:, None] * index[None, :]) % SUB))

    def parts(table, axis):
        upper = np.stack([table.real, table.imag], axis=axis)
        lower = np.stack([-table.imag, table.real], axis=axis)
        return upper, lower

    col = (factor / SUB).reshape(SUB, 4, 4, 2).transpose(2, 0, 3, 1)
    first = np.zeros((halves, 2, quad, SUB, 4, halves, 2, quad, 2, 4))
    for p, table in enumerate(parts(col, 0)):
        for h in range(halves):
            for r in range(quad):
                first[h, p, r, :, :, h, :, r] = table.transpose(2, 1, 0, 3, 4)
    second = np.zeros((groups, halves, 2, quad, 2, 4, 2, 2, 4, SUB))
    row = factor.reshape(groups, halves, quad, SUB)
    for p, table in enumerate(parts(row, 0)):
        for i in range(2):
            for g in range(4):
                second[:, :, p, :, i, g, :, i, g, :] = table.transpose(1, 2, 3, 0, 4)
    size = halves * 2 * LANES
    first = first.reshape(size, 4 * halves * 2 * quad * 8)
    second = second.reshape(groups * halves * 2 * quad * 8, 4 * LANES)
    return first.astype(jnp.bfloat16), second.astype(jnp.bfloat16)


def per_device(visibilities, coords, stations, tile_ids, offsets, screens):
    count, fields, nvis = visibilities.shape
    ncorr = fields // 2
    groups = lax.axis_size("corr")
    owners = lax.axis_size("tile")
    corr = lax.axis_index("corr")
    tile = lax.axis_index("tile")
    per_owner = NT // owners
    full = per_owner * groups * (2 * count // NT)
    halves = PIX // (groups * LANES)
    local = PIX // groups

    part = lax.dynamic_slice_in_dim(screens, corr * local, local, axis=2)
    part = part.reshape(-1, fields, halves, LANES).transpose(0, 2, 1, 3).reshape(-1, fields * local)
    all_screens = lax.all_gather(part, "tile", axis=0, tiled=True)

    facts = jnp.concatenate([tile_ids.T, offsets.T, stations.T], axis=0)
    facts = jnp.pad(facts, ((0, 8 - facts.shape[0]), (0, LANES - count)))
    every = jnp.broadcast_to(facts[None], (groups * owners, 8, LANES))
    every = lax.all_to_all(every, ("corr", "tile"), split_axis=0, concat_axis=0, tiled=True)

    images = make_images(visibilities, coords, groups)
    images = [
        lax.ppermute(piece, "corr", [(i, i ^ d) for i in range(groups)]) if d else piece for d, piece in enumerate(images)
    ]
    pick, order, places, most = make_plan(every, groups, owners, per_owner, count, all_screens.shape[0])

    tables = tuple(jnp.asarray(table) for table in uv_tables(groups))

    def finish(rows, images, screens, pick, order, places):
        sending = apply_aterms(images, screens, pick, order, 1.0 / nvis, ncorr, owners, rows)
        received = lax.all_to_all(
            sending.reshape(groups * owners, rows, 2 * local), ("corr", "tile"), split_axis=0, concat_axis=0, tiled=True
        )
        return place_on_grid(places, received.reshape(groups, owners * rows, 2 * local), rows, tables, per_owner)

    heights = sorted({min(full, -(-full * share // 64) * 8) for share in (5, 6, 8)})
    branches = [functools.partial(finish, rows) for rows in heights]
    if len(heights) == 1:
        grid = branches[0](images, all_screens, pick, order, places)
    else:
        index = sum((most[0, 0] > rows).astype(jnp.int32) for rows in heights[:-1])
        grid = lax.switch(index, branches, images, all_screens, pick, order, places)
    return grid[None]


def solution(mesh):
    return jax.shard_map(
        per_device,
        mesh=mesh,
        in_specs=(
            P(("corr", "tile"), None, None),
            P(("corr", "tile"), None, None),
            P(("corr", "tile"), None),
            P(("corr", "tile"), None),
            P(("corr", "tile"), None),
            P("tile", None, None),
        ),
        out_specs=P("corr", "tile", None, None, None),
        check_vma=False,
    )
```

```python
import functools
import math

import jax
import jax.numpy as jnp
import numpy as np
from jax import lax
from jax.experimental import pallas as pl
from jax.experimental.pallas import tpu as pltpu
from jax.sharding import PartitionSpec as P

SUB = 32
NT = 64
TILE_SIDE = 128
PIX = SUB * SUB
LANES = 128
VMEM_LIMIT = 36 * 1024 * 1024
VMEM_ALL = 63 * 1024 * 1024 + 512 * 1024

ROOT2 = math.sqrt(2.0)
NEAREST = 1.5 * 2.0**23


def half_turn_series():
    grid = np.cos(np.pi * (np.arange(400) + 0.5) / 800.0) * 0.5
    z = grid * grid
    sine = np.polynomial.polynomial.Polynomial.fit(z, np.sin(np.pi * grid) / grid, 3, domain=[0, 0.25], window=[0, 0.25]).coef
    cosine = np.polynomial.polynomial.Polynomial.fit(z, np.cos(np.pi * grid), 3, domain=[0, 0.25], window=[0, 0.25]).coef
    return [float(x) * ROOT2 for x in sine], [float(x) * ROOT2 for x in cosine]


SINE, COSINE = half_turn_series()


def horner(coefficients, z):
    total = coefficients[-1]
    for value in coefficients[-2::-1]:
        total = total * z + value
    return total


def cis_turns(turns):
    t = turns - ((turns + NEAREST) - NEAREST)
    z = t * t
    s = t * horner(SINE, z)
    c = horner(COSINE, z)
    return 1.0 - s * s, s * c


def image_kernel(ncorr, groups, vis_ref, coord_ref, *refs):
    out_refs, square = refs[:-1], refs[-1]
    me = lax.axis_index("corr")
    step = vis_ref.shape[0]
    nvis = vis_ref.shape[2]
    centred = (lax.broadcasted_iota(jnp.int32, (SUB, nvis), 0) - SUB // 2).astype(jnp.float32) * (1.0 / SUB)
    bend = 0.5 * centred * centred
    rows = ncorr * SUB
    pitch = rows + 1

    def one(s):
        u = coord_ref[0, pl.ds(s, 1), :]
        v = coord_ref[1, pl.ds(s, 1), :]
        w = coord_ref[2, pl.ds(s, 1), :]
        sag = w * bend
        e_re, e_im = cis_turns(u * centred - sag)
        f_re, f_im = cis_turns(v * centred - sag)
        vis = vis_ref[s].astype(jnp.float32)
        g_re = []
        g_im = []
        for e in range(ncorr):
            vr = vis[e : e + 1]
            vi = vis[ncorr + e : ncorr + e + 1]
            g_re.append((vr * e_re - vi * e_im).astype(jnp.bfloat16))
            g_im.append((vr * e_im + vi * e_re).astype(jnp.bfloat16))
        left = jnp.concatenate([jnp.concatenate(g_re, axis=0), jnp.concatenate(g_im, axis=0)], axis=1)
        f_re = f_re.astype(jnp.bfloat16)
        f_im = f_im.astype(jnp.bfloat16)
        right = jnp.concatenate(
            [jnp.concatenate([f_re, f_im], axis=0), jnp.concatenate([-f_im, f_re], axis=0)], axis=1
        )
        image = lax.dot_general(left, right, (((1,), (1,)), ((), ())), preferred_element_type=jnp.float32)
        square[pl.ds(s * pitch, rows), 0 : 2 * SUB] = image

    def several(i, carry):
        for j in range(4):
            one(i * 4 + j)
        return carry

    lax.fori_loop(0, step // 4, several, 0)

    lane = lax.broadcasted_iota(jnp.int32, (step, LANES), 1)
    low = lane < 2 * SUB
    even = (lane // SUB) % 2 == 0
    per_tile = LANES // SUB
    halves = SUB // groups // per_tile
    for d in range(groups):
        first = (me ^ d) * (halves * per_tile)
        for h in range(halves):
            for e in range(ncorr):
                p0, p1, p2, p3 = [
                    square[pl.ds(first + (e * SUB + h * per_tile + j), step, stride=pitch), :] for j in range(per_tile)
                ]
                evens = jnp.where(low, p0, pltpu.roll(p2, 2 * SUB, 1))
                odds = jnp.where(low, p1, pltpu.roll(p3, 2 * SUB, 1))
                real = jnp.where(even, evens, pltpu.roll(odds, SUB, 1))
                imag = jnp.where(even, pltpu.roll(evens, LANES - SUB, 1), odds)
                base = h * 2 * ncorr * LANES
                out_refs[d][:, base + e * LANES : base + (e + 1) * LANES] = real.astype(jnp.bfloat16)
                out_refs[d][:, base + (ncorr + e) * LANES : base + (ncorr + e + 1) * LANES] = imag.astype(jnp.bfloat16)


def make_images(visibilities, coords, groups):
    count, fields, nvis = visibilities.shape
    ncorr = fields // 2
    step = 16
    width = fields * PIX // groups
    return pl.pallas_call(
        functools.partial(image_kernel, ncorr, groups),
        grid=(count // step,),
        in_specs=[
            pl.BlockSpec((step, fields, nvis), lambda i: (i, 0, 0)),
            pl.BlockSpec((3, step, nvis), lambda i: (0, i, 0)),
        ],
        out_specs=[pl.BlockSpec((step, width), lambda i: (i, 0))] * groups,
        out_shape=[jax.ShapeDtypeStruct((count, width), jnp.bfloat16)] * groups,
        scratch_shapes=[pltpu.VMEM((step * (ncorr * SUB + 1), LANES), jnp.float32)],
        compiler_params=pltpu.CompilerParams(vmem_limit_bytes=VMEM_ALL),
        cost_estimate=pl.CostEstimate(flops=count << 27, bytes_accessed=2 << 20, transcendentals=0),
        name="images",
    )(visibilities, jnp.transpose(coords, (1, 0, 2)))


def plan_kernel(groups, owners, per_owner, count, every_ref, pick_ref, order_ref, place_ref, most_ref):
    nst = pick_ref.shape[1]
    n = groups * count
    together = LANES // count
    me = lax.axis_index("tile")
    side = lax.axis_index("corr")
    lane = lax.broadcasted_iota(jnp.int32, (8, LANES), 1)
    number = lax.broadcasted_iota(jnp.int32, (count, nst), 1).astype(jnp.float32)
    before = lax.broadcasted_iota(jnp.int32, (n, n), 0) < lax.broadcasted_iota(jnp.int32, (n, n), 1)
    before = before.astype(jnp.float32).astype(jnp.bfloat16)
    owner_row = lax.broadcasted_iota(jnp.int32, (owners, n), 0).astype(jnp.float32)
    slot = lax.broadcasted_iota(jnp.int32, (LANES, n), 0).astype(jnp.float32)
    row = lax.broadcasted_iota(jnp.int32, (8, LANES), 0)

    def group(t):
        tiles = []
        for g in range(0, groups, together):
            joined = None
            for k in range(together):
                facts = every_ref[t, side ^ (g + k)].astype(jnp.float32)
                facts = facts if k == 0 else pltpu.roll(facts, k * count, 1)
                joined = facts if k == 0 else jnp.where(lane < k * count, joined, facts)
            tiles.append(joined)
        return jnp.concatenate(tiles, axis=1)

    def ranks(facts):
        owner = jnp.floor(facts[0:1] * (1.0 / per_owner))
        hot = (owner_row == owner).astype(jnp.float32)
        ahead = jnp.dot(hot.astype(jnp.bfloat16), before, preferred_element_type=jnp.float32)
        return owner, jnp.sum(hot * ahead, axis=0, keepdims=True), jnp.sum(hot, axis=1, keepdims=True)

    for g in range(groups):
        columns = jnp.transpose(every_ref[me, side ^ g].astype(jnp.float32))
        for which in range(2):
            at = which * n + g * count
            station = columns[:count, 3 + which : 4 + which]
            pick_ref[at : at + count, :] = (number == station).astype(jnp.float32).astype(jnp.bfloat16)
    owner, rank, held = ranks(group(me))
    order_ref[0:1, :] = owner
    order_ref[1:2, :] = rank

    most = jnp.zeros((owners, 1), jnp.float32)
    for t in range(owners):
        facts = group(t)
        owner, rank, held = ranks(facts)
        most = jnp.maximum(most, held)
        here = jnp.where(owner == me.astype(jnp.float32), 1.0, 0.0)
        hit = jnp.where(slot == jnp.where(here > 0.0, rank, -1.0), 1.0, 0.0).astype(jnp.bfloat16)
        local = facts[0:1] - owner * per_owner
        values = jnp.concatenate([facts[1:3], local, jnp.zeros((5, n), jnp.float32)], axis=0).astype(jnp.bfloat16)
        found = lax.dot_general(values, hit, (((1,), (1,)), ((), ())), preferred_element_type=jnp.float32)
        total = jnp.sum(here, axis=1, keepdims=True)
        place_ref[t] = jnp.where(row == 4, total, found).astype(jnp.int32)
    most_ref[...] = jnp.broadcast_to(jnp.max(most, axis=0, keepdims=True), most_ref.shape).astype(jnp.int32)


def make_plan(every, groups, owners, per_owner, count, nst):
    n = groups * count
    return pl.pallas_call(
        functools.partial(plan_kernel, groups, owners, per_owner, count),
        out_shape=[
            jax.ShapeDtypeStruct((2 * n, nst), jnp.bfloat16),
            jax.ShapeDtypeStruct((8, n), jnp.float32),
            jax.ShapeDtypeStruct((owners, 8, LANES), jnp.int32),
            jax.ShapeDtypeStruct((8, LANES), jnp.int32),
        ],
        compiler_params=pltpu.CompilerParams(vmem_limit_bytes=VMEM_LIMIT),
        cost_estimate=pl.CostEstimate(flops=1 << 30, bytes_accessed=1 << 20, transcendentals=0),
        name="plan",
    )(every)


def aterm_kernel(ncorr, owners, rows_of, scale, *refs):
    groups = len(refs) - 6
    image_refs, refs = refs[:groups], refs[groups:]
    screen_ref, pick_ref, order_ref, out_ref, block_ref, jones_ref = refs
    count = image_refs[0].shape[0]
    n = groups * count
    me = lax.axis_index("corr")
    jones_ref[...] = jnp.dot(pick_ref[...], screen_ref[...], preferred_element_type=jnp.float32)
    pixel = lax.broadcasted_iota(jnp.int32, (1, LANES), 1) + (me * pl.num_programs(0) + pl.program_id(0)) * LANES
    row_at = ((pixel // SUB).astype(jnp.float32) - (SUB - 1) / 2.0) * (2.0 / SUB)
    col_at = ((pixel % SUB).astype(jnp.float32) - (SUB - 1) / 2.0) * (2.0 / SUB)
    taper = (1.0 - 0.8 * row_at * row_at) * (1.0 - 0.8 * col_at * col_at) * scale
    chunk = 16

    def part(ref, rows, field):
        return ref[rows, field * LANES : (field + 1) * LANES].astype(jnp.float32)

    def body(d, i, carry):
        held = pl.ds(pl.multiple_of(i * chunk, chunk), chunk)
        at = (me ^ d) * count + i * chunk
        rows = pl.ds(pl.multiple_of(at, chunk), chunk)
        far_rows = pl.ds(pl.multiple_of(at + n, chunk), chunk)
        image_re = [part(image_refs[d], held, e) for e in range(ncorr)]
        image_im = [part(image_refs[d], held, ncorr + e) for e in range(ncorr)]
        for row_out in range(2):
            mid_re = []
            mid_im = []
            for inner in range(2):
                m_re = 0.0
                m_im = 0.0
                for first in range(2):
                    near_re = part(jones_ref, rows, 2 * first + row_out)
                    near_im = part(jones_ref, rows, ncorr + 2 * first + row_out)
                    vis_re = image_re[2 * first + inner]
                    vis_im = image_im[2 * first + inner]
                    m_re = m_re + near_re * vis_re + near_im * vis_im
                    m_im = m_im + near_re * vis_im - near_im * vis_re
                mid_re.append(m_re)
                mid_im.append(m_im)
            for col_out in range(2):
                t_re = 0.0
                t_im = 0.0
                for inner in range(2):
                    far_re = part(jones_ref, far_rows, 2 * inner + col_out)
                    far_im = part(jones_ref, far_rows, ncorr + 2 * inner + col_out)
                    t_re = t_re + mid_re[inner] * far_re - mid_im[inner] * far_im
                    t_im = t_im + mid_re[inner] * far_im + mid_im[inner] * far_re
                place = 2 * (2 * row_out + col_out) * LANES
                block_ref[rows, place : place + LANES] = (t_re * taper).astype(jnp.bfloat16)
                block_ref[rows, place + LANES : place + 2 * LANES] = (t_im * taper).astype(jnp.bfloat16)
        return carry

    for d in range(groups):
        lax.fori_loop(0, count // chunk, functools.partial(body, d), 0)
    target = order_ref[0:1, :] * float(rows_of) + order_ref[1:2, :]
    row = lax.broadcasted_iota(jnp.int32, (owners * rows_of, n), 0).astype(jnp.float32)
    move = (row == target).astype(jnp.float32).astype(jnp.bfloat16)
    for e in range(ncorr):
        block = block_ref[:, 2 * e * LANES : 2 * (e + 1) * LANES]
        out_ref[e] = jnp.dot(move, block, preferred_element_type=jnp.float32).astype(jnp.bfloat16)


def apply_aterms(images, screens, pick, order, scale, ncorr, owners, rows):
    count = images[0].shape[0]
    n = count * len(images)
    nst = screens.shape[0]
    half = 2 * ncorr * LANES
    halves = screens.shape[1] // half
    return pl.pallas_call(
        functools.partial(aterm_kernel, ncorr, owners, rows, scale),
        grid=(halves,),
        in_specs=[pl.BlockSpec((count, half), lambda h: (0, h))] * len(images)
        + [
            pl.BlockSpec((nst, half), lambda h: (0, h)),
            pl.BlockSpec(pick.shape, lambda h: (0, 0)),
            pl.BlockSpec(order.shape, lambda h: (0, 0)),
        ],
        out_specs=pl.BlockSpec((ncorr, owners * rows, 2 * LANES), lambda h: (0, 0, h)),
        out_shape=jax.ShapeDtypeStruct((ncorr, owners * rows, halves * 2 * LANES), jnp.bfloat16),
        scratch_shapes=[pltpu.VMEM((n, half), jnp.bfloat16), pltpu.VMEM((2 * n, half), jnp.float32)],
        compiler_params=pltpu.CompilerParams(vmem_limit_bytes=VMEM_ALL),
        cost_estimate=pl.CostEstimate(flops=6 << 30, bytes_accessed=8 << 20, transcendentals=0),
        name="aterms",
    )(*images, screens, pick, order)


def grid_kernel(rows, place_ref, block_ref, col_ref, row_ref, out_ref, half_ref, uv_ref, turned_a, turned_b, re_a, im_a, re_b, im_b):
    groups, total, depth = block_ref.shape
    sources = total // rows
    per_slot = 2 * PIX // LANES + 1
    quarters = depth // LANES
    low = lax.broadcasted_iota(jnp.int32, (total, LANES), 1) < LANES // 2
    for c in range(groups):
        tiles = []
        for h in range(2):
            block = block_ref[c, :, 2 * h * LANES : 2 * (h + 1) * LANES]
            tiles.append(jnp.dot(block, col_ref[...], preferred_element_type=jnp.float32))
        for j in range(2):
            one, two = [tile[:, j * LANES : (j + 1) * LANES] for tile in tiles]
            first = jnp.where(low, one, pltpu.roll(two, LANES // 2, 1))
            second = jnp.where(low, pltpu.roll(one, LANES // 2, 1), two)
            half_ref[c, :, 2 * j * LANES : (2 * j + 1) * LANES] = first.astype(jnp.bfloat16)
            half_ref[c, :, (2 * j + 1) * LANES : (2 * j + 2) * LANES] = second.astype(jnp.bfloat16)
    for q in range(quarters):
        left = jnp.concatenate([half_ref[g, :, q * LANES : (q + 1) * LANES] for g in range(groups)], axis=1)
        uv = jnp.dot(left, row_ref[...], preferred_element_type=jnp.float32)
        for part in range(2):
            for i in range(2):
                j = part * 2 + i
                uv_ref[pl.ds(part * 8 + 2 * q + i, total, stride=per_slot), :] = uv[:, j * LANES : (j + 1) * LANES]
    for ref in (re_a, im_a, re_b, im_b):
        ref[...] = jnp.zeros_like(ref)

    lane = lax.broadcasted_iota(jnp.int32, (8, LANES), 1)
    pieces = LANES // SUB
    tall = 2 * pieces * 8
    batch = 8
    longest = place_ref[0, 4, 0]
    for t in range(1, sources):
        longest = jnp.maximum(longest, place_ref[t, 4, 0])
    trips = (longest + (batch - 1)) // batch
    turned = (turned_a, turned_b)

    def turn(t, i):
        for b in range(batch):
            j = i * batch + b
            y = place_ref[t, 1, j]
            inside = (lane >= y) & (lane < y + SUB)
            for part in range(2):
                at = (t * rows + j) * per_slot + part * 8
                block = uv_ref[pl.ds(at, 8), :]
                for g in range(pieces):
                    moved = pltpu.roll(block, (y + (LANES - g * SUB)) & (LANES - 1), 1)
                    at = pl.multiple_of(j * tall + (part * pieces + g) * 8, 8)
                    turned[t % 2][pl.ds(at, 8), :] = jnp.where(inside, moved, 0.0)

    def add(t, i):
        for b in range(batch):
            j = i * batch + b
            row = place_ref[t, 2, j] * TILE_SIDE + place_ref[t, 0, j]
            for part, ref in enumerate((re_a, im_a) if b % 2 == 0 else (re_b, im_b)):
                at = pl.multiple_of(j * tall + part * pieces * 8, 8)
                ref[pl.ds(row, SUB), :] = ref[pl.ds(row, SUB), :] + turned[t % 2][pl.ds(at, SUB), :]

    for t in range(sources + 1):

        def both(i, carry):
            if t < sources:
                turn(t, i)
            if t > 0:
                add(t - 1, i)
            return carry

        lax.fori_loop(0, trips, both, 0)

    for k in range(out_ref.shape[0]):
        span = slice(k * TILE_SIDE, (k + 1) * TILE_SIDE)
        for part, (one, two) in enumerate(((re_a, re_b), (im_a, im_b))):
            out_ref[k, part] = one[span, :] + two[span, :]


def place_on_grid(places, blocks, rows, tables, per_owner):
    groups, total, depth = blocks.shape
    whole = pl.BlockSpec(memory_space=pltpu.VMEM)
    accumulator = pltpu.VMEM((per_owner * TILE_SIDE, TILE_SIDE), jnp.float32)
    return pl.pallas_call(
        functools.partial(grid_kernel, rows),
        in_specs=[pl.BlockSpec(memory_space=pltpu.SMEM), whole, whole, whole],
        out_specs=whole,
        out_shape=jax.ShapeDtypeStruct((per_owner, 2, TILE_SIDE, TILE_SIDE), jnp.float32),
        scratch_shapes=[
            pltpu.VMEM((groups, total, depth), jnp.bfloat16),
            pltpu.VMEM((total * (2 * PIX // LANES + 1), LANES), jnp.float32),
            pltpu.VMEM((rows * 2 * PIX // SUB, LANES), jnp.float32),
            pltpu.VMEM((rows * 2 * PIX // SUB, LANES), jnp.float32),
            accumulator,
            accumulator,
            accumulator,
            accumulator,
        ],
        compiler_params=pltpu.CompilerParams(vmem_limit_bytes=VMEM_LIMIT),
        name="grid",
    )(places, blocks, *tables)


def uv_tables(groups):
    quad = LANES // SUB
    halves = SUB // (groups * quad)
    index = np.arange(SUB) - SUB // 2
    factor = np.exp(-2j * np.pi / SUB * ((index[:, None] * index[None, :]) % SUB))

    def parts(table, axis):
        upper = np.stack([table.real, table.imag], axis=axis)
        lower = np.stack([-table.imag, table.real], axis=axis)
        return upper, lower

    col = (factor / SUB).reshape(SUB, 4, 4, 2).transpose(2, 0, 3, 1)
    first = np.zeros((2, quad, SUB, 4, 2, quad, 2, 4))
    for p, table in enumerate(parts(col, 0)):
        for r in range(quad):
            first[p, r, :, :, :, r] = table.transpose(2, 1, 0, 3, 4)
    second = np.zeros((groups, halves, 2, quad, 2, 4, 2, 2, 4, SUB))
    row = factor.reshape(groups, halves, quad, SUB)
    for p, table in enumerate(parts(row, 0)):
        for i in range(2):
            for g in range(4):
                second[:, :, p, :, i, g, :, i, g, :] = table.transpose(1, 2, 3, 0, 4)
    first = first.reshape(2 * LANES, 2 * LANES)
    second = second.reshape(groups * halves * 2 * quad * 8, 4 * LANES)
    return first.astype(jnp.bfloat16), second.astype(jnp.bfloat16)


def per_device(visibilities, coords, stations, tile_ids, offsets, screens):
    count, fields, nvis = visibilities.shape
    ncorr = fields // 2
    groups = lax.axis_size("corr")
    owners = lax.axis_size("tile")
    corr = lax.axis_index("corr")
    tile = lax.axis_index("tile")
    per_owner = NT // owners
    full = per_owner * groups * (2 * count // NT)
    halves = PIX // (groups * LANES)
    local = PIX // groups

    part = lax.dynamic_slice_in_dim(screens, corr * local, local, axis=2)
    part = part.reshape(-1, fields, halves, LANES).transpose(0, 2, 1, 3).reshape(-1, fields * local)
    all_screens = lax.all_gather(part, "tile", axis=0, tiled=True)

    facts = jnp.concatenate([tile_ids.T, offsets.T, stations.T], axis=0)
    facts = jnp.pad(facts, ((0, 8 - facts.shape[0]), (0, LANES - count)))
    partners = [[(i, i ^ d) for i in range(groups)] for d in range(groups)]
    facts = jnp.stack([lax.ppermute(facts, "corr", partners[d]) if d else facts for d in range(groups)])

    images = list(make_images(visibilities, coords, groups))
    facts, images[0] = lax.optimization_barrier((facts, images[0]))
    every = jnp.broadcast_to(facts[None], (owners,) + facts.shape)
    every = lax.all_to_all(every, "tile", split_axis=0, concat_axis=0, tiled=True)
    images = [lax.ppermute(piece, "corr", partners[d]) if d else piece for d, piece in enumerate(images)]
    pick, order, places, most = make_plan(every, groups, owners, per_owner, count, all_screens.shape[0])

    tables = tuple(jnp.asarray(table) for table in uv_tables(groups))

    def finish(rows, images, screens, pick, order, places):
        sending = apply_aterms(images, screens, pick, order, 1.0 / nvis, ncorr, owners, rows)
        received = lax.all_to_all(
            sending.reshape(groups * owners, rows, 2 * local), ("corr", "tile"), split_axis=0, concat_axis=0, tiled=True
        )
        return place_on_grid(places, received.reshape(groups, owners * rows, 2 * local), rows, tables, per_owner)

    heights = sorted({min(full, -(-full * share // 64) * 8) for share in (5, 6, 8)})
    branches = [functools.partial(finish, rows) for rows in heights]
    if len(heights) == 1:
        grid = branches[0](images, all_screens, pick, order, places)
    else:
        index = sum((most[0, 0] > rows).astype(jnp.int32) for rows in heights[:-1])
        grid = lax.switch(index, branches, images, all_screens, pick, order, places)
    return grid[None]


def solution(mesh):
    return jax.shard_map(
        per_device,
        mesh=mesh,
        in_specs=(
            P(("corr", "tile"), None, None),
            P(("corr", "tile"), None, None),
            P(("corr", "tile"), None),
            P(("corr", "tile"), None),
            P(("corr", "tile"), None),
            P("tile", None, None),
        ),
        out_specs=P("corr", "tile", None, None, None),
        check_vma=False,
    )
```

```python
import functools
import math

import jax
import jax.numpy as jnp
import numpy as np
from jax import lax
from jax.experimental import pallas as pl
from jax.experimental.pallas import tpu as pltpu
from jax.sharding import PartitionSpec as P

SUB = 32
NT = 64
TILE_SIDE = 128
PIX = SUB * SUB
LANES = 128
VMEM_LIMIT = 36 * 1024 * 1024
VMEM_ALL = 63 * 1024 * 1024 + 512 * 1024

ROOT2 = math.sqrt(2.0)


def half_turn_series():
    grid = np.cos(np.pi * (np.arange(400) + 0.5) / 800.0) * 0.5
    z = grid * grid
    sine = np.polynomial.polynomial.Polynomial.fit(z, np.sin(np.pi * grid) / grid, 3, domain=[0, 0.25], window=[0, 0.25]).coef
    cosine = np.polynomial.polynomial.Polynomial.fit(z, np.cos(np.pi * grid), 3, domain=[0, 0.25], window=[0, 0.25]).coef
    return [float(x) * ROOT2 for x in sine], [float(x) * ROOT2 for x in cosine]


SINE, COSINE = half_turn_series()


def horner(coefficients, z):
    total = coefficients[-1]
    for value in coefficients[-2::-1]:
        total = total * z + value
    return total


def cis_turns(turns):
    t = turns - jnp.round(turns)
    z = t * t
    s = t * horner(SINE, z)
    c = horner(COSINE, z)
    return 1.0 - s * s, s * c


def image_kernel(ncorr, groups, vis_ref, coord_ref, *refs):
    out_refs, square = refs[:-1], refs[-1]
    me = lax.axis_index("corr")
    step = vis_ref.shape[0]
    nvis = vis_ref.shape[2]
    centred = (lax.broadcasted_iota(jnp.int32, (SUB, nvis), 0) - SUB // 2).astype(jnp.float32) * (1.0 / SUB)
    bend = 0.5 * centred * centred
    rows = ncorr * SUB
    pitch = rows + 1

    def one(s):
        u = coord_ref[0, pl.ds(s, 1), :]
        v = coord_ref[1, pl.ds(s, 1), :]
        w = coord_ref[2, pl.ds(s, 1), :]
        sag = w * bend
        e_re, e_im = cis_turns(u * centred - sag)
        f_re, f_im = cis_turns(v * centred - sag)
        vis = vis_ref[s].astype(jnp.float32)
        g_re = []
        g_im = []
        for e in range(ncorr):
            vr = vis[e : e + 1]
            vi = vis[ncorr + e : ncorr + e + 1]
            g_re.append((vr * e_re - vi * e_im).astype(jnp.bfloat16))
            g_im.append((vr * e_im + vi * e_re).astype(jnp.bfloat16))
        left = jnp.concatenate([jnp.concatenate(g_re, axis=0), jnp.concatenate(g_im, axis=0)], axis=1)
        f_re = f_re.astype(jnp.bfloat16)
        f_im = f_im.astype(jnp.bfloat16)
        right = jnp.concatenate(
            [jnp.concatenate([f_re, f_im], axis=0), jnp.concatenate([-f_im, f_re], axis=0)], axis=1
        )
        image = lax.dot_general(left, right, (((1,), (1,)), ((), ())), preferred_element_type=jnp.float32)
        square[pl.ds(s * pitch, rows), 0 : 2 * SUB] = image

    def several(i, carry):
        for j in range(4):
            one(i * 4 + j)
        return carry

    lax.fori_loop(0, step // 4, several, 0)

    lane = lax.broadcasted_iota(jnp.int32, (step, LANES), 1)
    per_tile = LANES // SUB
    halves = SUB // groups // per_tile
    for d in range(groups):
        first = (me ^ d) * (halves * per_tile)
        for h in range(halves):
            for e in range(ncorr):
                real = None
                imag = None
                for j in range(per_tile):
                    piece = square[pl.ds(first + (e * SUB + h * per_tile + j), step, stride=pitch), :]
                    a = piece if j == 0 else pltpu.roll(piece, SUB * j, 1)
                    b = piece if j == 1 else pltpu.roll(piece, (SUB * (j - 1)) % LANES, 1)
                    keep = lane < SUB * (j + 1)
                    real = a if real is None else jnp.where(lane < SUB * j, real, a)
                    imag = b if imag is None else jnp.where(lane < SUB * j, imag, b)
                base = h * 2 * ncorr * LANES
                out_refs[d][:, base + e * LANES : base + (e + 1) * LANES] = real.astype(jnp.bfloat16)
                out_refs[d][:, base + (ncorr + e) * LANES : base + (ncorr + e + 1) * LANES] = imag.astype(jnp.bfloat16)


def make_images(visibilities, coords, groups, first, size):
    count, fields, nvis = visibilities.shape
    ncorr = fields // 2
    step = 16
    width = fields * PIX // groups
    return pl.pallas_call(
        functools.partial(image_kernel, ncorr, groups),
        grid=(size // step,),
        in_specs=[
            pl.BlockSpec((step, fields, nvis), lambda i: (i + first // step, 0, 0)),
            pl.BlockSpec((3, step, nvis), lambda i: (0, i + first // step, 0)),
        ],
        out_specs=[pl.BlockSpec((step, width), lambda i: (i, 0))] * groups,
        out_shape=[jax.ShapeDtypeStruct((size, width), jnp.bfloat16)] * groups,
        scratch_shapes=[pltpu.VMEM((step * (ncorr * SUB + 1), LANES), jnp.float32)],
        compiler_params=pltpu.CompilerParams(vmem_limit_bytes=VMEM_LIMIT),
        cost_estimate=pl.CostEstimate(flops=size << 27, bytes_accessed=2 << 20, transcendentals=0),
        name="images",
    )(visibilities, jnp.transpose(coords, (1, 0, 2)))


def plan_kernel(groups, owners, per_owner, count, every_ref, pick_ref, order_ref, place_ref, most_ref):
    nst = pick_ref.shape[1]
    n = groups * count
    together = LANES // count
    me = lax.axis_index("tile")
    lane = lax.broadcasted_iota(jnp.int32, (8, LANES), 1)
    number = lax.broadcasted_iota(jnp.int32, (count, nst), 1).astype(jnp.float32)
    before = lax.broadcasted_iota(jnp.int32, (n, n), 0) < lax.broadcasted_iota(jnp.int32, (n, n), 1)
    before = before.astype(jnp.float32).astype(jnp.bfloat16)
    owner_row = lax.broadcasted_iota(jnp.int32, (owners, n), 0).astype(jnp.float32)
    slot = lax.broadcasted_iota(jnp.int32, (LANES, n), 0).astype(jnp.float32)
    row = lax.broadcasted_iota(jnp.int32, (8, LANES), 0)

    def group(t):
        tiles = []
        for g in range(0, groups, together):
            joined = None
            for k in range(together):
                facts = every_ref[(g + k) * owners + t].astype(jnp.float32)
                facts = facts if k == 0 else pltpu.roll(facts, k * count, 1)
                joined = facts if k == 0 else jnp.where(lane < k * count, joined, facts)
            tiles.append(joined)
        return jnp.concatenate(tiles, axis=1)

    def ranks(facts):
        owner = jnp.floor(facts[0:1] * (1.0 / per_owner))
        hot = (owner_row == owner).astype(jnp.float32)
        ahead = jnp.dot(hot.astype(jnp.bfloat16), before, preferred_element_type=jnp.float32)
        return owner, jnp.sum(hot * ahead, axis=0, keepdims=True), jnp.sum(hot, axis=1, keepdims=True)

    for g in range(groups):
        columns = jnp.transpose(every_ref[g * owners + me].astype(jnp.float32))
        for which in range(2):
            at = which * n + g * count
            station = columns[:count, 3 + which : 4 + which]
            pick_ref[at : at + count, :] = (number == station).astype(jnp.float32).astype(jnp.bfloat16)
    owner, rank, held = ranks(group(me))
    order_ref[0:1, :] = owner
    order_ref[1:2, :] = rank

    most = jnp.zeros((owners, 1), jnp.float32)
    for t in range(owners):
        facts = group(t)
        owner, rank, held = ranks(facts)
        most = jnp.maximum(most, held)
        here = jnp.where(owner == me.astype(jnp.float32), 1.0, 0.0)
        hit = jnp.where(slot == jnp.where(here > 0.0, rank, -1.0), 1.0, 0.0).astype(jnp.bfloat16)
        local = facts[0:1] - owner * per_owner
        values = jnp.concatenate([facts[1:3], local, jnp.zeros((5, n), jnp.float32)], axis=0).astype(jnp.bfloat16)
        found = lax.dot_general(values, hit, (((1,), (1,)), ((), ())), preferred_element_type=jnp.float32)
        total = jnp.sum(here, axis=1, keepdims=True)
        place_ref[t] = jnp.where(row == 4, total, found).astype(jnp.int32)
    most_ref[...] = jnp.broadcast_to(jnp.max(most, axis=0, keepdims=True), most_ref.shape).astype(jnp.int32)


def make_plan(every, groups, owners, per_owner, count, nst):
    n = groups * count
    return pl.pallas_call(
        functools.partial(plan_kernel, groups, owners, per_owner, count),
        out_shape=[
            jax.ShapeDtypeStruct((2 * n, nst), jnp.bfloat16),
            jax.ShapeDtypeStruct((8, n), jnp.float32),
            jax.ShapeDtypeStruct((owners, 8, LANES), jnp.int32),
            jax.ShapeDtypeStruct((8, LANES), jnp.int32),
        ],
        compiler_params=pltpu.CompilerParams(vmem_limit_bytes=VMEM_LIMIT),
        cost_estimate=pl.CostEstimate(flops=1 << 30, bytes_accessed=1 << 20, transcendentals=0),
        name="plan",
    )(every)


def aterm_kernel(ncorr, owners, rows_of, scale, groups, *refs):
    image_refs, refs = refs[:-6], refs[-6:]
    screen_ref, pick_ref, order_ref, out_ref, block_ref, jones_ref = refs
    n = order_ref.shape[1]
    count = n // groups
    me = lax.axis_index("corr")
    jones_ref[...] = jnp.dot(pick_ref[...], screen_ref[...], preferred_element_type=jnp.float32)
    pixel = lax.broadcasted_iota(jnp.int32, (1, LANES), 1) + (me * pl.num_programs(0) + pl.program_id(0)) * LANES
    row_at = ((pixel // SUB).astype(jnp.float32) - (SUB - 1) / 2.0) * (2.0 / SUB)
    col_at = ((pixel % SUB).astype(jnp.float32) - (SUB - 1) / 2.0) * (2.0 / SUB)
    taper = (1.0 - 0.8 * row_at * row_at) * (1.0 - 0.8 * col_at * col_at) * scale
    chunk = 16

    def part(ref, rows, field):
        return ref[rows, field * LANES : (field + 1) * LANES].astype(jnp.float32)

    def body(ref, d, begin, i, carry):
        held = pl.ds(pl.multiple_of(i * chunk, chunk), chunk)
        at = (me ^ d) * count + begin + i * chunk
        rows = pl.ds(pl.multiple_of(at, chunk), chunk)
        far_rows = pl.ds(pl.multiple_of(at + n, chunk), chunk)
        image_re = [part(ref, held, e) for e in range(ncorr)]
        image_im = [part(ref, held, ncorr + e) for e in range(ncorr)]
        for row_out in range(2):
            mid_re = []
            mid_im = []
            for inner in range(2):
                m_re = 0.0
                m_im = 0.0
                for first in range(2):
                    near_re = part(jones_ref, rows, 2 * first + row_out)
                    near_im = part(jones_ref, rows, ncorr + 2 * first + row_out)
                    vis_re = image_re[2 * first + inner]
                    vis_im = image_im[2 * first + inner]
                    m_re = m_re + near_re * vis_re + near_im * vis_im
                    m_im = m_im + near_re * vis_im - near_im * vis_re
                mid_re.append(m_re)
                mid_im.append(m_im)
            for col_out in range(2):
                t_re = 0.0
                t_im = 0.0
                for inner in range(2):
                    far_re = part(jones_ref, far_rows, 2 * inner + col_out)
                    far_im = part(jones_ref, far_rows, ncorr + 2 * inner + col_out)
                    t_re = t_re + mid_re[inner] * far_re - mid_im[inner] * far_im
                    t_im = t_im + mid_re[inner] * far_im + mid_im[inner] * far_re
                place = 2 * (2 * row_out + col_out) * LANES
                block_ref[rows, place : place + LANES] = (t_re * taper).astype(jnp.bfloat16)
                block_ref[rows, place + LANES : place + 2 * LANES] = (t_im * taper).astype(jnp.bfloat16)
        return carry

    for p, ref in enumerate(image_refs):
        begin = sum(other.shape[0] for other in image_refs[p % groups : p : groups])
        lax.fori_loop(0, ref.shape[0] // chunk, functools.partial(body, ref, p % groups, begin), 0)
    target = order_ref[0:1, :] * float(rows_of) + order_ref[1:2, :]
    row = lax.broadcasted_iota(jnp.int32, (owners * rows_of, n), 0).astype(jnp.float32)
    move = (row == target).astype(jnp.float32).astype(jnp.bfloat16)
    for e in range(ncorr):
        block = block_ref[:, 2 * e * LANES : 2 * (e + 1) * LANES]
        out_ref[e] = jnp.dot(move, block, preferred_element_type=jnp.float32).astype(jnp.bfloat16)


def apply_aterms(images, groups, screens, pick, order, scale, ncorr, owners, rows):
    n = order.shape[1]
    nst = screens.shape[0]
    half = 2 * ncorr * LANES
    halves = screens.shape[1] // half
    return pl.pallas_call(
        functools.partial(aterm_kernel, ncorr, owners, rows, scale, groups),
        grid=(halves,),
        in_specs=[pl.BlockSpec((image.shape[0], half), lambda h: (0, h)) for image in images]
        + [
            pl.BlockSpec((nst, half), lambda h: (0, h)),
            pl.BlockSpec(pick.shape, lambda h: (0, 0)),
            pl.BlockSpec(order.shape, lambda h: (0, 0)),
        ],
        out_specs=pl.BlockSpec((ncorr, owners * rows, 2 * LANES), lambda h: (0, 0, h)),
        out_shape=jax.ShapeDtypeStruct((ncorr, owners * rows, halves * 2 * LANES), jnp.bfloat16),
        scratch_shapes=[pltpu.VMEM((n, half), jnp.bfloat16), pltpu.VMEM((2 * n, half), jnp.float32)],
        compiler_params=pltpu.CompilerParams(vmem_limit_bytes=VMEM_ALL),
        cost_estimate=pl.CostEstimate(flops=6 << 30, bytes_accessed=8 << 20, transcendentals=0),
        name="aterms",
    )(*images, screens, pick, order)


def grid_kernel(rows, place_ref, block_ref, col_ref, row_ref, out_ref, half_ref, uv_ref, turned_a, turned_b, re_a, im_a, re_b, im_b):
    groups, total, depth = block_ref.shape
    sources = total // rows
    per_slot = 2 * PIX // LANES + 1
    quarters = depth // LANES
    low = lax.broadcasted_iota(jnp.int32, (total, LANES), 1) < LANES // 2
    for c in range(groups):
        tiles = []
        for h in range(2):
            block = block_ref[c, :, 2 * h * LANES : 2 * (h + 1) * LANES]
            tiles.append(jnp.dot(block, col_ref[...], preferred_element_type=jnp.float32))
        for j in range(2):
            one, two = [tile[:, j * LANES : (j + 1) * LANES] for tile in tiles]
            first = jnp.where(low, one, pltpu.roll(two, LANES // 2, 1))
            second = jnp.where(low, pltpu.roll(one, LANES // 2, 1), two)
            half_ref[c, :, 2 * j * LANES : (2 * j + 1) * LANES] = first.astype(jnp.bfloat16)
            half_ref[c, :, (2 * j + 1) * LANES : (2 * j + 2) * LANES] = second.astype(jnp.bfloat16)
    for q in range(quarters):
        left = jnp.concatenate([half_ref[g, :, q * LANES : (q + 1) * LANES] for g in range(groups)], axis=1)
        uv = jnp.dot(left, row_ref[...], preferred_element_type=jnp.float32)
        for part in range(2):
            for i in range(2):
                j = part * 2 + i
                uv_ref[pl.ds(part * 8 + 2 * q + i, total, stride=per_slot), :] = uv[:, j * LANES : (j + 1) * LANES]
    for ref in (re_a, im_a, re_b, im_b):
        ref[...] = jnp.zeros_like(ref)

    lane = lax.broadcasted_iota(jnp.int32, (8, LANES), 1)
    pieces = LANES // SUB
    tall = 2 * pieces * 8
    batch = 8
    longest = place_ref[0, 4, 0]
    for t in range(1, sources):
        longest = jnp.maximum(longest, place_ref[t, 4, 0])
    trips = (longest + (batch - 1)) // batch
    turned = (turned_a, turned_b)

    def turn(t, i):
        for b in range(batch):
            j = i * batch + b
            y = place_ref[t, 1, j]
            inside = (lane >= y) & (lane < y + SUB)
            for part in range(2):
                at = (t * rows + j) * per_slot + part * 8
                block = uv_ref[pl.ds(at, 8), :]
                for g in range(pieces):
                    moved = pltpu.roll(block, (y + (LANES - g * SUB)) & (LANES - 1), 1)
                    at = pl.multiple_of(j * tall + (part * pieces + g) * 8, 8)
                    turned[t % 2][pl.ds(at, 8), :] = jnp.where(inside, moved, 0.0)

    def add(t, i):
        for b in range(batch):
            j = i * batch + b
            row = place_ref[t, 2, j] * TILE_SIDE + place_ref[t, 0, j]
            for part, ref in enumerate((re_a, im_a) if b % 2 == 0 else (re_b, im_b)):
                at = pl.multiple_of(j * tall + part * pieces * 8, 8)
                ref[pl.ds(row, SUB), :] = ref[pl.ds(row, SUB), :] + turned[t % 2][pl.ds(at, SUB), :]

    for t in range(sources + 1):

        def both(i, carry):
            if t < sources:
                turn(t, i)
            if t > 0:
                add(t - 1, i)
            return carry

        lax.fori_loop(0, trips, both, 0)

    for k in range(out_ref.shape[0]):
        span = slice(k * TILE_SIDE, (k + 1) * TILE_SIDE)
        for part, (one, two) in enumerate(((re_a, re_b), (im_a, im_b))):
            out_ref[k, part] = one[span, :] + two[span, :]


def place_on_grid(places, blocks, rows, tables, per_owner):
    groups, total, depth = blocks.shape
    whole = pl.BlockSpec(memory_space=pltpu.VMEM)
    accumulator = pltpu.VMEM((per_owner * TILE_SIDE, TILE_SIDE), jnp.float32)
    return pl.pallas_call(
        functools.partial(grid_kernel, rows),
        in_specs=[pl.BlockSpec(memory_space=pltpu.SMEM), whole, whole, whole],
        out_specs=whole,
        out_shape=jax.ShapeDtypeStruct((per_owner, 2, TILE_SIDE, TILE_SIDE), jnp.float32),
        scratch_shapes=[
            pltpu.VMEM((groups, total, depth), jnp.bfloat16),
            pltpu.VMEM((total * (2 * PIX // LANES + 1), LANES), jnp.float32),
            pltpu.VMEM((rows * 2 * PIX // SUB, LANES), jnp.float32),
            pltpu.VMEM((rows * 2 * PIX // SUB, LANES), jnp.float32),
            accumulator,
            accumulator,
            accumulator,
            accumulator,
        ],
        compiler_params=pltpu.CompilerParams(vmem_limit_bytes=VMEM_LIMIT),
        name="grid",
    )(places, blocks, *tables)


def uv_tables(groups):
    quad = LANES // SUB
    halves = SUB // (groups * quad)
    index = np.arange(SUB) - SUB // 2
    factor = np.exp(-2j * np.pi / SUB * ((index[:, None] * index[None, :]) % SUB))

    def parts(table, axis):
        upper = np.stack([table.real, table.imag], axis=axis)
        lower = np.stack([-table.imag, table.real], axis=axis)
        return upper, lower

    col = (factor / SUB).reshape(SUB, 4, 4, 2).transpose(2, 0, 3, 1)
    first = np.zeros((2, quad, SUB, 4, 2, quad, 2, 4))
    for p, table in enumerate(parts(col, 0)):
        for r in range(quad):
            first[p, r, :, :, :, r] = table.transpose(2, 1, 0, 3, 4)
    second = np.zeros((groups, halves, 2, quad, 2, 4, 2, 2, 4, SUB))
    row = factor.reshape(groups, halves, quad, SUB)
    for p, table in enumerate(parts(row, 0)):
        for i in range(2):
            for g in range(4):
                second[:, :, p, :, i, g, :, i, g, :] = table.transpose(1, 2, 3, 0, 4)
    first = first.reshape(2 * LANES, 2 * LANES)
    second = second.reshape(groups * halves * 2 * quad * 8, 4 * LANES)
    return first.astype(jnp.bfloat16), second.astype(jnp.bfloat16)


def per_device(visibilities, coords, stations, tile_ids, offsets, screens):
    count, fields, nvis = visibilities.shape
    ncorr = fields // 2
    groups = lax.axis_size("corr")
    owners = lax.axis_size("tile")
    corr = lax.axis_index("corr")
    tile = lax.axis_index("tile")
    per_owner = NT // owners
    full = per_owner * groups * (2 * count // NT)
    halves = PIX // (groups * LANES)
    local = PIX // groups

    part = lax.dynamic_slice_in_dim(screens, corr * local, local, axis=2)
    part = part.reshape(-1, fields, halves, LANES).transpose(0, 2, 1, 3).reshape(-1, fields * local)
    all_screens = lax.all_gather(part, "tile", axis=0, tiled=True)

    facts = jnp.concatenate([tile_ids.T, offsets.T, stations.T], axis=0)
    facts = jnp.pad(facts, ((0, 8 - facts.shape[0]), (0, LANES - count)))
    every = jnp.broadcast_to(facts[None], (groups * owners, 8, LANES))
    every = lax.all_to_all(every, ("corr", "tile"), split_axis=0, concat_axis=0, tiled=True)

    images = []
    for first, size in ((0, count * 3 // 4), (count * 3 // 4, count // 4)):
        for d, piece in enumerate(make_images(visibilities, coords, groups, first, size)):
            if first and d == groups - 1:
                images[1], piece = lax.optimization_barrier((images[1], piece))
            images.append(lax.ppermute(piece, "corr", [(i, i ^ d) for i in range(groups)]) if d else piece)
    pick, order, places, most = make_plan(every, groups, owners, per_owner, count, all_screens.shape[0])

    tables = tuple(jnp.asarray(table) for table in uv_tables(groups))

    def finish(rows, images, screens, pick, order, places):
        sending = apply_aterms(images, groups, screens, pick, order, 1.0 / nvis, ncorr, owners, rows)
        received = lax.all_to_all(
            sending.reshape(groups * owners, rows, 2 * local), ("corr", "tile"), split_axis=0, concat_axis=0, tiled=True
        )
        return place_on_grid(places, received.reshape(groups, owners * rows, 2 * local), rows, tables, per_owner)

    heights = sorted({min(full, -(-full * share // 64) * 8) for share in (5, 6, 8)})
    branches = [functools.partial(finish, rows) for rows in heights]
    if len(heights) == 1:
        grid = branches[0](images, all_screens, pick, order, places)
    else:
        index = sum((most[0, 0] > rows).astype(jnp.int32) for rows in heights[:-1])
        grid = lax.switch(index, branches, images, all_screens, pick, order, places)
    return grid[None]


def solution(mesh):
    return jax.shard_map(
        per_device,
        mesh=mesh,
        in_specs=(
            P(("corr", "tile"), None, None),
            P(("corr", "tile"), None, None),
            P(("corr", "tile"), None),
            P(("corr", "tile"), None),
            P(("corr", "tile"), None),
            P("tile", None, None),
        ),
        out_specs=P("corr", "tile", None, None, None),
        check_vma=False,
    )
```

```python
import functools
import math

import jax
import jax.numpy as jnp
import numpy as np
from jax import lax
from jax.experimental import pallas as pl
from jax.experimental.pallas import tpu as pltpu
from jax.sharding import PartitionSpec as P

SUB = 32
NT = 64
TILE_SIDE = 128
PIX = SUB * SUB
LANES = 128
VMEM_LIMIT = 36 * 1024 * 1024
VMEM_ALL = 63 * 1024 * 1024 + 512 * 1024

ROOT2 = math.sqrt(2.0)


def half_turn_series():
    grid = np.cos(np.pi * (np.arange(400) + 0.5) / 800.0) * 0.5
    z = grid * grid
    sine = np.polynomial.polynomial.Polynomial.fit(z, np.sin(np.pi * grid) / grid, 3, domain=[0, 0.25], window=[0, 0.25]).coef
    cosine = np.polynomial.polynomial.Polynomial.fit(z, np.cos(np.pi * grid), 3, domain=[0, 0.25], window=[0, 0.25]).coef
    return [float(x) * ROOT2 for x in sine], [float(x) * ROOT2 for x in cosine]


SINE, COSINE = half_turn_series()


def horner(coefficients, z):
    total = coefficients[-1]
    for value in coefficients[-2::-1]:
        total = total * z + value
    return total


def cis_turns(turns):
    t = turns - jnp.round(turns)
    z = t * t
    s = t * horner(SINE, z)
    c = horner(COSINE, z)
    return 1.0 - s * s, s * c


def image_kernel(ncorr, groups, vis_ref, coord_ref, *refs):
    out_refs, square = refs[:-1], refs[-1]
    me = lax.axis_index("corr")
    step = vis_ref.shape[0]
    nvis = vis_ref.shape[2]
    centred = (lax.broadcasted_iota(jnp.int32, (SUB, nvis), 0) - SUB // 2).astype(jnp.float32) * (1.0 / SUB)
    bend = 0.5 * centred * centred
    rows = ncorr * SUB
    pitch = rows + 1

    def one(s):
        u = coord_ref[0, pl.ds(s, 1), :]
        v = coord_ref[1, pl.ds(s, 1), :]
        w = coord_ref[2, pl.ds(s, 1), :]
        sag = w * bend
        e_re, e_im = cis_turns(u * centred - sag)
        f_re, f_im = cis_turns(v * centred - sag)
        vis = vis_ref[s].astype(jnp.float32)
        g_re = []
        g_im = []
        for e in range(ncorr):
            vr = vis[e : e + 1]
            vi = vis[ncorr + e : ncorr + e + 1]
            g_re.append((vr * e_re - vi * e_im).astype(jnp.bfloat16))
            g_im.append((vr * e_im + vi * e_re).astype(jnp.bfloat16))
        left = jnp.concatenate([jnp.concatenate(g_re, axis=0), jnp.concatenate(g_im, axis=0)], axis=1)
        f_re = f_re.astype(jnp.bfloat16)
        f_im = f_im.astype(jnp.bfloat16)
        right = jnp.concatenate(
            [jnp.concatenate([f_re, f_im], axis=0), jnp.concatenate([-f_im, f_re], axis=0)], axis=1
        )
        image = lax.dot_general(left, right, (((1,), (1,)), ((), ())), preferred_element_type=jnp.float32)
        square[pl.ds(s * pitch, rows), 0 : 2 * SUB] = image

    def several(i, carry):
        for j in range(4):
            one(i * 4 + j)
        return carry

    lax.fori_loop(0, step // 4, several, 0)

    lane = lax.broadcasted_iota(jnp.int32, (step, LANES), 1)
    per_tile = LANES // SUB
    halves = SUB // groups // per_tile
    for d in range(groups):
        first = (me ^ d) * (halves * per_tile)
        for h in range(halves):
            for e in range(ncorr):
                real = None
                imag = None
                for j in range(per_tile):
                    piece = square[pl.ds(first + (e * SUB + h * per_tile + j), step, stride=pitch), :]
                    a = piece if j == 0 else pltpu.roll(piece, SUB * j, 1)
                    b = piece if j == 1 else pltpu.roll(piece, (SUB * (j - 1)) % LANES, 1)
                    keep = lane < SUB * (j + 1)
                    real = a if real is None else jnp.where(lane < SUB * j, real, a)
                    imag = b if imag is None else jnp.where(lane < SUB * j, imag, b)
                base = h * 2 * ncorr * LANES
                out_refs[d][:, base + e * LANES : base + (e + 1) * LANES] = real.astype(jnp.bfloat16)
                out_refs[d][:, base + (ncorr + e) * LANES : base + (ncorr + e + 1) * LANES] = imag.astype(jnp.bfloat16)


def make_images(visibilities, coords, groups, first, size):
    count, fields, nvis = visibilities.shape
    ncorr = fields // 2
    step = 16
    width = fields * PIX // groups
    return pl.pallas_call(
        functools.partial(image_kernel, ncorr, groups),
        grid=(size // step,),
        in_specs=[
            pl.BlockSpec((step, fields, nvis), lambda i: (i + first // step, 0, 0)),
            pl.BlockSpec((3, step, nvis), lambda i: (0, i + first // step, 0)),
        ],
        out_specs=[pl.BlockSpec((step, width), lambda i: (i, 0))] * groups,
        out_shape=[jax.ShapeDtypeStruct((size, width), jnp.bfloat16)] * groups,
        scratch_shapes=[pltpu.VMEM((step * (ncorr * SUB + 1), LANES), jnp.float32)],
        compiler_params=pltpu.CompilerParams(vmem_limit_bytes=VMEM_LIMIT),
        cost_estimate=pl.CostEstimate(flops=size << 27, bytes_accessed=2 << 20, transcendentals=0),
        name="images",
    )(visibilities, jnp.transpose(coords, (1, 0, 2)))


def pixels_kernel(screen_ref, out_ref, held, rows_ref, sem):
    stations, fields, local = held.shape
    me = lax.axis_index("corr")
    copy = pltpu.make_async_copy(screen_ref.at[:, :, pl.ds(pl.multiple_of(me * local, local), local)], held, sem)
    copy.start()
    copy.wait()
    pitch = fields + 1
    halves = local // LANES
    for s in range(stations):
        station = held[s].astype(jnp.float32)
        for h in range(halves):
            rows_ref[h, s * pitch : s * pitch + fields, :] = station[:, h * LANES : (h + 1) * LANES]
    for h in range(halves):
        for f in range(fields):
            at = (h * fields + f) * LANES
            out_ref[:, at : at + LANES] = rows_ref[h, pl.ds(f, stations, stride=pitch), :].astype(jnp.bfloat16)


def own_pixels(screens, groups):
    stations, fields, pixels = screens.shape
    local = pixels // groups
    return pl.pallas_call(
        pixels_kernel,
        in_specs=[pl.BlockSpec(memory_space=pl.ANY)],
        out_specs=pl.BlockSpec(memory_space=pltpu.VMEM),
        out_shape=jax.ShapeDtypeStruct((stations, fields * local), jnp.bfloat16),
        scratch_shapes=[
            pltpu.VMEM((stations, fields, local), jnp.bfloat16),
            pltpu.VMEM((local // LANES, stations * (fields + 1), LANES), jnp.float32),
            pltpu.SemaphoreType.DMA(()),
        ],
        compiler_params=pltpu.CompilerParams(vmem_limit_bytes=VMEM_ALL),
        name="pixels",
    )(screens)


def plan_kernel(groups, owners, per_owner, count, every_ref, pick_ref, order_ref, place_ref, most_ref):
    nst = pick_ref.shape[1]
    n = groups * count
    together = LANES // count
    me = lax.axis_index("tile")
    lane = lax.broadcasted_iota(jnp.int32, (8, LANES), 1)
    number = lax.broadcasted_iota(jnp.int32, (count, nst), 1).astype(jnp.float32)
    before = lax.broadcasted_iota(jnp.int32, (n, n), 0) < lax.broadcasted_iota(jnp.int32, (n, n), 1)
    before = before.astype(jnp.float32).astype(jnp.bfloat16)
    owner_row = lax.broadcasted_iota(jnp.int32, (owners, n), 0).astype(jnp.float32)
    slot = lax.broadcasted_iota(jnp.int32, (LANES, n), 0).astype(jnp.float32)
    row = lax.broadcasted_iota(jnp.int32, (8, LANES), 0)

    def group(t):
        tiles = []
        for g in range(0, groups, together):
            joined = None
            for k in range(together):
                facts = every_ref[(g + k) * owners + t].astype(jnp.float32)
                facts = facts if k == 0 else pltpu.roll(facts, k * count, 1)
                joined = facts if k == 0 else jnp.where(lane < k * count, joined, facts)
            tiles.append(joined)
        return jnp.concatenate(tiles, axis=1)

    def ranks(facts):
        owner = jnp.floor(facts[0:1] * (1.0 / per_owner))
        hot = (owner_row == owner).astype(jnp.float32)
        ahead = jnp.dot(hot.astype(jnp.bfloat16), before, preferred_element_type=jnp.float32)
        return owner, jnp.sum(hot * ahead, axis=0, keepdims=True), jnp.sum(hot, axis=1, keepdims=True)

    for g in range(groups):
        columns = jnp.transpose(every_ref[g * owners + me].astype(jnp.float32))
        for which in range(2):
            at = which * n + g * count
            station = columns[:count, 3 + which : 4 + which]
            pick_ref[at : at + count, :] = (number == station).astype(jnp.float32).astype(jnp.bfloat16)
    owner, rank, held = ranks(group(me))
    order_ref[0:1, :] = owner
    order_ref[1:2, :] = rank

    most = jnp.zeros((owners, 1), jnp.float32)
    for t in range(owners):
        facts = group(t)
        owner, rank, held = ranks(facts)
        most = jnp.maximum(most, held)
        here = jnp.where(owner == me.astype(jnp.float32), 1.0, 0.0)
        hit = jnp.where(slot == jnp.where(here > 0.0, rank, -1.0), 1.0, 0.0).astype(jnp.bfloat16)
        local = facts[0:1] - owner * per_owner
        values = jnp.concatenate([facts[1:3], local, jnp.zeros((5, n), jnp.float32)], axis=0).astype(jnp.bfloat16)
        found = lax.dot_general(values, hit, (((1,), (1,)), ((), ())), preferred_element_type=jnp.float32)
        total = jnp.sum(here, axis=1, keepdims=True)
        place_ref[t] = jnp.where(row == 4, total, found).astype(jnp.int32)
    most_ref[...] = jnp.broadcast_to(jnp.max(most, axis=0, keepdims=True), most_ref.shape).astype(jnp.int32)


def make_plan(every, groups, owners, per_owner, count, nst):
    n = groups * count
    return pl.pallas_call(
        functools.partial(plan_kernel, groups, owners, per_owner, count),
        out_shape=[
            jax.ShapeDtypeStruct((2 * n, nst), jnp.bfloat16),
            jax.ShapeDtypeStruct((8, n), jnp.float32),
            jax.ShapeDtypeStruct((owners, 8, LANES), jnp.int32),
            jax.ShapeDtypeStruct((8, LANES), jnp.int32),
        ],
        compiler_params=pltpu.CompilerParams(vmem_limit_bytes=VMEM_LIMIT),
        cost_estimate=pl.CostEstimate(flops=1 << 30, bytes_accessed=1 << 20, transcendentals=0),
        name="plan",
    )(every)


def aterm_kernel(ncorr, owners, rows_of, scale, groups, *refs):
    image_refs, refs = refs[:-8], refs[-8:]
    screen_ref, pick_ref, order_ref, out_ref, block_ref, jones_ref, held, sems = refs
    n = order_ref.shape[1]
    count = n // groups
    me = lax.axis_index("corr")
    step = pl.program_id(0)
    copies = [
        pltpu.make_async_copy(screen_ref.at[:, h * held.shape[2] : (h + 1) * held.shape[2]], held.at[h], sems.at[h])
        for h in range(held.shape[0])
    ]
    for h, copy in enumerate(copies):
        pl.when(step == 0)(copy.start)
    for h, copy in enumerate(copies):
        pl.when(step == h)(copy.wait)
    jones_ref[...] = jnp.dot(pick_ref[...], held[step], preferred_element_type=jnp.float32)
    pixel = lax.broadcasted_iota(jnp.int32, (1, LANES), 1) + (me * pl.num_programs(0) + pl.program_id(0)) * LANES
    row_at = ((pixel // SUB).astype(jnp.float32) - (SUB - 1) / 2.0) * (2.0 / SUB)
    col_at = ((pixel % SUB).astype(jnp.float32) - (SUB - 1) / 2.0) * (2.0 / SUB)
    taper = (1.0 - 0.8 * row_at * row_at) * (1.0 - 0.8 * col_at * col_at) * scale
    chunk = 16

    def part(ref, rows, field):
        return ref[rows, field * LANES : (field + 1) * LANES].astype(jnp.float32)

    def body(ref, d, begin, i, carry):
        held = pl.ds(pl.multiple_of(i * chunk, chunk), chunk)
        at = (me ^ d) * count + begin + i * chunk
        rows = pl.ds(pl.multiple_of(at, chunk), chunk)
        far_rows = pl.ds(pl.multiple_of(at + n, chunk), chunk)
        image_re = [part(ref, held, e) for e in range(ncorr)]
        image_im = [part(ref, held, ncorr + e) for e in range(ncorr)]
        for row_out in range(2):
            mid_re = []
            mid_im = []
            for inner in range(2):
                m_re = 0.0
                m_im = 0.0
                for first in range(2):
                    near_re = part(jones_ref, rows, 2 * first + row_out)
                    near_im = part(jones_ref, rows, ncorr + 2 * first + row_out)
                    vis_re = image_re[2 * first + inner]
                    vis_im = image_im[2 * first + inner]
                    m_re = m_re + near_re * vis_re + near_im * vis_im
                    m_im = m_im + near_re * vis_im - near_im * vis_re
                mid_re.append(m_re)
                mid_im.append(m_im)
            for col_out in range(2):
                t_re = 0.0
                t_im = 0.0
                for inner in range(2):
                    far_re = part(jones_ref, far_rows, 2 * inner + col_out)
                    far_im = part(jones_ref, far_rows, ncorr + 2 * inner + col_out)
                    t_re = t_re + mid_re[inner] * far_re - mid_im[inner] * far_im
                    t_im = t_im + mid_re[inner] * far_im + mid_im[inner] * far_re
                place = 2 * (2 * row_out + col_out) * LANES
                block_ref[rows, place : place + LANES] = (t_re * taper).astype(jnp.bfloat16)
                block_ref[rows, place + LANES : place + 2 * LANES] = (t_im * taper).astype(jnp.bfloat16)
        return carry

    for p, ref in enumerate(image_refs):
        begin = sum(other.shape[0] for other in image_refs[p % groups : p : groups])
        lax.fori_loop(0, ref.shape[0] // chunk, functools.partial(body, ref, p % groups, begin), 0)
    target = order_ref[0:1, :] * float(rows_of) + order_ref[1:2, :]
    row = lax.broadcasted_iota(jnp.int32, (owners * rows_of, n), 0).astype(jnp.float32)
    move = (row == target).astype(jnp.float32).astype(jnp.bfloat16)
    for e in range(ncorr):
        block = block_ref[:, 2 * e * LANES : 2 * (e + 1) * LANES]
        out_ref[e] = jnp.dot(move, block, preferred_element_type=jnp.float32).astype(jnp.bfloat16)


def apply_aterms(images, groups, screens, pick, order, scale, ncorr, owners, rows):
    n = order.shape[1]
    nst = screens.shape[0]
    half = 2 * ncorr * LANES
    halves = screens.shape[1] // half
    return pl.pallas_call(
        functools.partial(aterm_kernel, ncorr, owners, rows, scale, groups),
        grid=(halves,),
        in_specs=[pl.BlockSpec((image.shape[0], half), lambda h: (0, h)) for image in images]
        + [
            pl.BlockSpec(memory_space=pltpu.HBM),
            pl.BlockSpec(pick.shape, lambda h: (0, 0)),
            pl.BlockSpec(order.shape, lambda h: (0, 0)),
        ],
        out_specs=pl.BlockSpec((ncorr, owners * rows, 2 * LANES), lambda h: (0, 0, h)),
        out_shape=jax.ShapeDtypeStruct((ncorr, owners * rows, halves * 2 * LANES), jnp.bfloat16),
        scratch_shapes=[
            pltpu.VMEM((n, half), jnp.bfloat16),
            pltpu.VMEM((2 * n, half), jnp.float32),
            pltpu.VMEM((halves, nst, half), jnp.bfloat16),
            pltpu.SemaphoreType.DMA((halves,)),
        ],
        compiler_params=pltpu.CompilerParams(vmem_limit_bytes=VMEM_LIMIT),
        cost_estimate=pl.CostEstimate(flops=6 << 30, bytes_accessed=8 << 20, transcendentals=0),
        name="aterms",
    )(*images, screens, pick, order)


def grid_kernel(rows, place_ref, block_ref, col_ref, row_ref, out_ref, half_ref, uv_ref, turned_a, turned_b, re_a, im_a, re_b, im_b):
    groups, total, depth = block_ref.shape
    sources = total // rows
    per_slot = 2 * PIX // LANES + 1
    quarters = depth // LANES
    low = lax.broadcasted_iota(jnp.int32, (total, LANES), 1) < LANES // 2
    for c in range(groups):
        tiles = []
        for h in range(2):
            block = block_ref[c, :, 2 * h * LANES : 2 * (h + 1) * LANES]
            tiles.append(jnp.dot(block, col_ref[...], preferred_element_type=jnp.float32))
        for j in range(2):
            one, two = [tile[:, j * LANES : (j + 1) * LANES] for tile in tiles]
            first = jnp.where(low, one, pltpu.roll(two, LANES // 2, 1))
            second = jnp.where(low, pltpu.roll(one, LANES // 2, 1), two)
            half_ref[c, :, 2 * j * LANES : (2 * j + 1) * LANES] = first.astype(jnp.bfloat16)
            half_ref[c, :, (2 * j + 1) * LANES : (2 * j + 2) * LANES] = second.astype(jnp.bfloat16)
    for q in range(quarters):
        left = jnp.concatenate([half_ref[g, :, q * LANES : (q + 1) * LANES] for g in range(groups)], axis=1)
        uv = jnp.dot(left, row_ref[...], preferred_element_type=jnp.float32)
        for part in range(2):
            for i in range(2):
                j = part * 2 + i
                uv_ref[pl.ds(part * 8 + 2 * q + i, total, stride=per_slot), :] = uv[:, j * LANES : (j + 1) * LANES]
    for ref in (re_a, im_a, re_b, im_b):
        ref[...] = jnp.zeros_like(ref)

    lane = lax.broadcasted_iota(jnp.int32, (8, LANES), 1)
    pieces = LANES // SUB
    tall = 2 * pieces * 8
    batch = 8
    longest = place_ref[0, 4, 0]
    for t in range(1, sources):
        longest = jnp.maximum(longest, place_ref[t, 4, 0])
    trips = (longest + (batch - 1)) // batch
    turned = (turned_a, turned_b)

    def turn(t, i):
        for b in range(batch):
            j = i * batch + b
            y = place_ref[t, 1, j]
            inside = (lane >= y) & (lane < y + SUB)
            for part in range(2):
                at = (t * rows + j) * per_slot + part * 8
                block = uv_ref[pl.ds(at, 8), :]
                for g in range(pieces):
                    moved = pltpu.roll(block, (y + (LANES - g * SUB)) & (LANES - 1), 1)
                    at = pl.multiple_of(j * tall + (part * pieces + g) * 8, 8)
                    turned[t % 2][pl.ds(at, 8), :] = jnp.where(inside, moved, 0.0)

    def add(t, i):
        for b in range(batch):
            j = i * batch + b
            row = place_ref[t, 2, j] * TILE_SIDE + place_ref[t, 0, j]
            for part, ref in enumerate((re_a, im_a) if b % 2 == 0 else (re_b, im_b)):
                at = pl.multiple_of(j * tall + part * pieces * 8, 8)
                ref[pl.ds(row, SUB), :] = ref[pl.ds(row, SUB), :] + turned[t % 2][pl.ds(at, SUB), :]

    for t in range(sources + 1):

        def both(i, carry):
            if t < sources:
                turn(t, i)
            if t > 0:
                add(t - 1, i)
            return carry

        lax.fori_loop(0, trips, both, 0)

    for k in range(out_ref.shape[0]):
        span = slice(k * TILE_SIDE, (k + 1) * TILE_SIDE)
        for part, (one, two) in enumerate(((re_a, re_b), (im_a, im_b))):
            out_ref[k, part] = one[span, :] + two[span, :]


def place_on_grid(places, blocks, rows, tables, per_owner):
    groups, total, depth = blocks.shape
    whole = pl.BlockSpec(memory_space=pltpu.VMEM)
    accumulator = pltpu.VMEM((per_owner * TILE_SIDE, TILE_SIDE), jnp.float32)
    return pl.pallas_call(
        functools.partial(grid_kernel, rows),
        in_specs=[pl.BlockSpec(memory_space=pltpu.SMEM), whole, whole, whole],
        out_specs=whole,
        out_shape=jax.ShapeDtypeStruct((per_owner, 2, TILE_SIDE, TILE_SIDE), jnp.float32),
        scratch_shapes=[
            pltpu.VMEM((groups, total, depth), jnp.bfloat16),
            pltpu.VMEM((total * (2 * PIX // LANES + 1), LANES), jnp.float32),
            pltpu.VMEM((rows * 2 * PIX // SUB, LANES), jnp.float32),
            pltpu.VMEM((rows * 2 * PIX // SUB, LANES), jnp.float32),
            accumulator,
            accumulator,
            accumulator,
            accumulator,
        ],
        compiler_params=pltpu.CompilerParams(vmem_limit_bytes=VMEM_LIMIT),
        name="grid",
    )(places, blocks, *tables)


def uv_tables(groups):
    quad = LANES // SUB
    halves = SUB // (groups * quad)
    index = np.arange(SUB) - SUB // 2
    factor = np.exp(-2j * np.pi / SUB * ((index[:, None] * index[None, :]) % SUB))

    def parts(table, axis):
        upper = np.stack([table.real, table.imag], axis=axis)
        lower = np.stack([-table.imag, table.real], axis=axis)
        return upper, lower

    col = (factor / SUB).reshape(SUB, 4, 4, 2).transpose(2, 0, 3, 1)
    first = np.zeros((2, quad, SUB, 4, 2, quad, 2, 4))
    for p, table in enumerate(parts(col, 0)):
        for r in range(quad):
            first[p, r, :, :, :, r] = table.transpose(2, 1, 0, 3, 4)
    second = np.zeros((groups, halves, 2, quad, 2, 4, 2, 2, 4, SUB))
    row = factor.reshape(groups, halves, quad, SUB)
    for p, table in enumerate(parts(row, 0)):
        for i in range(2):
            for g in range(4):
                second[:, :, p, :, i, g, :, i, g, :] = table.transpose(1, 2, 3, 0, 4)
    first = first.reshape(2 * LANES, 2 * LANES)
    second = second.reshape(groups * halves * 2 * quad * 8, 4 * LANES)
    return first.astype(jnp.bfloat16), second.astype(jnp.bfloat16)


def per_device(visibilities, coords, stations, tile_ids, offsets, screens):
    count, fields, nvis = visibilities.shape
    ncorr = fields // 2
    groups = lax.axis_size("corr")
    owners = lax.axis_size("tile")
    corr = lax.axis_index("corr")
    tile = lax.axis_index("tile")
    per_owner = NT // owners
    full = per_owner * groups * (2 * count // NT)
    halves = PIX // (groups * LANES)
    local = PIX // groups

    part = own_pixels(screens, groups)
    all_screens = lax.all_gather(part, "tile", axis=0, tiled=True)

    facts = jnp.concatenate([tile_ids.T, offsets.T, stations.T], axis=0)
    facts = jnp.pad(facts, ((0, 8 - facts.shape[0]), (0, LANES - count)))
    every = jnp.broadcast_to(facts[None], (groups * owners, 8, LANES))
    every = lax.all_to_all(every, ("corr", "tile"), split_axis=0, concat_axis=0, tiled=True)

    images = []
    for first, size in ((0, count * 3 // 4), (count * 3 // 4, count // 4)):
        for d, piece in enumerate(make_images(visibilities, coords, groups, first, size)):
            if first and d == groups - 1:
                images[1], piece = lax.optimization_barrier((images[1], piece))
            images.append(lax.ppermute(piece, "corr", [(i, i ^ d) for i in range(groups)]) if d else piece)
    pick, order, places, most = make_plan(every, groups, owners, per_owner, count, all_screens.shape[0])

    tables = tuple(jnp.asarray(table) for table in uv_tables(groups))

    def finish(rows, images, screens, pick, order, places):
        sending = apply_aterms(images, groups, screens, pick, order, 1.0 / nvis, ncorr, owners, rows)
        received = lax.all_to_all(
            sending.reshape(groups * owners, rows, 2 * local), ("corr", "tile"), split_axis=0, concat_axis=0, tiled=True
        )
        return place_on_grid(places, received.reshape(groups, owners * rows, 2 * local), rows, tables, per_owner)

    heights = sorted({min(full, -(-full * share // 64) * 8) for share in (5, 6, 8)})
    branches = [functools.partial(finish, rows) for rows in heights]
    if len(heights) == 1:
        grid = branches[0](images, all_screens, pick, order, places)
    else:
        index = sum((most[0, 0] > rows).astype(jnp.int32) for rows in heights[:-1])
        grid = lax.switch(index, branches, images, all_screens, pick, order, places)
    return grid[None]


def solution(mesh):
    return jax.shard_map(
        per_device,
        mesh=mesh,
        in_specs=(
            P(("corr", "tile"), None, None),
            P(("corr", "tile"), None, None),
            P(("corr", "tile"), None),
            P(("corr", "tile"), None),
            P(("corr", "tile"), None),
            P("tile", None, None),
        ),
        out_specs=P("corr", "tile", None, None, None),
        check_vma=False,
    )
```

```python
import functools
import math

import jax
import jax.numpy as jnp
import numpy as np
from jax import lax
from jax.experimental import pallas as pl
from jax.experimental.pallas import tpu as pltpu
from jax.sharding import PartitionSpec as P

SUB = 32
NT = 64
TILE_SIDE = 128
PIX = SUB * SUB
LANES = 128
VMEM_LIMIT = 36 * 1024 * 1024
VMEM_ALL = 63 * 1024 * 1024 + 512 * 1024

ROOT2 = math.sqrt(2.0)


def half_turn_series():
    grid = np.cos(np.pi * (np.arange(400) + 0.5) / 800.0) * 0.5
    z = grid * grid
    sine = np.polynomial.polynomial.Polynomial.fit(z, np.sin(np.pi * grid) / grid, 3, domain=[0, 0.25], window=[0, 0.25]).coef
    cosine = np.polynomial.polynomial.Polynomial.fit(z, np.cos(np.pi * grid), 3, domain=[0, 0.25], window=[0, 0.25]).coef
    return [float(x) * ROOT2 for x in sine], [float(x) * ROOT2 for x in cosine]


SINE, COSINE = half_turn_series()


def horner(coefficients, z):
    total = coefficients[-1]
    for value in coefficients[-2::-1]:
        total = total * z + value
    return total


def cis_turns(turns):
    t = turns - jnp.round(turns)
    z = t * t
    s = t * horner(SINE, z)
    c = horner(COSINE, z)
    return 1.0 - s * s, s * c


def image_kernel(ncorr, groups, vis_ref, coord_ref, *refs):
    out_refs, square = refs[:-1], refs[-1]
    me = lax.axis_index("corr")
    step = vis_ref.shape[0]
    nvis = vis_ref.shape[2]
    centred = (lax.broadcasted_iota(jnp.int32, (SUB, nvis), 0) - SUB // 2).astype(jnp.float32) * (1.0 / SUB)
    bend = 0.5 * centred * centred
    rows = ncorr * SUB
    pitch = rows + 1

    def one(s):
        u = coord_ref[0, pl.ds(s, 1), :]
        v = coord_ref[1, pl.ds(s, 1), :]
        w = coord_ref[2, pl.ds(s, 1), :]
        sag = w * bend
        e_re, e_im = cis_turns(u * centred - sag)
        f_re, f_im = cis_turns(v * centred - sag)
        vis = vis_ref[s].astype(jnp.float32)
        g_re = []
        g_im = []
        for e in range(ncorr):
            vr = vis[e : e + 1]
            vi = vis[ncorr + e : ncorr + e + 1]
            g_re.append((vr * e_re - vi * e_im).astype(jnp.bfloat16))
            g_im.append((vr * e_im + vi * e_re).astype(jnp.bfloat16))
        left = jnp.concatenate([jnp.concatenate(g_re, axis=0), jnp.concatenate(g_im, axis=0)], axis=1)
        f_re = f_re.astype(jnp.bfloat16)
        f_im = f_im.astype(jnp.bfloat16)
        right = jnp.concatenate(
            [jnp.concatenate([f_re, f_im], axis=0), jnp.concatenate([-f_im, f_re], axis=0)], axis=1
        )
        image = lax.dot_general(left, right, (((1,), (1,)), ((), ())), preferred_element_type=jnp.float32)
        square[pl.ds(s * pitch, rows), 0 : 2 * SUB] = image

    def several(i, carry):
        for j in range(4):
            one(i * 4 + j)
        return carry

    lax.fori_loop(0, step // 4, several, 0)

    lane = lax.broadcasted_iota(jnp.int32, (step, LANES), 1)
    per_tile = LANES // SUB
    halves = SUB // groups // per_tile
    for d in range(groups):
        first = (me ^ d) * (halves * per_tile)
        for h in range(halves):
            for e in range(ncorr):
                real = None
                imag = None
                for j in range(per_tile):
                    piece = square[pl.ds(first + (e * SUB + h * per_tile + j), step, stride=pitch), :]
                    a = piece if j == 0 else pltpu.roll(piece, SUB * j, 1)
                    b = piece if j == 1 else pltpu.roll(piece, (SUB * (j - 1)) % LANES, 1)
                    keep = lane < SUB * (j + 1)
                    real = a if real is None else jnp.where(lane < SUB * j, real, a)
                    imag = b if imag is None else jnp.where(lane < SUB * j, imag, b)
                base = h * 2 * ncorr * LANES
                out_refs[d][:, base + e * LANES : base + (e + 1) * LANES] = real.astype(jnp.bfloat16)
                out_refs[d][:, base + (ncorr + e) * LANES : base + (ncorr + e + 1) * LANES] = imag.astype(jnp.bfloat16)


def make_images(visibilities, coords, groups, first, size):
    count, fields, nvis = visibilities.shape
    ncorr = fields // 2
    step = 16
    width = fields * PIX // groups
    return pl.pallas_call(
        functools.partial(image_kernel, ncorr, groups),
        grid=(size // step,),
        in_specs=[
            pl.BlockSpec((step, fields, nvis), lambda i: (i + first // step, 0, 0)),
            pl.BlockSpec((3, step, nvis), lambda i: (0, i + first // step, 0)),
        ],
        out_specs=[pl.BlockSpec((step, width), lambda i: (i, 0))] * groups,
        out_shape=[jax.ShapeDtypeStruct((size, width), jnp.bfloat16)] * groups,
        scratch_shapes=[pltpu.VMEM((step * (ncorr * SUB + 1), LANES), jnp.float32)],
        compiler_params=pltpu.CompilerParams(vmem_limit_bytes=VMEM_LIMIT),
        cost_estimate=pl.CostEstimate(flops=size << 27, bytes_accessed=2 << 20, transcendentals=0),
        name="images",
    )(visibilities, jnp.transpose(coords, (1, 0, 2)))


def pixels_kernel(screen_ref, out_ref, held, rows_ref, sem):
    stations, fields, local = held.shape
    me = lax.axis_index("corr")
    copy = pltpu.make_async_copy(screen_ref.at[:, :, pl.ds(pl.multiple_of(me * local, local), local)], held, sem)
    copy.start()
    copy.wait()
    pitch = fields + 1
    halves = local // LANES
    for s in range(stations):
        station = held[s].astype(jnp.float32)
        for h in range(halves):
            rows_ref[h, s * pitch : s * pitch + fields, :] = station[:, h * LANES : (h + 1) * LANES]
    for h in range(halves):
        for f in range(fields):
            at = (h * fields + f) * LANES
            out_ref[:, at : at + LANES] = rows_ref[h, pl.ds(f, stations, stride=pitch), :].astype(jnp.bfloat16)


def own_pixels(screens, groups):
    stations, fields, pixels = screens.shape
    local = pixels // groups
    return pl.pallas_call(
        pixels_kernel,
        in_specs=[pl.BlockSpec(memory_space=pl.ANY)],
        out_specs=pl.BlockSpec(memory_space=pltpu.VMEM),
        out_shape=jax.ShapeDtypeStruct((stations, fields * local), jnp.bfloat16),
        scratch_shapes=[
            pltpu.VMEM((stations, fields, local), jnp.bfloat16),
            pltpu.VMEM((local // LANES, stations * (fields + 1), LANES), jnp.float32),
            pltpu.SemaphoreType.DMA(()),
        ],
        compiler_params=pltpu.CompilerParams(vmem_limit_bytes=VMEM_ALL),
        name="pixels",
    )(screens)


def plan_kernel(groups, owners, per_owner, count, every_ref, pick_ref, order_ref, place_ref, most_ref):
    nst = pick_ref.shape[1]
    n = groups * count
    together = LANES // count
    me = lax.axis_index("tile")
    lane = lax.broadcasted_iota(jnp.int32, (8, LANES), 1)
    number = lax.broadcasted_iota(jnp.int32, (count, nst), 1).astype(jnp.float32)
    before = lax.broadcasted_iota(jnp.int32, (n, n), 0) < lax.broadcasted_iota(jnp.int32, (n, n), 1)
    before = before.astype(jnp.float32).astype(jnp.bfloat16)
    owner_row = lax.broadcasted_iota(jnp.int32, (owners, n), 0).astype(jnp.float32)
    slot = lax.broadcasted_iota(jnp.int32, (LANES, n), 0).astype(jnp.float32)
    row = lax.broadcasted_iota(jnp.int32, (8, LANES), 0)

    def group(t):
        tiles = []
        for g in range(0, groups, together):
            joined = None
            for k in range(together):
                facts = every_ref[(g + k) * owners + t].astype(jnp.float32)
                facts = facts if k == 0 else pltpu.roll(facts, k * count, 1)
                joined = facts if k == 0 else jnp.where(lane < k * count, joined, facts)
            tiles.append(joined)
        return jnp.concatenate(tiles, axis=1)

    def ranks(facts):
        owner = jnp.floor(facts[0:1] * (1.0 / per_owner))
        hot = (owner_row == owner).astype(jnp.float32)
        ahead = jnp.dot(hot.astype(jnp.bfloat16), before, preferred_element_type=jnp.float32)
        return owner, jnp.sum(hot * ahead, axis=0, keepdims=True), jnp.sum(hot, axis=1, keepdims=True)

    for g in range(groups):
        columns = jnp.transpose(every_ref[g * owners + me].astype(jnp.float32))
        for which in range(2):
            at = which * n + g * count
            station = columns[:count, 3 + which : 4 + which]
            pick_ref[at : at + count, :] = (number == station).astype(jnp.float32).astype(jnp.bfloat16)
    owner, rank, held = ranks(group(me))
    order_ref[0:1, :] = owner
    order_ref[1:2, :] = rank

    most = jnp.zeros((owners, 1), jnp.float32)
    for t in range(owners):
        facts = group(t)
        owner, rank, held = ranks(facts)
        most = jnp.maximum(most, held)
        here = jnp.where(owner == me.astype(jnp.float32), 1.0, 0.0)
        hit = jnp.where(slot == jnp.where(here > 0.0, rank, -1.0), 1.0, 0.0).astype(jnp.bfloat16)
        local = facts[0:1] - owner * per_owner
        values = jnp.concatenate([facts[1:3], local, jnp.zeros((5, n), jnp.float32)], axis=0).astype(jnp.bfloat16)
        found = lax.dot_general(values, hit, (((1,), (1,)), ((), ())), preferred_element_type=jnp.float32)
        total = jnp.sum(here, axis=1, keepdims=True)
        place_ref[t] = jnp.where(row == 4, total, found).astype(jnp.int32)
    most_ref[...] = jnp.broadcast_to(jnp.max(most, axis=0, keepdims=True), most_ref.shape).astype(jnp.int32)


def make_plan(every, groups, owners, per_owner, count, nst):
    n = groups * count
    return pl.pallas_call(
        functools.partial(plan_kernel, groups, owners, per_owner, count),
        out_shape=[
            jax.ShapeDtypeStruct((2 * n, nst), jnp.bfloat16),
            jax.ShapeDtypeStruct((8, n), jnp.float32),
            jax.ShapeDtypeStruct((owners, 8, LANES), jnp.int32),
            jax.ShapeDtypeStruct((8, LANES), jnp.int32),
        ],
        compiler_params=pltpu.CompilerParams(vmem_limit_bytes=VMEM_LIMIT),
        cost_estimate=pl.CostEstimate(flops=1 << 30, bytes_accessed=1 << 20, transcendentals=0),
        name="plan",
    )(every)


def aterm_kernel(ncorr, owners, rows_of, scale, groups, *refs):
    image_refs, refs = refs[:-8], refs[-8:]
    screen_ref, pick_ref, order_ref, out_ref, block_ref, jones_ref, held, sems = refs
    n = order_ref.shape[1]
    count = n // groups
    me = lax.axis_index("corr")
    step = pl.program_id(0)
    copies = [
        pltpu.make_async_copy(screen_ref.at[:, h * held.shape[2] : (h + 1) * held.shape[2]], held.at[h], sems.at[h])
        for h in range(held.shape[0])
    ]
    for h, copy in enumerate(copies):
        pl.when(step == 0)(copy.start)
    for h, copy in enumerate(copies):
        pl.when(step == h)(copy.wait)
    jones_ref[...] = jnp.dot(pick_ref[...], held[step], preferred_element_type=jnp.float32)
    pixel = lax.broadcasted_iota(jnp.int32, (1, LANES), 1) + (me * pl.num_programs(0) + pl.program_id(0)) * LANES
    row_at = ((pixel // SUB).astype(jnp.float32) - (SUB - 1) / 2.0) * (2.0 / SUB)
    col_at = ((pixel % SUB).astype(jnp.float32) - (SUB - 1) / 2.0) * (2.0 / SUB)
    taper = (1.0 - 0.8 * row_at * row_at) * (1.0 - 0.8 * col_at * col_at) * scale
    chunk = 16

    def part(ref, rows, field):
        return ref[rows, field * LANES : (field + 1) * LANES].astype(jnp.float32)

    def body(ref, d, begin, i, carry):
        held = pl.ds(pl.multiple_of(i * chunk, chunk), chunk)
        at = (me ^ d) * count + begin + i * chunk
        rows = pl.ds(pl.multiple_of(at, chunk), chunk)
        far_rows = pl.ds(pl.multiple_of(at + n, chunk), chunk)
        image_re = [part(ref, held, e) for e in range(ncorr)]
        image_im = [part(ref, held, ncorr + e) for e in range(ncorr)]
        for row_out in range(2):
            mid_re = []
            mid_im = []
            for inner in range(2):
                m_re = 0.0
                m_im = 0.0
                for first in range(2):
                    near_re = part(jones_ref, rows, 2 * first + row_out)
                    near_im = part(jones_ref, rows, ncorr + 2 * first + row_out)
                    vis_re = image_re[2 * first + inner]
                    vis_im = image_im[2 * first + inner]
                    m_re = m_re + near_re * vis_re + near_im * vis_im
                    m_im = m_im + near_re * vis_im - near_im * vis_re
                mid_re.append(m_re)
                mid_im.append(m_im)
            for col_out in range(2):
                t_re = 0.0
                t_im = 0.0
                for inner in range(2):
                    far_re = part(jones_ref, far_rows, 2 * inner + col_out)
                    far_im = part(jones_ref, far_rows, ncorr + 2 * inner + col_out)
                    t_re = t_re + mid_re[inner] * far_re - mid_im[inner] * far_im
                    t_im = t_im + mid_re[inner] * far_im + mid_im[inner] * far_re
                place = 2 * (2 * row_out + col_out) * LANES
                block_ref[rows, place : place + LANES] = (t_re * taper).astype(jnp.bfloat16)
                block_ref[rows, place + LANES : place + 2 * LANES] = (t_im * taper).astype(jnp.bfloat16)
        return carry

    for p, ref in enumerate(image_refs):
        begin = sum(other.shape[0] for other in image_refs[p % groups : p : groups])
        lax.fori_loop(0, ref.shape[0] // chunk, functools.partial(body, ref, p % groups, begin), 0)
    target = order_ref[0:1, :] * float(rows_of) + order_ref[1:2, :]
    row = lax.broadcasted_iota(jnp.int32, (owners * rows_of, n), 0).astype(jnp.float32)
    move = (row == target).astype(jnp.float32).astype(jnp.bfloat16)
    for e in range(ncorr):
        block = block_ref[:, 2 * e * LANES : 2 * (e + 1) * LANES]
        out_ref[e] = jnp.dot(move, block, preferred_element_type=jnp.float32).astype(jnp.bfloat16)


def apply_aterms(images, groups, screens, pick, order, scale, ncorr, owners, rows):
    n = order.shape[1]
    nst = screens.shape[0]
    half = 2 * ncorr * LANES
    halves = screens.shape[1] // half
    return pl.pallas_call(
        functools.partial(aterm_kernel, ncorr, owners, rows, scale, groups),
        grid=(halves,),
        in_specs=[pl.BlockSpec((image.shape[0], half), lambda h: (0, h)) for image in images]
        + [
            pl.BlockSpec(memory_space=pltpu.HBM),
            pl.BlockSpec(pick.shape, lambda h: (0, 0)),
            pl.BlockSpec(order.shape, lambda h: (0, 0)),
        ],
        out_specs=pl.BlockSpec((ncorr, owners * rows, 2 * LANES), lambda h: (0, 0, h)),
        out_shape=jax.ShapeDtypeStruct((ncorr, owners * rows, halves * 2 * LANES), jnp.bfloat16),
        scratch_shapes=[
            pltpu.VMEM((n, half), jnp.bfloat16),
            pltpu.VMEM((2 * n, half), jnp.float32),
            pltpu.VMEM((halves, nst, half), jnp.bfloat16),
            pltpu.SemaphoreType.DMA((halves,)),
        ],
        compiler_params=pltpu.CompilerParams(vmem_limit_bytes=VMEM_LIMIT),
        cost_estimate=pl.CostEstimate(flops=6 << 30, bytes_accessed=8 << 20, transcendentals=0),
        name="aterms",
    )(*images, screens, pick, order)


def grid_kernel(rows, place_ref, block_ref, col_ref, row_ref, out_ref, half_ref, uv_ref, *sums):
    groups, total, depth = block_ref.shape
    sources = total // rows
    per_slot = 2 * PIX // LANES + 1
    quarters = depth // LANES
    low = lax.broadcasted_iota(jnp.int32, (total, LANES), 1) < LANES // 2
    for c in range(groups):
        tiles = []
        for h in range(2):
            block = block_ref[c, :, 2 * h * LANES : 2 * (h + 1) * LANES]
            tiles.append(jnp.dot(block, col_ref[...], preferred_element_type=jnp.float32))
        for j in range(2):
            one, two = [tile[:, j * LANES : (j + 1) * LANES] for tile in tiles]
            first = jnp.where(low, one, pltpu.roll(two, LANES // 2, 1))
            second = jnp.where(low, pltpu.roll(one, LANES // 2, 1), two)
            half_ref[c, :, 2 * j * LANES : (2 * j + 1) * LANES] = first.astype(jnp.bfloat16)
            half_ref[c, :, (2 * j + 1) * LANES : (2 * j + 2) * LANES] = second.astype(jnp.bfloat16)
    for q in range(quarters):
        left = jnp.concatenate([half_ref[g, :, q * LANES : (q + 1) * LANES] for g in range(groups)], axis=1)
        uv = jnp.dot(left, row_ref[...], preferred_element_type=jnp.float32)
        for part in range(2):
            for i in range(2):
                j = part * 2 + i
                uv_ref[pl.ds(part * 8 + 2 * q + i, total, stride=per_slot), :] = uv[:, j * LANES : (j + 1) * LANES]
    for ref in sums:
        ref[...] = jnp.zeros_like(ref)

    lane = lax.broadcasted_iota(jnp.int32, (8, LANES), 1)
    pieces = LANES // SUB
    batch = 8
    for t in range(sources):

        def add(i, carry):
            for b in range(batch):
                j = i * batch + b
                y = place_ref[t, 1, j]
                row = place_ref[t, 2, j] * TILE_SIDE + place_ref[t, 0, j]
                band = lax.shift_right_logical((lane - y) & (LANES - 1), SUB.bit_length() - 1)
                for part in range(2):
                    at = (t * rows + j) * per_slot + part * 8
                    turned = pltpu.roll(uv_ref[pl.ds(at, 8), :], y, 1)
                    for g in range(pieces):
                        ref = sums[part * pieces + g]
                        span = pl.ds(row + 8 * g, 8)
                        ref[span, :] = ref[span, :] + jnp.where(band == g, turned, 0.0)
            return carry

        lax.fori_loop(0, (place_ref[t, 4, 0] + (batch - 1)) // batch, add, 0)

    for k in range(out_ref.shape[0]):
        span = slice(k * TILE_SIDE, (k + 1) * TILE_SIDE)
        for part in range(2):
            total_here = sums[part * pieces][span, :]
            for g in range(1, pieces):
                total_here = total_here + pltpu.roll(sums[part * pieces + g][span, :], LANES - g * SUB, 1)
            out_ref[k, part] = total_here


def place_on_grid(places, blocks, rows, tables, per_owner):
    groups, total, depth = blocks.shape
    whole = pl.BlockSpec(memory_space=pltpu.VMEM)
    accumulator = pltpu.VMEM((per_owner * TILE_SIDE, TILE_SIDE), jnp.float32)
    return pl.pallas_call(
        functools.partial(grid_kernel, rows),
        in_specs=[pl.BlockSpec(memory_space=pltpu.SMEM), whole, whole, whole],
        out_specs=whole,
        out_shape=jax.ShapeDtypeStruct((per_owner, 2, TILE_SIDE, TILE_SIDE), jnp.float32),
        scratch_shapes=[
            pltpu.VMEM((groups, total, depth), jnp.bfloat16),
            pltpu.VMEM((total * (2 * PIX // LANES + 1), LANES), jnp.float32),
        ]
        + [accumulator] * (2 * LANES // SUB),
        compiler_params=pltpu.CompilerParams(vmem_limit_bytes=VMEM_LIMIT),
        name="grid",
    )(places, blocks, *tables)


def uv_tables(groups):
    quad = LANES // SUB
    halves = SUB // (groups * quad)
    index = np.arange(SUB) - SUB // 2
    factor = np.exp(-2j * np.pi / SUB * ((index[:, None] * index[None, :]) % SUB))

    def parts(table, axis):
        upper = np.stack([table.real, table.imag], axis=axis)
        lower = np.stack([-table.imag, table.real], axis=axis)
        return upper, lower

    col = (factor / SUB).reshape(SUB, 4, 4, 2).transpose(2, 0, 3, 1)
    first = np.zeros((2, quad, SUB, 4, 2, quad, 2, 4))
    for p, table in enumerate(parts(col, 0)):
        for r in range(quad):
            first[p, r, :, :, :, r] = table.transpose(2, 1, 0, 3, 4)
    second = np.zeros((groups, halves, 2, quad, 2, 4, 2, 2, 4, SUB))
    row = factor.reshape(groups, halves, quad, SUB)
    for p, table in enumerate(parts(row, 0)):
        for i in range(2):
            for g in range(4):
                second[:, :, p, :, i, g, :, i, g, :] = table.transpose(1, 2, 3, 0, 4)
    first = first.reshape(2 * LANES, 2 * LANES)
    second = second.reshape(groups * halves * 2 * quad * 8, 4 * LANES)
    return first.astype(jnp.bfloat16), second.astype(jnp.bfloat16)


def per_device(visibilities, coords, stations, tile_ids, offsets, screens):
    count, fields, nvis = visibilities.shape
    ncorr = fields // 2
    groups = lax.axis_size("corr")
    owners = lax.axis_size("tile")
    corr = lax.axis_index("corr")
    tile = lax.axis_index("tile")
    per_owner = NT // owners
    full = per_owner * groups * (2 * count // NT)
    halves = PIX // (groups * LANES)
    local = PIX // groups

    part = own_pixels(screens, groups)
    all_screens = lax.all_gather(part, "tile", axis=0, tiled=True)

    facts = jnp.concatenate([tile_ids.T, offsets.T, stations.T], axis=0)
    facts = jnp.pad(facts, ((0, 8 - facts.shape[0]), (0, LANES - count)))
    every = jnp.broadcast_to(facts[None], (groups * owners, 8, LANES))
    every = lax.all_to_all(every, ("corr", "tile"), split_axis=0, concat_axis=0, tiled=True)

    images = []
    for first, size in ((0, count * 3 // 4), (count * 3 // 4, count // 4)):
        for d, piece in enumerate(make_images(visibilities, coords, groups, first, size)):
            if first and d == groups - 1:
                images[1], piece = lax.optimization_barrier((images[1], piece))
            images.append(lax.ppermute(piece, "corr", [(i, i ^ d) for i in range(groups)]) if d else piece)
    pick, order, places, most = make_plan(every, groups, owners, per_owner, count, all_screens.shape[0])

    tables = tuple(jnp.asarray(table) for table in uv_tables(groups))

    def finish(rows, images, screens, pick, order, places):
        sending = apply_aterms(images, groups, screens, pick, order, 1.0 / nvis, ncorr, owners, rows)
        received = lax.all_to_all(
            sending.reshape(groups * owners, rows, 2 * local), ("corr", "tile"), split_axis=0, concat_axis=0, tiled=True
        )
        return place_on_grid(places, received.reshape(groups, owners * rows, 2 * local), rows, tables, per_owner)

    heights = sorted({min(full, -(-full * share // 64) * 8) for share in (5, 6, 8)})
    branches = [functools.partial(finish, rows) for rows in heights]
    if len(heights) == 1:
        grid = branches[0](images, all_screens, pick, order, places)
    else:
        index = sum((most[0, 0] > rows).astype(jnp.int32) for rows in heights[:-1])
        grid = lax.switch(index, branches, images, all_screens, pick, order, places)
    return grid[None]


def solution(mesh):
    return jax.shard_map(
        per_device,
        mesh=mesh,
        in_specs=(
            P(("corr", "tile"), None, None),
            P(("corr", "tile"), None, None),
            P(("corr", "tile"), None),
            P(("corr", "tile"), None),
            P(("corr", "tile"), None),
            P("tile", None, None),
        ),
        out_specs=P("corr", "tile", None, None, None),
        check_vma=False,
    )
```

```python
import functools
import math

import jax
import jax.numpy as jnp
import numpy as np
from jax import lax
from jax.experimental import pallas as pl
from jax.experimental.pallas import tpu as pltpu
from jax.sharding import PartitionSpec as P

SUB = 32
NT = 64
TILE_SIDE = 128
PIX = SUB * SUB
LANES = 128
VMEM_LIMIT = 36 * 1024 * 1024
VMEM_ALL = 63 * 1024 * 1024 + 512 * 1024

ROOT2 = math.sqrt(2.0)


def half_turn_series():
    grid = np.cos(np.pi * (np.arange(400) + 0.5) / 800.0) * 0.5
    z = grid * grid
    sine = np.polynomial.polynomial.Polynomial.fit(z, np.sin(np.pi * grid) / grid, 3, domain=[0, 0.25], window=[0, 0.25]).coef
    cosine = np.polynomial.polynomial.Polynomial.fit(z, np.cos(np.pi * grid), 3, domain=[0, 0.25], window=[0, 0.25]).coef
    return [float(x) * ROOT2 for x in sine], [float(x) * ROOT2 for x in cosine]


SINE, COSINE = half_turn_series()


def horner(coefficients, z):
    total = coefficients[-1]
    for value in coefficients[-2::-1]:
        total = total * z + value
    return total


def cis_turns(turns):
    t = turns - jnp.round(turns)
    z = t * t
    s = t * horner(SINE, z)
    c = horner(COSINE, z)
    return 1.0 - s * s, s * c


def image_kernel(ncorr, groups, vis_ref, coord_ref, *refs):
    out_refs, square = refs[:-1], refs[-1]
    me = lax.axis_index("corr")
    step = vis_ref.shape[0]
    nvis = vis_ref.shape[2]
    centred = (lax.broadcasted_iota(jnp.int32, (SUB, nvis), 0) - SUB // 2).astype(jnp.float32) * (1.0 / SUB)
    bend = 0.5 * centred * centred
    rows = ncorr * SUB
    pitch = rows + 1

    def one(s):
        u = coord_ref[0, pl.ds(s, 1), :]
        v = coord_ref[1, pl.ds(s, 1), :]
        w = coord_ref[2, pl.ds(s, 1), :]
        sag = w * bend
        e_re, e_im = cis_turns(u * centred - sag)
        f_re, f_im = cis_turns(v * centred - sag)
        vis = vis_ref[s].astype(jnp.float32)
        g_re = []
        g_im = []
        for e in range(ncorr):
            vr = vis[e : e + 1]
            vi = vis[ncorr + e : ncorr + e + 1]
            g_re.append((vr * e_re - vi * e_im).astype(jnp.bfloat16))
            g_im.append((vr * e_im + vi * e_re).astype(jnp.bfloat16))
        left = jnp.concatenate([jnp.concatenate(g_re, axis=0), jnp.concatenate(g_im, axis=0)], axis=1)
        f_re = f_re.astype(jnp.bfloat16)
        f_im = f_im.astype(jnp.bfloat16)
        right = jnp.concatenate(
            [jnp.concatenate([f_re, f_im], axis=0), jnp.concatenate([-f_im, f_re], axis=0)], axis=1
        )
        image = lax.dot_general(left, right, (((1,), (1,)), ((), ())), preferred_element_type=jnp.float32)
        square[pl.ds(s * pitch, rows), 0 : 2 * SUB] = image

    def several(i, carry):
        for j in range(4):
            one(i * 4 + j)
        return carry

    lax.fori_loop(0, step // 4, several, 0)

    lane = lax.broadcasted_iota(jnp.int32, (step, LANES), 1)
    per_tile = LANES // SUB
    halves = SUB // groups // per_tile
    for d in range(groups):
        first = (me ^ d) * (halves * per_tile)
        for h in range(halves):
            for e in range(ncorr):
                real = None
                imag = None
                for j in range(per_tile):
                    piece = square[pl.ds(first + (e * SUB + h * per_tile + j), step, stride=pitch), :]
                    a = piece if j == 0 else pltpu.roll(piece, SUB * j, 1)
                    b = piece if j == 1 else pltpu.roll(piece, (SUB * (j - 1)) % LANES, 1)
                    keep = lane < SUB * (j + 1)
                    real = a if real is None else jnp.where(lane < SUB * j, real, a)
                    imag = b if imag is None else jnp.where(lane < SUB * j, imag, b)
                base = h * 2 * ncorr * LANES
                out_refs[d][:, base + e * LANES : base + (e + 1) * LANES] = real.astype(jnp.bfloat16)
                out_refs[d][:, base + (ncorr + e) * LANES : base + (ncorr + e + 1) * LANES] = imag.astype(jnp.bfloat16)


def make_images(visibilities, coords, groups, first, size):
    count, fields, nvis = visibilities.shape
    ncorr = fields // 2
    step = 16
    width = fields * PIX // groups
    return pl.pallas_call(
        functools.partial(image_kernel, ncorr, groups),
        grid=(size // step,),
        in_specs=[
            pl.BlockSpec((step, fields, nvis), lambda i: (i + first // step, 0, 0)),
            pl.BlockSpec((3, step, nvis), lambda i: (0, i + first // step, 0)),
        ],
        out_specs=[pl.BlockSpec((step, width), lambda i: (i, 0))] * groups,
        out_shape=[jax.ShapeDtypeStruct((size, width), jnp.bfloat16)] * groups,
        scratch_shapes=[pltpu.VMEM((step * (ncorr * SUB + 1), LANES), jnp.float32)],
        compiler_params=pltpu.CompilerParams(vmem_limit_bytes=VMEM_LIMIT),
        cost_estimate=pl.CostEstimate(flops=size << 27, bytes_accessed=2 << 20, transcendentals=0),
        name="images",
    )(visibilities, jnp.transpose(coords, (1, 0, 2)))


def pixels_kernel(screen_ref, out_ref, held, rows_ref, sems):
    blocks, stations, fields, local = held.shape
    me = lax.axis_index("corr")
    step = pl.program_id(0)
    mine = pl.ds(pl.multiple_of(me * local, local), local)
    copies = [
        pltpu.make_async_copy(screen_ref.at[i * stations : (i + 1) * stations, :, mine], held.at[i], sems.at[i])
        for i in range(blocks)
    ]
    for copy in copies:
        pl.when(step == 0)(copy.start)
    for i, copy in enumerate(copies):
        pl.when(step == i)(copy.wait)
    pitch = fields + 1
    halves = local // LANES
    for s in range(stations):
        station = held[step, s].astype(jnp.float32)
        for h in range(halves):
            rows_ref[h, s * pitch : s * pitch + fields, :] = station[:, h * LANES : (h + 1) * LANES]
    for h in range(halves):
        for f in range(fields):
            at = (h * fields + f) * LANES
            out_ref[:, at : at + LANES] = rows_ref[h, pl.ds(f, stations, stride=pitch), :].astype(jnp.bfloat16)


def own_pixels(screens, groups):
    stations, fields, pixels = screens.shape
    local = pixels // groups
    block = 16
    return pl.pallas_call(
        pixels_kernel,
        grid=(stations // block,),
        in_specs=[pl.BlockSpec(memory_space=pl.ANY)],
        out_specs=pl.BlockSpec((block, fields * local), lambda i: (i, 0)),
        out_shape=jax.ShapeDtypeStruct((stations, fields * local), jnp.bfloat16),
        scratch_shapes=[
            pltpu.VMEM((stations // block, block, fields, local), jnp.bfloat16),
            pltpu.VMEM((local // LANES, block * (fields + 1), LANES), jnp.float32),
            pltpu.SemaphoreType.DMA((stations // block,)),
        ],
        compiler_params=pltpu.CompilerParams(vmem_limit_bytes=VMEM_ALL),
        name="pixels",
    )(screens)


def plan_kernel(groups, owners, per_owner, count, every_ref, pick_ref, order_ref, place_ref, most_ref):
    nst = pick_ref.shape[1]
    n = groups * count
    together = LANES // count
    me = lax.axis_index("tile")
    lane = lax.broadcasted_iota(jnp.int32, (8, LANES), 1)
    number = lax.broadcasted_iota(jnp.int32, (count, nst), 1).astype(jnp.float32)
    before = lax.broadcasted_iota(jnp.int32, (n, n), 0) < lax.broadcasted_iota(jnp.int32, (n, n), 1)
    before = before.astype(jnp.float32).astype(jnp.bfloat16)
    owner_row = lax.broadcasted_iota(jnp.int32, (owners, n), 0).astype(jnp.float32)
    slot = lax.broadcasted_iota(jnp.int32, (LANES, n), 0).astype(jnp.float32)
    row = lax.broadcasted_iota(jnp.int32, (8, LANES), 0)

    def group(t):
        tiles = []
        for g in range(0, groups, together):
            joined = None
            for k in range(together):
                facts = every_ref[(g + k) * owners + t].astype(jnp.float32)
                facts = facts if k == 0 else pltpu.roll(facts, k * count, 1)
                joined = facts if k == 0 else jnp.where(lane < k * count, joined, facts)
            tiles.append(joined)
        return jnp.concatenate(tiles, axis=1)

    def ranks(facts):
        owner = jnp.floor(facts[0:1] * (1.0 / per_owner))
        hot = (owner_row == owner).astype(jnp.float32)
        ahead = jnp.dot(hot.astype(jnp.bfloat16), before, preferred_element_type=jnp.float32)
        return owner, jnp.sum(hot * ahead, axis=0, keepdims=True), jnp.sum(hot, axis=1, keepdims=True)

    for g in range(groups):
        columns = jnp.transpose(every_ref[g * owners + me].astype(jnp.float32))
        for which in range(2):
            at = which * n + g * count
            station = columns[:count, 3 + which : 4 + which]
            pick_ref[at : at + count, :] = (number == station).astype(jnp.float32).astype(jnp.bfloat16)
    owner, rank, held = ranks(group(me))
    order_ref[0:1, :] = owner
    order_ref[1:2, :] = rank

    most = jnp.zeros((owners, 1), jnp.float32)
    for t in range(owners):
        facts = group(t)
        owner, rank, held = ranks(facts)
        most = jnp.maximum(most, held)
        here = jnp.where(owner == me.astype(jnp.float32), 1.0, 0.0)
        hit = jnp.where(slot == jnp.where(here > 0.0, rank, -1.0), 1.0, 0.0).astype(jnp.bfloat16)
        local = facts[0:1] - owner * per_owner
        values = jnp.concatenate([facts[1:3], local, jnp.zeros((5, n), jnp.float32)], axis=0).astype(jnp.bfloat16)
        found = lax.dot_general(values, hit, (((1,), (1,)), ((), ())), preferred_element_type=jnp.float32)
        total = jnp.sum(here, axis=1, keepdims=True)
        place_ref[t] = jnp.where(row == 4, total, found).astype(jnp.int32)
    most_ref[...] = jnp.broadcast_to(jnp.max(most, axis=0, keepdims=True), most_ref.shape).astype(jnp.int32)


def make_plan(every, groups, owners, per_owner, count, nst):
    n = groups * count
    return pl.pallas_call(
        functools.partial(plan_kernel, groups, owners, per_owner, count),
        out_shape=[
            jax.ShapeDtypeStruct((2 * n, nst), jnp.bfloat16),
            jax.ShapeDtypeStruct((8, n), jnp.float32),
            jax.ShapeDtypeStruct((owners, 8, LANES), jnp.int32),
            jax.ShapeDtypeStruct((8, LANES), jnp.int32),
        ],
        compiler_params=pltpu.CompilerParams(vmem_limit_bytes=VMEM_LIMIT),
        cost_estimate=pl.CostEstimate(flops=1 << 30, bytes_accessed=1 << 20, transcendentals=0),
        name="plan",
    )(every)


def aterm_kernel(ncorr, owners, rows_of, scale, groups, *refs):
    image_refs, refs = refs[:-8], refs[-8:]
    screen_ref, pick_ref, order_ref, out_ref, block_ref, jones_ref, held, sems = refs
    n = order_ref.shape[1]
    count = n // groups
    me = lax.axis_index("corr")
    step = pl.program_id(0)
    copies = [
        pltpu.make_async_copy(screen_ref.at[:, h * held.shape[2] : (h + 1) * held.shape[2]], held.at[h], sems.at[h])
        for h in range(held.shape[0])
    ]
    for h, copy in enumerate(copies):
        pl.when(step == 0)(copy.start)
    for h, copy in enumerate(copies):
        pl.when(step == h)(copy.wait)
    jones_ref[...] = jnp.dot(pick_ref[...], held[step], preferred_element_type=jnp.float32)
    pixel = lax.broadcasted_iota(jnp.int32, (1, LANES), 1) + (me * pl.num_programs(0) + pl.program_id(0)) * LANES
    row_at = ((pixel // SUB).astype(jnp.float32) - (SUB - 1) / 2.0) * (2.0 / SUB)
    col_at = ((pixel % SUB).astype(jnp.float32) - (SUB - 1) / 2.0) * (2.0 / SUB)
    taper = (1.0 - 0.8 * row_at * row_at) * (1.0 - 0.8 * col_at * col_at) * scale
    chunk = 16

    def part(ref, rows, field):
        return ref[rows, field * LANES : (field + 1) * LANES].astype(jnp.float32)

    def body(ref, d, begin, i, carry):
        held = pl.ds(pl.multiple_of(i * chunk, chunk), chunk)
        at = (me ^ d) * count + begin + i * chunk
        rows = pl.ds(pl.multiple_of(at, chunk), chunk)
        far_rows = pl.ds(pl.multiple_of(at + n, chunk), chunk)
        image_re = [part(ref, held, e) for e in range(ncorr)]
        image_im = [part(ref, held, ncorr + e) for e in range(ncorr)]
        for row_out in range(2):
            mid_re = []
            mid_im = []
            for inner in range(2):
                m_re = 0.0
                m_im = 0.0
                for first in range(2):
                    near_re = part(jones_ref, rows, 2 * first + row_out)
                    near_im = part(jones_ref, rows, ncorr + 2 * first + row_out)
                    vis_re = image_re[2 * first + inner]
                    vis_im = image_im[2 * first + inner]
                    m_re = m_re + near_re * vis_re + near_im * vis_im
                    m_im = m_im + near_re * vis_im - near_im * vis_re
                mid_re.append(m_re)
                mid_im.append(m_im)
            for col_out in range(2):
                t_re = 0.0
                t_im = 0.0
                for inner in range(2):
                    far_re = part(jones_ref, far_rows, 2 * inner + col_out)
                    far_im = part(jones_ref, far_rows, ncorr + 2 * inner + col_out)
                    t_re = t_re + mid_re[inner] * far_re - mid_im[inner] * far_im
                    t_im = t_im + mid_re[inner] * far_im + mid_im[inner] * far_re
                place = 2 * (2 * row_out + col_out) * LANES
                block_ref[rows, place : place + LANES] = (t_re * taper).astype(jnp.bfloat16)
                block_ref[rows, place + LANES : place + 2 * LANES] = (t_im * taper).astype(jnp.bfloat16)
        return carry

    for p, ref in enumerate(image_refs):
        begin = sum(other.shape[0] for other in image_refs[p % groups : p : groups])
        lax.fori_loop(0, ref.shape[0] // chunk, functools.partial(body, ref, p % groups, begin), 0)
    target = order_ref[0:1, :] * float(rows_of) + order_ref[1:2, :]
    row = lax.broadcasted_iota(jnp.int32, (owners * rows_of, n), 0).astype(jnp.float32)
    move = (row == target).astype(jnp.float32).astype(jnp.bfloat16)
    for e in range(ncorr):
        block = block_ref[:, 2 * e * LANES : 2 * (e + 1) * LANES]
        out_ref[e] = jnp.dot(move, block, preferred_element_type=jnp.float32).astype(jnp.bfloat16)


def apply_aterms(images, groups, screens, pick, order, scale, ncorr, owners, rows):
    n = order.shape[1]
    nst = screens.shape[0]
    half = 2 * ncorr * LANES
    halves = screens.shape[1] // half
    return pl.pallas_call(
        functools.partial(aterm_kernel, ncorr, owners, rows, scale, groups),
        grid=(halves,),
        in_specs=[pl.BlockSpec((image.shape[0], half), lambda h: (0, h)) for image in images]
        + [
            pl.BlockSpec(memory_space=pltpu.HBM),
            pl.BlockSpec(pick.shape, lambda h: (0, 0)),
            pl.BlockSpec(order.shape, lambda h: (0, 0)),
        ],
        out_specs=pl.BlockSpec((ncorr, owners * rows, 2 * LANES), lambda h: (0, 0, h)),
        out_shape=jax.ShapeDtypeStruct((ncorr, owners * rows, halves * 2 * LANES), jnp.bfloat16),
        scratch_shapes=[
            pltpu.VMEM((n, half), jnp.bfloat16),
            pltpu.VMEM((2 * n, half), jnp.float32),
            pltpu.VMEM((halves, nst, half), jnp.bfloat16),
            pltpu.SemaphoreType.DMA((halves,)),
        ],
        compiler_params=pltpu.CompilerParams(vmem_limit_bytes=VMEM_LIMIT),
        cost_estimate=pl.CostEstimate(flops=6 << 30, bytes_accessed=8 << 20, transcendentals=0),
        name="aterms",
    )(*images, screens, pick, order)


def grid_kernel(rows, place_ref, block_ref, col_ref, row_ref, out_ref, half_ref, uv_ref, *sums):
    groups, total, depth = block_ref.shape
    sources = total // rows
    per_slot = 2 * PIX // LANES + 1
    quarters = depth // LANES
    low = lax.broadcasted_iota(jnp.int32, (total, LANES), 1) < LANES // 2
    for c in range(groups):
        tiles = []
        for h in range(2):
            block = block_ref[c, :, 2 * h * LANES : 2 * (h + 1) * LANES]
            tiles.append(jnp.dot(block, col_ref[...], preferred_element_type=jnp.float32))
        for j in range(2):
            one, two = [tile[:, j * LANES : (j + 1) * LANES] for tile in tiles]
            first = jnp.where(low, one, pltpu.roll(two, LANES // 2, 1))
            second = jnp.where(low, pltpu.roll(one, LANES // 2, 1), two)
            half_ref[c, :, 2 * j * LANES : (2 * j + 1) * LANES] = first.astype(jnp.bfloat16)
            half_ref[c, :, (2 * j + 1) * LANES : (2 * j + 2) * LANES] = second.astype(jnp.bfloat16)
    for q in range(quarters):
        left = jnp.concatenate([half_ref[g, :, q * LANES : (q + 1) * LANES] for g in range(groups)], axis=1)
        uv = jnp.dot(left, row_ref[...], preferred_element_type=jnp.float32)
        for part in range(2):
            for i in range(2):
                j = part * 2 + i
                uv_ref[pl.ds(part * 8 + 2 * q + i, total, stride=per_slot), :] = uv[:, j * LANES : (j + 1) * LANES]
    for ref in sums:
        ref[...] = jnp.zeros_like(ref)

    lane = lax.broadcasted_iota(jnp.int32, (8, LANES), 1)
    pieces = LANES // SUB
    batch = 8
    for t in range(sources):

        def add(i, carry):
            for b in range(batch):
                j = i * batch + b
                y = place_ref[t, 1, j]
                row = place_ref[t, 2, j] * TILE_SIDE + place_ref[t, 0, j]
                band = lax.shift_right_logical((lane - y) & (LANES - 1), SUB.bit_length() - 1)
                for part in range(2):
                    at = (t * rows + j) * per_slot + part * 8
                    turned = pltpu.roll(uv_ref[pl.ds(at, 8), :], y, 1)
                    for g in range(pieces):
                        ref = sums[part * pieces + g]
                        span = pl.ds(row + 8 * g, 8)
                        ref[span, :] = ref[span, :] + jnp.where(band == g, turned, 0.0)
            return carry

        lax.fori_loop(0, (place_ref[t, 4, 0] + (batch - 1)) // batch, add, 0)

    for k in range(out_ref.shape[0]):
        span = slice(k * TILE_SIDE, (k + 1) * TILE_SIDE)
        for part in range(2):
            total_here = sums[part * pieces][span, :]
            for g in range(1, pieces):
                total_here = total_here + pltpu.roll(sums[part * pieces + g][span, :], LANES - g * SUB, 1)
            out_ref[k, part] = total_here


def place_on_grid(places, blocks, rows, tables, per_owner):
    groups, total, depth = blocks.shape
    whole = pl.BlockSpec(memory_space=pltpu.VMEM)
    accumulator = pltpu.VMEM((per_owner * TILE_SIDE, TILE_SIDE), jnp.float32)
    return pl.pallas_call(
        functools.partial(grid_kernel, rows),
        in_specs=[pl.BlockSpec(memory_space=pltpu.SMEM), whole, whole, whole],
        out_specs=whole,
        out_shape=jax.ShapeDtypeStruct((per_owner, 2, TILE_SIDE, TILE_SIDE), jnp.float32),
        scratch_shapes=[
            pltpu.VMEM((groups, total, depth), jnp.bfloat16),
            pltpu.VMEM((total * (2 * PIX // LANES + 1), LANES), jnp.float32),
        ]
        + [accumulator] * (2 * LANES // SUB),
        compiler_params=pltpu.CompilerParams(vmem_limit_bytes=VMEM_LIMIT),
        name="grid",
    )(places, blocks, *tables)


def uv_tables(groups):
    quad = LANES // SUB
    halves = SUB // (groups * quad)
    index = np.arange(SUB) - SUB // 2
    factor = np.exp(-2j * np.pi / SUB * ((index[:, None] * index[None, :]) % SUB))

    def parts(table, axis):
        upper = np.stack([table.real, table.imag], axis=axis)
        lower = np.stack([-table.imag, table.real], axis=axis)
        return upper, lower

    col = (factor / SUB).reshape(SUB, 4, 4, 2).transpose(2, 0, 3, 1)
    first = np.zeros((2, quad, SUB, 4, 2, quad, 2, 4))
    for p, table in enumerate(parts(col, 0)):
        for r in range(quad):
            first[p, r, :, :, :, r] = table.transpose(2, 1, 0, 3, 4)
    second = np.zeros((groups, halves, 2, quad, 2, 4, 2, 2, 4, SUB))
    row = factor.reshape(groups, halves, quad, SUB)
    for p, table in enumerate(parts(row, 0)):
        for i in range(2):
            for g in range(4):
                second[:, :, p, :, i, g, :, i, g, :] = table.transpose(1, 2, 3, 0, 4)
    first = first.reshape(2 * LANES, 2 * LANES)
    second = second.reshape(groups * halves * 2 * quad * 8, 4 * LANES)
    return first.astype(jnp.bfloat16), second.astype(jnp.bfloat16)


def per_device(visibilities, coords, stations, tile_ids, offsets, screens):
    count, fields, nvis = visibilities.shape
    ncorr = fields // 2
    groups = lax.axis_size("corr")
    owners = lax.axis_size("tile")
    corr = lax.axis_index("corr")
    tile = lax.axis_index("tile")
    per_owner = NT // owners
    full = per_owner * groups * (2 * count // NT)
    halves = PIX // (groups * LANES)
    local = PIX // groups

    part = own_pixels(screens, groups)
    all_screens = lax.all_gather(part, "tile", axis=0, tiled=True)

    facts = jnp.concatenate([tile_ids.T, offsets.T, stations.T], axis=0)
    facts = jnp.pad(facts, ((0, 8 - facts.shape[0]), (0, LANES - count)))
    every = jnp.broadcast_to(facts[None], (groups * owners, 8, LANES))
    every = lax.all_to_all(every, ("corr", "tile"), split_axis=0, concat_axis=0, tiled=True)

    images = []
    for first, size in ((0, count * 3 // 4), (count * 3 // 4, count // 4)):
        for d, piece in enumerate(make_images(visibilities, coords, groups, first, size)):
            if first and d == groups - 1:
                images[1], piece = lax.optimization_barrier((images[1], piece))
            images.append(lax.ppermute(piece, "corr", [(i, i ^ d) for i in range(groups)]) if d else piece)
    pick, order, places, most = make_plan(every, groups, owners, per_owner, count, all_screens.shape[0])

    tables = tuple(jnp.asarray(table) for table in uv_tables(groups))

    def finish(rows, images, screens, pick, order, places):
        sending = apply_aterms(images, groups, screens, pick, order, 1.0 / nvis, ncorr, owners, rows)
        received = lax.all_to_all(
            sending.reshape(groups * owners, rows, 2 * local), ("corr", "tile"), split_axis=0, concat_axis=0, tiled=True
        )
        return place_on_grid(places, received.reshape(groups, owners * rows, 2 * local), rows, tables, per_owner)

    heights = sorted({min(full, -(-full * share // 64) * 8) for share in (5, 6, 8)})
    branches = [functools.partial(finish, rows) for rows in heights]
    if len(heights) == 1:
        grid = branches[0](images, all_screens, pick, order, places)
    else:
        index = sum((most[0, 0] > rows).astype(jnp.int32) for rows in heights[:-1])
        grid = lax.switch(index, branches, images, all_screens, pick, order, places)
    return grid[None]


def solution(mesh):
    return jax.shard_map(
        per_device,
        mesh=mesh,
        in_specs=(
            P(("corr", "tile"), None, None),
            P(("corr", "tile"), None, None),
            P(("corr", "tile"), None),
            P(("corr", "tile"), None),
            P(("corr", "tile"), None),
            P("tile", None, None),
        ),
        out_specs=P("corr", "tile", None, None, None),
        check_vma=False,
    )
```
